32 devices in a mesh: dp: 8 (over y, x, core), tensor: 4 (over z).
Axes of the slice: x: 2, y: 2, z: 4, core: 2. Of those that a mesh axis runs over, the one named last changes fastest.
Arguments:
- inputs: bfloat16 [16384, 768], P('dp'), may hold values from -6 to 6
- qkv_weight: bfloat16 [3, 768, 768], P(None, None, 'tensor'), may hold values from -0.21875 to 0.21875
- qv_bias: bfloat16 [2, 768], P(None, 'tensor'), may hold values from -3 to 3
- out_weight: bfloat16 [768, 768], P('tensor'), may hold values from -1.75 to 1.75
- out_bias: bfloat16 [768], replicated, may hold values from -3 to 3
- attn_gain: bfloat16 [768], replicated, may hold values from 0.25 to 1.75
- attn_shift: bfloat16 [768], replicated, may hold values from -3 to 3
- up_weight: bfloat16 [768, 3072], P(None, 'tensor'), may hold values from -0.21875 to 0.21875
- up_bias: bfloat16 [3072], P('tensor'), may hold values from -3 to 3
- down_weight: bfloat16 [3072, 768], P('tensor'), may hold values from -0.15625 to 0.15625
- down_bias: bfloat16 [768], replicated, may hold values from -3 to 3
- ffn_gain: bfloat16 [768], replicated, may hold values from 0.25 to 1.75
- ffn_shift: bfloat16 [768], replicated, may hold values from -3 to 3
- keep_mask: int32 [16], P('dp'), may hold values 0 or 1
- cotangent: bfloat16 [16384, 768], P('dp'), may hold values from -6 to 6
Outputs:
- outputs: bfloat16 [16384, 768], P('dp')
- grad_inputs: float32 [16384, 768], P('dp')
- grad_qkv: float32 [3, 768, 768], P(None, 'dp', 'tensor')
- grad_qv_bias: float32 [2, 768], P(None, 'tensor')
- grad_out_weight: float32 [768, 768], P('tensor', 'dp')
- grad_out_bias: float32 [768], replicated
- grad_attn_gain: float32 [768], replicated
- grad_attn_shift: float32 [768], replicated
- grad_up_weight: float32 [768, 3072], P('dp', 'tensor')
- grad_up_bias: float32 [3072], P('tensor')
- grad_down_weight: float32 [3072, 768], P('tensor', 'dp')
- grad_down_bias: float32 [768], replicated
- grad_ffn_gain: float32 [768], replicated
- grad_ffn_shift: float32 [768], replicated
The draws below stay inside these ranges and needn't reach their ends.
Inputs may be any that keep to these rules, and one draw needn't show every extreme that they name: `keep_mask`: 1 keeps the layer for that sequence, 0 skips it.
All inputs are finite; a program needn't handle non-finite values. No bound on the sum of `keep_mask` on one device may be relied on, other than what follows from the above.
Results may differ from the reference program's by a relative error of at most 0.019.
The reference program's roundings to bfloat16 on the way count: a program that leaves them out, or rounds other values in their place, can miss the bound.
Values may be sent and summed in bfloat16 or wider, within the bound.
No kernel may reach another device: no remote copies, remote signals or barrier semaphores. Data moves between devices by JAX's collectives and lax.ppermute only.
A program may use at most 128 MiB of HBM per device.

```python
import jax
import jax.numpy as jnp
from jax import lax

D = 768
HEADS = 12
HEAD_DIM = 64
FF = 3072
SEQ_LEN = 1024
SEQS = 16
TOKENS = 16384
N_TENSOR = 4


def place_ends(array, key, low, high):
    spot = [jax.random.randint(jax.random.fold_in(key, axis), (), 0, length) for axis, length in enumerate(array.shape)]
    main_axis = array.shape.index(max(array.shape))
    neighbour = spot[:main_axis] + [(spot[main_axis] + 1) % array.shape[main_axis]] + spot[main_axis + 1:]
    return array.at[tuple(spot)].set(low).at[tuple(neighbour)].set(high)


def spiked(array, own_key, source, target, blocks, factor):
    def block_of(axis_at):
        return (jnp.arange(array.shape[axis_at]) // (array.shape[axis_at] // blocks)).reshape((-1,) + (1,) * (array.ndim - 1 - axis_at))

    near = jax.random.permutation(own_key, blocks)[block_of(target)]
    second = (block_of(target) + blocks // 2) % blocks
    return jnp.where((block_of(source) == near) | (block_of(source) == second), factor * array, array)


def level_of(rng, shape, cuts, smallest, high):
    loudness, own = 1.0, jax.random.fold_in(rng, 6)
    for dim, blocks in cuts:
        draws = jnp.exp(jax.random.uniform(jax.random.fold_in(own, dim), (blocks,), jnp.float32, smallest / len(cuts), high / len(cuts)))
        loudness = loudness * jnp.repeat(draws, shape[dim] // blocks).reshape([-1 if axis == dim else 1 for axis in range(len(shape))])
    return loudness


def scatter_about(own_key, shape, spread, limit, cuts=(), dtype=jnp.bfloat16):
    array = jax.random.normal(own_key, shape, jnp.float32) * spread
    if len(cuts) > 0:
        array = level_of(own_key, shape, cuts, -0.22, 0.18) * array
    return jnp.clip(array, min=-limit, max=limit).astype(dtype)


def gaussian_with(key, shape, deviation, limit, shards, heavy, dtype=jnp.bfloat16):
    array = deviation * jax.random.normal(key, shape, jnp.float32)
    if shards:
        array = array * level_of(key, shape, shards, -0.22, 0.18)
    return jnp.clip(spiked(array, jax.random.fold_in(key, 3), *heavy), -limit, limit).astype(dtype)


def setup_inputs(seed: int = 0) -> dict:
    seeds = jax.random.split(jax.random.key(seed), 16)
    inputs = gaussian_with(seeds[0], (TOKENS, D), 1.0, 6.0, ((0, 8),), (0, 1, 8, 2.0))
    qkv_weight = scatter_about(seeds[1], (3, D, D), D ** -0.5, 0.21875, ((2, 4),))
    qv_bias = scatter_about(seeds[2], (2, D), 0.5, 3.0, ((1, 4),))
    out_weight = scatter_about(seeds[3], (D, D), (D // 64) ** -0.5, 1.75, ((0, 4),))
    out_bias = scatter_about(seeds[4], (D,), 0.5, 3.0)
    attn_gain = jnp.clip(1.0 + 0.15 * jax.random.normal(seeds[5], (D,), jnp.float32), 0.25, 1.75).astype(jnp.bfloat16)
    attn_shift = scatter_about(seeds[6], (D,), 0.5, 3.0)
    up_weight = scatter_about(seeds[7], (D, FF), D ** -0.5, 0.21875, ((1, 4),))
    up_bias = scatter_about(seeds[8], (FF,), 0.5, 3.0, ((0, 4),))
    down_weight = scatter_about(seeds[9], (FF, D), (FF // 2) ** -0.5, 0.15625, ((0, 4),))
    down_bias = scatter_about(seeds[10], (D,), 0.5, 3.0)
    ffn_gain = jnp.clip(1.0 + 0.15 * jax.random.normal(seeds[11], (D,), jnp.float32), 0.25, 1.75).astype(jnp.bfloat16)
    ffn_shift = scatter_about(seeds[12], (D,), 0.5, 3.0)
    keep_mask = place_ends((jax.random.randint(seeds[13], (SEQS,), 0, 3) < 2).astype(jnp.int32), jax.random.fold_in(seeds[13], 1), 0, 1)
    cotangent = gaussian_with(seeds[14], (TOKENS, D), 1.0, 6.0, ((0, 8),), (0, 1, 8, 2.0))
    return dict(inputs=inputs, qkv_weight=qkv_weight, qv_bias=qv_bias, out_weight=out_weight, out_bias=out_bias, attn_gain=attn_gain, attn_shift=attn_shift, up_weight=up_weight, up_bias=up_bias, down_weight=down_weight, down_bias=down_bias, ffn_gain=ffn_gain, ffn_shift=ffn_shift, keep_mask=keep_mask, cotangent=cotangent)


HIGH = lax.Precision.HIGHEST
EPS = 1e-05

@jax.custom_vjp
def low(v):
    return lax.optimization_barrier(v.astype(jnp.bfloat16)).astype(jnp.float32)

@jax.custom_vjp
def low_back(v):
    return v

def low_keep(v):
    return (low(v), None)

def low_pass(kept, grad):
    return (grad,)

def back_keep(v):
    return (v, None)

def back_low(kept, grad):
    return (low(grad),)
low.defvjp(low_keep, low_pass)
low_back.defvjp(back_keep, back_low)

def matmul(left, right):
    return jnp.dot(left, right, precision=HIGH)

def normalize(values, gain, shift):
    row_mean = lax.optimization_barrier(jnp.mean(values, axis=-1, keepdims=True))
    centred = values - row_mean
    variance = lax.optimization_barrier(jnp.mean(centred * centred, axis=-1, keepdims=True))
    return centred * lax.rsqrt(variance + EPS) * gain + shift

def encoder_layer(params, tokens, keep_value):
    qkv_weight, qv_bias, out_weight, out_bias, attn_gain, attn_shift, up_weight, up_bias, down_weight, down_bias, ffn_gain, ffn_shift = params
    local_width = D // N_TENSOR
    local_hidden = FF // N_TENSOR
    local_heads = HEADS // N_TENSOR
    score_scale = HEAD_DIM ** (-0.5)
    head_shape = (SEQ_LEN, local_heads, HEAD_DIM)
    attention = jnp.zeros((SEQ_LEN, D), jnp.float32)
    for group_index in range(N_TENSOR):
        columns = slice(group_index * local_width, (group_index + 1) * local_width)
        shared = low_back(tokens)
        queries = low_back(low(matmul(shared, qkv_weight[0][:, columns]) + qv_bias[0][columns]))
        key_vectors = low_back(low(matmul(shared, qkv_weight[1][:, columns])))
        value_vectors = low_back(low(matmul(shared, qkv_weight[2][:, columns]) + qv_bias[1][columns]))
        scores = low_back(score_scale * jnp.einsum('qhd,khd->hqk', queries.reshape(head_shape), key_vectors.reshape(head_shape), precision=HIGH))
        weights = jax.nn.softmax(scores, axis=-1)
        mixed_heads = jnp.einsum('hqk,khd->qhd', low(weights), value_vectors.reshape(head_shape), precision=HIGH)
        mixed_heads = low_back(low(mixed_heads.reshape(SEQ_LEN, local_width)))
        attention = attention + low(matmul(mixed_heads, out_weight[columns, :]))
    attention = low_back(attention) + out_bias
    first_norm = normalize(tokens + attention, attn_gain, attn_shift)
    first_low = low(first_norm)
    feed = jnp.zeros((SEQ_LEN, D), jnp.float32)
    for group_index in range(N_TENSOR):
        columns = slice(group_index * local_hidden, (group_index + 1) * local_hidden)
        pre_gelu = low_back(matmul(low_back(first_low), up_weight[:, columns]) + up_bias[columns])
        active = low(jax.nn.gelu(pre_gelu, approximate=False))
        feed = feed + low(matmul(active, down_weight[columns, :]))
    feed = low_back(feed) + down_bias
    second_norm = normalize(first_norm + feed, ffn_gain, ffn_shift)
    return jnp.where(keep_value > 0, second_norm, tokens)

def reference(inputs, qkv_weight, qv_bias, out_weight, out_bias, attn_gain, attn_shift, up_weight, up_bias, down_weight, down_bias, ffn_gain, ffn_shift, keep_mask, cotangent):
    params = tuple((argument.astype(jnp.float32) for argument in (qkv_weight, qv_bias, out_weight, out_bias, attn_gain, attn_shift, up_weight, up_bias, down_weight, down_bias, ffn_gain, ffn_shift)))
    tokens = inputs.astype(jnp.float32).reshape(SEQS, SEQ_LEN, D)
    cotangents = cotangent.astype(jnp.float32).reshape(SEQS, SEQ_LEN, D)

    def per_sequence(totals, scan_item):
        sequence, keep_value, seq_cotangent = scan_item

        def apply_layer(weights_all, rows_in):
            return encoder_layer(weights_all, rows_in, keep_value)
        result, pullback = jax.vjp(apply_layer, params, sequence)
        grads, grad_rows = pullback(seq_cotangent)
        return (jax.tree.map(jnp.add, totals, grads), (result.astype(jnp.bfloat16), grad_rows))
    zeros_all = jax.tree.map(jnp.zeros_like, params)
    totals, (outputs, grad_tokens) = lax.scan(per_sequence, zeros_all, (tokens, keep_mask, cotangents))
    return (outputs.reshape(TOKENS, D), grad_tokens.reshape(TOKENS, D), totals[0], totals[1], totals[2], totals[3], totals[4], totals[5], totals[6], totals[7], totals[8], totals[9], totals[10], totals[11])
```

```python
from functools import partial

import jax
import jax.numpy as jnp
import numpy as np
from jax import lax
from jax.experimental import pallas as pl
from jax.experimental.pallas import tpu as pltpu
from jax.sharding import PartitionSpec as P

HEAD_DIM = 64
EPS = 1e-05
LOG2E = 1.4426950408889634
BF = jnp.bfloat16
F32 = jnp.float32
ANY = pl.BlockSpec(memory_space=pl.ANY)
VM = pl.BlockSpec(memory_space=pltpu.VMEM)
LIMIT = 60 * 1024 * 1024


def nn(a, b):
    return lax.dot_general(a, b, (((1,), (0,)), ((), ())), preferred_element_type=F32)


def nt(a, b):
    return lax.dot_general(a, b, (((1,), (1,)), ((), ())), preferred_element_type=F32)


def cost(us):
    return pl.CostEstimate(flops=int(us * 9e8), bytes_accessed=1024, transcendentals=0)


def params(**kw):
    return pltpu.CompilerParams(vmem_limit_bytes=LIMIT, **kw)


def head_mask(rows, width, head):
    lane = lax.broadcasted_iota(jnp.int32, (rows, width), 1)
    return (lane >= head * HEAD_DIM) & (lane < (head + 1) * HEAD_DIM)


def row_norm(values):
    row_mean = jnp.mean(values, axis=-1, keepdims=True)
    centred = values - row_mean
    variance = jnp.mean(centred * centred, axis=-1, keepdims=True)
    inverse = lax.rsqrt(variance + EPS)
    return centred * inverse, inverse


def row_norm_back(grad_normed, normed, inverse):
    first_term = jnp.mean(grad_normed, axis=-1, keepdims=True)
    second_term = jnp.mean(grad_normed * normed, axis=-1, keepdims=True)
    return inverse * (grad_normed - first_term - normed * second_term)


def gelu_both(x):
    e = jnp.exp2(x * x * (-0.5 * LOG2E))
    t = 1.0 / (1.0 + (0.3275911 * 0.7071067811865476) * jnp.abs(x))
    poly = t * (
        0.5 * 0.254829592
        + t
        * (
            0.5 * -0.284496736
            + t * (0.5 * 1.421413741 + t * (0.5 * -1.453152027 + t * (0.5 * 1.061405429)))
        )
    )
    tail = poly * e
    cdf = jnp.where(x < 0, tail, 1.0 - tail)
    return x * cdf, cdf + x * (e * 0.3989422804014327)


def place_copies(pieces, parts, meta, sems):
    copies = []
    index = 0
    for place, piece in enumerate(pieces):
        quarter = meta[1] ^ (place % 4)
        side = meta[2] ^ (place // 4)
        lanes = piece.shape[2]
        for scratch, first, rows, spread in parts:
            start = pl.multiple_of(quarter * rows + spread, 16)
            copies.append(
                pltpu.make_async_copy(
                    piece.at[:, pl.ds(first, rows), :],
                    scratch.at[:, pl.ds(start, rows), pl.ds(pl.multiple_of(side * lanes, 128), lanes)],
                    sems.at[index],
                )
            )
            index += 1
    return copies


def attend_kernel(meta, x_ref, w_ref, b_ref, o0_ref, o1_ref, l0_ref, l1_ref, q_s, k_s, v_s):
    x = x_ref[...]
    length, width = q_s.shape
    heads = width // HEAD_DIM
    half = length // 2
    scale = HEAD_DIM ** (-0.5) * LOG2E
    q_s[...] = (nn(x, w_ref[0]) + b_ref[0:1, :].astype(F32)).astype(BF)
    k_s[...] = nn(x, w_ref[1]).astype(BF)
    v_s[...] = (nn(x, w_ref[2]) + b_ref[1:2, :].astype(F32)).astype(BF)
    block = 256
    for k, (o_ref, l_ref) in enumerate(((o0_ref, l0_ref), (o1_ref, l1_ref))):
        start = ((meta[0] % 2) ^ k) * half
        for part in range(half // block):
            rows = pl.ds(pl.multiple_of(start + part * block, block), block)
            q = q_s[rows, :]
            mixed = jnp.zeros((block, width), F32)
            stats = jnp.zeros((block, 128), F32)
            stat_lane = lax.broadcasted_iota(jnp.int32, (block, 128), 1)
            for h in range(heads):
                mask = head_mask(block, width, h)
                s = nt(jnp.where(mask, q, jnp.zeros_like(q)), k_s[...])
                top = jnp.max(s, axis=-1, keepdims=True)
                p = jnp.exp2((s - top) * scale)
                total = jnp.sum(p, axis=-1, keepdims=True)
                o = nn(p.astype(BF), v_s[...]) * (1.0 / total)
                mixed = jnp.where(mask, o, mixed)
                stats = jnp.where(stat_lane == h, top * scale + jnp.log2(total), stats)
            o_ref[part * block : (part + 1) * block, :] = mixed.astype(BF)
            l_ref[:, part * block : (part + 1) * block] = jnp.transpose(stats)[:8, :]


def attend(meta, inputs, qkv_weight, qv_bias, length, other):
    width = qkv_weight.shape[2]
    dim = inputs.shape[1]
    half = length // 2
    return pl.pallas_call(
        attend_kernel,
        grid_spec=pltpu.PrefetchScalarGridSpec(
            num_scalar_prefetch=1,
            grid=(1,),
            in_specs=[
                pl.BlockSpec((length, dim), lambda i, m: ((m[0] // 2) ^ other, 0)),
                VM,
                VM,
            ],
            out_specs=[VM] * 4,
            scratch_shapes=[pltpu.VMEM((length, width), BF)] * 3,
        ),
        out_shape=[jax.ShapeDtypeStruct((half, width), BF)] * 2
        + [jax.ShapeDtypeStruct((8, half), F32)] * 2,
        compiler_params=params(),
        cost_estimate=cost(8),
    )(meta, inputs, qkv_weight, qv_bias)


def up_kernel(
    meta, x_ref, o0, o1, o2, o3, ob_ref, ag_ref, as_ref, ub_ref, wo_ref, wu_ref,
    p0, p1, p2, p3, p4, p5, p6, p7,
    n1_ref, r1_ref, ulow_ref, act_ref, der_ref, wo_s, wu_s, sems,
):
    dim = x_ref.shape[1]
    up_rows = wu_ref.shape[0] // 4
    out_rows = wo_ref.shape[0] // 4
    pieces = (p0, p1, p2, p3, p4, p5, p6, p7)
    out_copies = place_copies(pieces, ((wo_s, up_rows, out_rows, 0),), meta, sems.at[0])
    up_copies = place_copies(pieces, ((wu_s, 0, up_rows, 0),), meta, sems.at[1])
    for copy in out_copies + up_copies:
        copy.start()
    total = x_ref[...].astype(F32) + ob_ref[...].astype(F32) + nn(o0[...], wo_ref[...])
    for copy in out_copies:
        copy.wait()
    for r, o_ref in ((1, o1), (2, o2), (3, o3)):
        total = total + nn(o_ref[...], wo_s[r - 1])
    normed, inverse = row_norm(total)
    n1_ref[...] = normed
    r1_ref[...] = inverse
    low = (normed * ag_ref[...].astype(F32) + as_ref[...].astype(F32)).astype(BF)
    ulow_ref[...] = low

    def hidden(r, weight):
        for c in range(0, dim, 256):
            z = nn(ulow_ref[...], weight[:, c : c + 256]) + ub_ref[r : r + 1, c : c + 256].astype(F32)
            act, der = gelu_both(z)
            act_ref[r, :, c : c + 256] = act.astype(BF)
            der_ref[r, :, c : c + 256] = der.astype(BF)

    hidden(0, wu_ref)
    for copy in up_copies:
        copy.wait()
    for r in range(1, 4):
        hidden(r, wu_s.at[r - 1])


def down_kernel(
    meta, n1_ref, ag_ref, as_ref, db_ref, fg_ref, fs_ref, act_ref, x_ref, cot_ref, wd_ref,
    p0, p1, p2, p3, p4, p5, p6, p7,
    out_ref, dh2_ref, df_ref, small_ref, wd_s, sems,
):
    pieces = (p0, p1, p2, p3, p4, p5, p6, p7)
    copies = place_copies(pieces, ((wd_s, 0, wd_ref.shape[0] // 4, 0),), meta, sems)
    for copy in copies:
        copy.start()
    first = n1_ref[...] * ag_ref[...].astype(F32) + as_ref[...].astype(F32)
    total = first + db_ref[...].astype(F32) + nn(act_ref[0], wd_ref[...])
    for copy in copies:
        copy.wait()
    for r in range(1, 4):
        total = total + nn(act_ref[r], wd_s[r - 1])
    normed, inverse = row_norm(total)
    gain = fg_ref[...].astype(F32)
    keep = meta[3] > 0
    second = normed * gain + fs_ref[...].astype(F32)
    out_ref[...] = jnp.where(keep, second, x_ref[...].astype(F32)).astype(BF)
    grad = jnp.where(keep, cot_ref[...].astype(F32), 0.0)
    dh2 = row_norm_back(grad * gain, normed, inverse)
    dh2_ref[...] = dh2
    df_ref[...] = dh2.astype(BF)
    small_ref[...] = jnp.zeros_like(small_ref)
    small_ref[0:1, :] = jnp.sum(grad * normed, axis=0, keepdims=True)
    small_ref[1:2, :] = jnp.sum(grad, axis=0, keepdims=True)
    small_ref[2:3, :] = jnp.sum(dh2, axis=0, keepdims=True)


def ffn_back_kernel(
    meta, df_ref, dh2_ref, der_ref, n1_ref, r1_ref, ag_ref, o0, o1, o2, o3, wd_ref, wu_ref, wo_ref,
    d0, d1, d2, d3, d4, d5, d6, d7, p0, p1, p2, p3, p4, p5, p6, p7,
    dz_ref, dh1_ref, da_ref, do_ref, delta_ref, small_ref, wd_s, wu_s, wo_s, sems,
):
    dim = df_ref.shape[1]
    up_rows = wu_ref.shape[0] // 4
    out_rows = wo_ref.shape[0] // 4
    downs = (d0, d1, d2, d3, d4, d5, d6, d7)
    pieces = (p0, p1, p2, p3, p4, p5, p6, p7)
    down_copies = place_copies(downs, ((wd_s, 0, wd_ref.shape[0] // 4, 0),), meta, sems.at[0])
    up_copies = place_copies(pieces, ((wu_s, 0, up_rows, 0),), meta, sems.at[1])
    out_copies = place_copies(pieces, ((wo_s, up_rows, out_rows, 0),), meta, sems.at[2])
    for copy in down_copies + up_copies + out_copies:
        copy.start()
    small_ref[...] = jnp.zeros_like(small_ref)
    dh1_ref[...] = dh2_ref[...]

    def hidden(r, down, up):
        for c in range(0, dim, 256):
            dz = (nt(df_ref[...], down[c : c + 256, :]) * der_ref[r, :, c : c + 256].astype(F32)).astype(BF)
            dz_ref[r, :, c : c + 256] = dz
            small_ref[8 + r : 9 + r, c : c + 256] = jnp.sum(dz.astype(F32), axis=0, keepdims=True)
        dh1_ref[...] += nt(dz_ref[r], up[...])

    hidden(0, wd_ref, wu_ref)
    for copy in down_copies + up_copies:
        copy.wait()
    for r in range(1, 4):
        hidden(r, wd_s.at[r - 1], wu_s.at[r - 1])
    du1 = dh1_ref[...]
    normed = n1_ref[...]
    small_ref[0:1, :] = jnp.sum(du1 * normed, axis=0, keepdims=True)
    small_ref[1:2, :] = jnp.sum(du1, axis=0, keepdims=True)
    dh1 = row_norm_back(du1 * ag_ref[...].astype(F32), normed, r1_ref[...])
    small_ref[2:3, :] = jnp.sum(dh1, axis=0, keepdims=True)
    dh1_ref[...] = dh1
    da_ref[...] = dh1.astype(BF)
    for copy in out_copies:
        copy.wait()
    rows, width = o0.shape
    stat_lane = lax.broadcasted_iota(jnp.int32, (rows, 128), 1)
    for r, o_ref in enumerate((o0, o1, o2, o3)):
        weight = wo_ref[...] if r == 0 else wo_s[r - 1]
        do = nt(da_ref[...], weight).astype(BF)
        do_ref[r] = do
        product = do.astype(F32) * o_ref[...].astype(F32)
        stats = jnp.zeros((rows, 128), F32)
        for h in range(width // HEAD_DIM):
            inner = jnp.sum(
                jnp.where(head_mask(rows, width, h), product, 0.0), axis=-1, keepdims=True
            )
            stats = jnp.where(stat_lane == h, inner, stats)
        delta_ref[r] = jnp.transpose(stats)[:8, :]


def spread_rows(meta, acc, keep_ref, send_ref, lanes=None):
    rows = keep_ref.shape[-2]
    me = meta[1] * 2 + meta[2]
    for j in range(4):
        for side, ref in ((0, keep_ref), (1, send_ref)):
            start = pl.multiple_of((me ^ (2 * j + side)) * rows, 8)
            ref[j, 0] = acc[pl.ds(start, rows), :].astype(BF)


def ffn_weight_kernel(meta, u_ref, df_ref, dz_ref, act_ref, uk_ref, us_ref, dk_ref, ds_ref, ut_s, dt_s, acc):
    @pl.when(pl.program_id(0) == 0)
    def _():
        ut_s[...] = jnp.transpose(u_ref[...])
        dt_s[...] = jnp.transpose(df_ref[...])

    acc[...] = nn(ut_s[...], dz_ref[0])
    spread_rows(meta, acc, uk_ref, us_ref)
    acc[...] = nn(dt_s[...], act_ref[0])
    spread_rows(meta, acc, dk_ref, ds_ref)


def ffn_weight_grads(meta, ulow, dfeed, dz, act):
    rows, dim = ulow.shape
    part = dim // 8
    full = pl.BlockSpec((rows, dim), lambda r, m: (0, 0))
    group = pl.BlockSpec((1, rows, dim), lambda r, m: (r, 0, 0))
    out = pl.BlockSpec((4, 1, part, dim), lambda r, m: (0, r, 0, 0))
    return pl.pallas_call(
        ffn_weight_kernel,
        grid_spec=pltpu.PrefetchScalarGridSpec(
            num_scalar_prefetch=1,
            grid=(4,),
            in_specs=[full, full, group, group],
            out_specs=[out] * 4,
            scratch_shapes=[pltpu.VMEM((dim, rows), BF)] * 2 + [pltpu.VMEM((dim, dim), F32)],
        ),
        out_shape=[jax.ShapeDtypeStruct((4, 4, part, dim), BF)] * 4,
        compiler_params=params(),
        cost_estimate=cost(9),
    )(meta, ulow, dfeed, dz, act)


def attend_back_kernel(
    own, meta, xq_ref, xk_ref, wt_ref, b_ref, do_ref, lse_ref, delta_ref, *refs,
):
    pieces = refs[:8]
    if own:
        dqt_ref, dx_ref, dq_ref, dk_ref, dv_ref, small_ref, w_s, sems, qm_s, dom_s, kt_s = refs[8:]
    else:
        dqt_ref, dx_ref, dk_ref, dv_ref, small_ref, w_s, sems, qm_s, dom_s, kt_s = refs[8:]
    width = wt_ref.shape[1]
    heads = width // HEAD_DIM
    rows, dim = xq_ref.shape
    keys = xk_ref.shape[0]
    scale = HEAD_DIM ** (-0.5)
    quarter_rows = width // 4
    copies = [
        pltpu.make_async_copy(wt_ref.at[m], w_s.at[0, pl.ds(m * width, width), :], sems.at[1, m])
        for m in range(3)
    ]
    copies += place_copies(
        pieces,
        tuple((w_s.at[pl.ds(1, 3)], m * quarter_rows, quarter_rows, m * width) for m in range(3)),
        meta,
        sems.at[0],
    )
    for copy in copies:
        copy.start()
    for copy in copies:
        copy.wait()
    dx = dx_acc = None
    small_ref[...] = jnp.zeros_like(small_ref)
    dx_ref[...] = jnp.zeros_like(dx_ref)
    block = 256

    def group(r, carry):
        bias = b_ref[r].astype(F32)
        q = (nt(xq_ref[...], w_s[r, 0:width, :]) + bias[0:1, :]).astype(BF)
        k = nt(xk_ref[...], w_s[r, width : 2 * width, :]).astype(BF)
        v = (nt(xk_ref[...], w_s[r, 2 * width : 3 * width, :]) + bias[1:2, :]).astype(BF)
        do = do_ref[r]
        zero = jnp.zeros_like(q)
        for h in range(heads):
            mask = head_mask(rows, width, h)
            qm_s[h] = jnp.where(mask, q, zero)
            dom_s[h] = jnp.where(mask, do, zero)
        kt_s[...] = jnp.transpose(k)
        dqt = [None] * heads
        for kb in range(keys // block):
            span = slice(kb * block, (kb + 1) * block)
            dk = dv = None
            for h in range(heads):
                s = nt(k[span, :], qm_s[h])
                p = jnp.exp2(s * (scale * LOG2E) - lse_ref[r, h : h + 1, :])
                dp = nt(v[span, :], dom_s[h])
                ds = (p * (dp - delta_ref[r, h : h + 1, :])).astype(BF)
                dv_part = nn(p.astype(BF), dom_s[h])
                dk_part = nn(ds, qm_s[h])
                dq_part = nn(kt_s[h * HEAD_DIM : (h + 1) * HEAD_DIM, span], ds)
                dv = dv_part if dv is None else dv + dv_part
                dk = dk_part if dk is None else dk + dk_part
                dqt[h] = dq_part if dqt[h] is None else dqt[h] + dq_part
            dk_low = (dk * scale).astype(BF)
            dv_low = dv.astype(BF)
            dk_ref[r, span, :] = dk_low
            dv_ref[r, span, :] = dv_low
            small_ref[r, 1:2, :] += jnp.sum(dv_low.astype(F32), axis=0, keepdims=True)
            dx_ref[span, :] += (
                nn(dk_low, w_s[r, width : 2 * width, :]) + nn(dv_low, w_s[r, 2 * width : 3 * width, :])
            ).astype(dx_ref.dtype)
        whole = jnp.concatenate(dqt, axis=0)
        if own:
            dq_low = (jnp.transpose(whole + dqt_ref[r]) * scale).astype(BF)
            dq_ref[r] = dq_low
            small_ref[r, 0:1, :] = jnp.sum(dq_low.astype(F32), axis=0, keepdims=True)
            dx_ref[...] += nn(dq_low, w_s[r, 0:width, :])
        else:
            dqt_ref[r] = whole
        return carry

    lax.fori_loop(0, 4, group, 0)


def attend_back(meta, own, inputs, wt, bias, do, lse, delta, pieces, dqt=None):
    rows, width = do.shape[1:]
    dim = inputs.shape[1]
    other = 0 if own else 1
    outs = [
        jax.ShapeDtypeStruct((rows, dim), F32),
        jax.ShapeDtypeStruct((4, rows, width), BF),
        jax.ShapeDtypeStruct((4, rows, width), BF),
        jax.ShapeDtypeStruct((4, 2, width), F32),
    ]
    partial_shape = jax.ShapeDtypeStruct((4, width, rows), F32)
    if own:
        outs = outs[:1] + [jax.ShapeDtypeStruct((4, rows, width), BF)] + outs[1:]
    else:
        outs = [partial_shape] + outs
    extra = [dqt] if own else []
    return pl.pallas_call(
        partial(attend_back_kernel, own),
        grid_spec=pltpu.PrefetchScalarGridSpec(
            num_scalar_prefetch=1,
            grid=(1,),
            in_specs=[
                pl.BlockSpec((rows, dim), lambda i, m: (m[0], 0)),
                pl.BlockSpec((rows, dim), lambda i, m: (m[0] ^ other, 0)),
                ANY,
                VM,
                VM,
                VM,
                VM,
            ]
            + [ANY] * 8
            + [VM] * len(extra),
            out_specs=[VM] * len(outs),
            scratch_shapes=[
                pltpu.VMEM((4, 3 * width, dim), BF),
                pltpu.SemaphoreType.DMA((2, 24)),
                pltpu.VMEM((width // HEAD_DIM, rows, width), BF),
                pltpu.VMEM((width // HEAD_DIM, rows, width), BF),
                pltpu.VMEM((width, rows), BF),
            ],
        ),
        out_shape=outs,
        compiler_params=params(),
        cost_estimate=cost(14),
    )(meta, inputs, inputs, wt, bias, do, lse, delta, *pieces, *extra)


def attend_weight_kernel(
    meta, xq_ref, xk_ref, da_ref, dq_ref, dko_ref, dvo_ref, dkp_ref, dvp_ref, o_ref, keep_ref, send_ref, xq_s, xk_s, da_s, acc
):
    @pl.when(pl.program_id(0) == 0)
    def _():
        xq_s[...] = jnp.transpose(xq_ref[...])
        xk_s[...] = jnp.transpose(xk_ref[...])
        da_s[...] = jnp.transpose(da_ref[...])

    acc[...] = jnp.concatenate(
        [
            nn(xq_s[...], dq_ref[0]),
            nn(xq_s[...], dko_ref[0]) + nn(xk_s[...], dkp_ref[0]),
            nn(xq_s[...], dvo_ref[0]) + nn(xk_s[...], dvp_ref[0]),
            nn(da_s[...], o_ref[0]),
        ],
        axis=1,
    )
    spread_rows(meta, acc, keep_ref, send_ref)


def attend_weight_grads(meta, inputs, dattn, dq, dk_own, dv_own, dk_other, dv_other, mixed):
    rows, dim = dattn.shape
    width = dq.shape[2]
    part = dim // 8
    group = pl.BlockSpec((1, rows, width), lambda r, m: (r, 0, 0))
    out = pl.BlockSpec((4, 1, part, dim), lambda r, m: (0, r, 0, 0))
    return pl.pallas_call(
        attend_weight_kernel,
        grid_spec=pltpu.PrefetchScalarGridSpec(
            num_scalar_prefetch=1,
            grid=(4,),
            in_specs=[
                pl.BlockSpec((rows, dim), lambda r, m: (m[0], 0)),
                pl.BlockSpec((rows, dim), lambda r, m: (m[0] ^ 1, 0)),
                pl.BlockSpec((rows, dim), lambda r, m: (0, 0)),
            ]
            + [group] * 6,
            out_specs=[out] * 2,
            scratch_shapes=[pltpu.VMEM((dim, rows), BF)] * 3 + [pltpu.VMEM((dim, dim), F32)],
        ),
        out_shape=[jax.ShapeDtypeStruct((4, 4, part, dim), BF)] * 2,
        compiler_params=params(),
        cost_estimate=cost(8),
    )(meta, inputs, inputs, dattn, dq, dk_own, dv_own, dk_other, dv_other, mixed)


def over_z(x, r):
    return lax.ppermute(x, "tensor", [(i, i ^ r) for i in range(4)])


def over_dp(x, offset, size):
    return lax.ppermute(x, "dp", [(i, i ^ offset) for i in range(size)])


def gather_pieces(piece, dp):
    remote = jnp.stack([over_z(piece, r) for r in (1, 2, 3)])
    own = [remote] + [over_dp(remote, 2 * j, dp) for j in (1, 2, 3)]
    return own + [over_dp(p, 1, dp) for p in own]


def add_low(*terms):
    total = terms[0].astype(F32)
    for term in terms[1:]:
        total = total + term.astype(F32)
    return total.astype(BF)


def reduce_weight(keep, send, dp, me):
    if dp == 8:
        other = over_dp(send, 1, dp)
        sums = [add_low(keep[j], other[j]) for j in range(4)]
        arrived = [over_dp(sums[j], 2 * j, dp) for j in (1, 2, 3)]
        mine = add_low(sums[0], *arrived)
    else:
        both = jnp.stack([keep, send], 1).reshape((8,) + keep.shape[1:])
        both = jnp.take(both, jnp.arange(8) ^ (me % 8), axis=0)
        both = both.transpose(0, 2, 1, 3).reshape(-1, 4, keep.shape[3])
        mine = lax.psum_scatter(both.astype(F32), "dp", scatter_dimension=0, tiled=True)
        mine = mine.transpose(1, 0, 2).astype(BF)
    total = mine[0].astype(F32)
    for r in (1, 2, 3):
        total = total + over_z(mine[r], r).astype(F32)
    return total


def sum_over_dp(x, dp):
    offset = 1
    while offset < dp:
        x = x + over_dp(x, offset, dp)
        offset *= 2
    return x


def per_device(
    dp,
    inputs,
    qkv_weight,
    qv_bias,
    out_weight,
    out_bias,
    attn_gain,
    attn_shift,
    up_weight,
    up_bias,
    down_weight,
    down_bias,
    ffn_gain,
    ffn_shift,
    keep_mask,
    cotangent,
):
    tokens, dim = inputs.shape
    length = tokens // keep_mask.shape[0]
    width = qkv_weight.shape[2]
    rows = tokens // 4
    z = lax.axis_index("tensor")
    me = lax.axis_index("dp")
    core = me % 2
    quarter = (me // 2) % 4
    keep_value = lax.dynamic_index_in_dim(keep_mask, z // 2, 0, keepdims=False)
    meta = jnp.stack([z, quarter, core, keep_value]).astype(jnp.int32)
    lanes = dim // 2
    row = lambda v: v.reshape(1, dim)

    def piece_of(weight):
        part = weight.shape[0] // 4
        return lax.dynamic_slice(weight, (quarter * part, core * lanes), (part, lanes))

    up_out = gather_pieces(jnp.concatenate([piece_of(up_weight), piece_of(out_weight)]), dp)
    down = gather_pieces(piece_of(down_weight), dp)
    wt = qkv_weight.transpose(0, 2, 1)
    part = width // 4
    wt_piece = lax.dynamic_slice(wt, (0, quarter * part, core * lanes), (3, part, lanes))
    qkv = gather_pieces(wt_piece.reshape(3 * part, lanes), dp)
    bias_pack = jnp.concatenate([row(up_bias), jnp.pad(qv_bias, ((0, 0), (0, dim - width)))])
    bias_packs = jnp.stack([bias_pack] + [over_z(bias_pack, r) for r in (1, 2, 3)])
    up_bias_all = bias_packs[:, 0]
    qv_bias_all = bias_packs[:, 1:3, :width]

    far0, far1, far_l0, far_l1 = attend(meta, inputs, qkv_weight, qv_bias, length, 1)
    o2, l2 = over_z(far0, 2), over_z(far_l0, 2)
    o3, l3 = over_z(far1, 3), over_z(far_l1, 3)
    o0, near, l0, near_l = attend(meta, inputs, qkv_weight, qv_bias, length, 0)
    o1, l1 = over_z(near, 1), over_z(near_l, 1)
    lse = jnp.stack([l0, l1, l2, l3])

    own_rows = pl.BlockSpec((rows, dim), lambda i, m: (m[0], 0))
    hidden_low = jax.ShapeDtypeStruct((4, rows, dim), BF)
    wide = jax.ShapeDtypeStruct((rows, dim), F32)
    low = jax.ShapeDtypeStruct((rows, dim), BF)
    out_scratch = pltpu.VMEM((3, width, dim), BF)
    square = pltpu.VMEM((3, dim, dim), BF)

    n1, r1, ulow, act, der = pl.pallas_call(
        up_kernel,
        grid_spec=pltpu.PrefetchScalarGridSpec(
            num_scalar_prefetch=1,
            grid=(1,),
            in_specs=[own_rows] + [VM] * 10 + [ANY] * 8,
            out_specs=[VM] * 5,
            scratch_shapes=[out_scratch, square, pltpu.SemaphoreType.DMA((2, 8))],
        ),
        out_shape=[wide, jax.ShapeDtypeStruct((rows, 1), F32), low, hidden_low, hidden_low],
        compiler_params=params(),
        cost_estimate=cost(12),
    )(
        meta, inputs, o0, o1, o2, o3, row(out_bias), row(attn_gain), row(attn_shift), up_bias_all,
        out_weight, up_weight, *up_out,
    )

    outputs_own, dh2, dfeed, small_down = pl.pallas_call(
        down_kernel,
        grid_spec=pltpu.PrefetchScalarGridSpec(
            num_scalar_prefetch=1,
            grid=(1,),
            in_specs=[VM] * 7 + [own_rows] * 2 + [VM] + [ANY] * 8,
            out_specs=[VM] * 4,
            scratch_shapes=[square, pltpu.SemaphoreType.DMA((8,))],
        ),
        out_shape=[low, wide, low, jax.ShapeDtypeStruct((8, dim), F32)],
        compiler_params=params(),
        cost_estimate=cost(6),
    )(
        meta, n1, row(attn_gain), row(attn_shift), row(down_bias), row(ffn_gain), row(ffn_shift), act,
        inputs, cotangent, down_weight, *down,
    )

    dz, dh1, dattn, do, delta, small_up = pl.pallas_call(
        ffn_back_kernel,
        grid_spec=pltpu.PrefetchScalarGridSpec(
            num_scalar_prefetch=1,
            grid=(1,),
            in_specs=[VM] * 13 + [ANY] * 16,
            out_specs=[VM] * 6,
            scratch_shapes=[square, square, out_scratch, pltpu.SemaphoreType.DMA((3, 8))],
        ),
        out_shape=[
            hidden_low,
            wide,
            low,
            jax.ShapeDtypeStruct((4, rows, width), BF),
            jax.ShapeDtypeStruct((4, 8, rows), F32),
            jax.ShapeDtypeStruct((16, dim), F32),
        ],
        compiler_params=params(),
        cost_estimate=cost(10),
    )(
        meta, dfeed, dh2, der, n1, r1, row(attn_gain), o0, o1, o2, o3, down_weight, up_weight, out_weight,
        *down, *up_out,
    )

    outputs_parts = [outputs_own] + [over_z(outputs_own, r) for r in (1, 2, 3)]

    dqt, dx_other, dk_other, dv_other, small_other = attend_back(
        meta, False, inputs, wt, qv_bias_all, do, lse, delta, qkv
    )
    dx_arrived = over_z(dx_other.astype(BF), 1)
    up_keep, up_send, down_keep, down_send = ffn_weight_grads(meta, ulow, dfeed, dz, act)
    dx_own, dq, dk_own, dv_own, small_own = attend_back(
        meta, True, inputs, wt, qv_bias_all, do, lse, delta, qkv, dqt
    )
    cot_own = lax.dynamic_slice(cotangent, (z * rows, 0), (rows, dim))
    grad_own = jnp.where(keep_value > 0, (dh1 + (dx_own + dx_arrived.astype(F32))).astype(BF), cot_own)
    grad_parts = [grad_own] + [over_z(grad_own, r) for r in (1, 2, 3)]
    qkvo_keep, qkvo_send = attend_weight_grads(
        meta, inputs, dattn, dq, dk_own, dv_own, dk_other, dv_other, jnp.stack([o0, o1, o2, o3])
    )

    grad_up = reduce_weight(up_keep, up_send, dp, me)
    grad_down = reduce_weight(down_keep, down_send, dp, me).T
    grad_qkvo = reduce_weight(qkvo_keep, qkvo_send, dp, me)
    grad_qkv = jnp.stack([grad_qkvo[:, m * width : (m + 1) * width] for m in range(3)])
    grad_out = grad_qkvo[:, 3 * width :].T

    small = sum_over_dp(jnp.concatenate([small_down[:3], small_up[:3], small_up[8:12]]), dp)
    same = small[:6]
    for r in (1, 2):
        same = same + over_z(same, r)
    grad_up_bias = small[6]
    for r in (1, 2, 3):
        grad_up_bias = grad_up_bias + over_z(small[6 + r], r)
    qv = sum_over_dp(small_own + small_other, dp)
    grad_qv_bias = qv[0]
    for r in (1, 2, 3):
        grad_qv_bias = grad_qv_bias + over_z(qv[r], r)

    outputs = jnp.zeros((tokens, dim), BF)
    grad_inputs = jnp.zeros((tokens, dim), F32)
    for r in range(4):
        outputs = lax.dynamic_update_slice(outputs, outputs_parts[r], ((z ^ r) * rows, 0))
        grad_inputs = lax.dynamic_update_slice(
            grad_inputs, grad_parts[r].astype(F32), ((z ^ r) * rows, 0)
        )
    return (
        outputs,
        grad_inputs,
        grad_qkv,
        grad_qv_bias,
        grad_out,
        same[5],
        same[3],
        same[4],
        grad_up,
        grad_up_bias,
        grad_down,
        same[2],
        same[0],
        same[1],
    )


def solution(mesh):
    placed = (
        P("dp", None),
        P(None, None, "tensor"),
        P(None, "tensor"),
        P("tensor", None),
        P(),
        P(),
        P(),
        P(None, "tensor"),
        P("tensor"),
        P("tensor", None),
        P(),
        P(),
        P(),
        P("dp"),
        P("dp", None),
    )
    return jax.shard_map(
        partial(per_device, mesh.shape["dp"]),
        mesh=mesh,
        in_specs=placed,
        out_specs=(
            P("dp", None),
            P("dp", None),
            P(None, "dp", "tensor"),
            P(None, "tensor"),
            P("tensor", "dp"),
            P(),
            P(),
            P(),
            P("dp", "tensor"),
            P("tensor"),
            P("tensor", "dp"),
            P(),
            P(),
            P(),
        ),
        check_vma=False,
    )
```

```python
from functools import partial

import jax
import jax.numpy as jnp
import numpy as np
from jax import lax
from jax.experimental import pallas as pl
from jax.experimental.pallas import tpu as pltpu
from jax.sharding import PartitionSpec as P

HEAD_DIM = 64
EPS = 1e-05
PADDED = 256
LOG2E = 1.4426950408889634
BF = jnp.bfloat16
F32 = jnp.float32
ANY = pl.BlockSpec(memory_space=pl.ANY)
VM = pl.BlockSpec(memory_space=pltpu.VMEM)
LIMIT = 60 * 1024 * 1024


def nn(a, b):
    return lax.dot_general(a, b, (((1,), (0,)), ((), ())), preferred_element_type=F32)


def nt(a, b):
    return lax.dot_general(a, b, (((1,), (1,)), ((), ())), preferred_element_type=F32)


def cost(us):
    return pl.CostEstimate(flops=int(us * 1e3), bytes_accessed=1024, transcendentals=0)


def params(**kw):
    return pltpu.CompilerParams(vmem_limit_bytes=LIMIT, **kw)


def head_mask(rows, width, head):
    lane = lax.broadcasted_iota(jnp.int32, (rows, width), 1)
    return (lane >= head * HEAD_DIM) & (lane < (head + 1) * HEAD_DIM)


def row_norm(values):
    row_mean = jnp.mean(values, axis=-1, keepdims=True)
    centred = values - row_mean
    variance = jnp.mean(centred * centred, axis=-1, keepdims=True)
    inverse = lax.rsqrt(variance + EPS)
    return centred * inverse, inverse


def row_norm_back(grad_normed, normed, inverse):
    first_term = jnp.mean(grad_normed, axis=-1, keepdims=True)
    second_term = jnp.mean(grad_normed * normed, axis=-1, keepdims=True)
    return inverse * (grad_normed - first_term - normed * second_term)


def gelu_both(x):
    e = jnp.exp2(x * x * (-0.5 * LOG2E))
    t = 1.0 / (1.0 + (0.3275911 * 0.7071067811865476) * jnp.abs(x))
    poly = t * (
        0.5 * 0.254829592
        + t
        * (
            0.5 * -0.284496736
            + t * (0.5 * 1.421413741 + t * (0.5 * -1.453152027 + t * (0.5 * 1.061405429)))
        )
    )
    tail = poly * e
    cdf = jnp.where(x < 0, tail, 1.0 - tail)
    return x * cdf, cdf + x * (e * 0.3989422804014327)


def row_of(ref):
    return ref[...].astype(F32).reshape(1, ref.shape[0])


def whole(*shape, dtype=F32):
    return jax.ShapeDtypeStruct(shape, dtype)


def full(*shape):
    return pl.BlockSpec(shape, lambda *_: (0,) * len(shape))


def local_call(kernel, meta, args, outs, specs=None, scratch=(), us=1, out_specs=None, grid=(1,), aliases=None):
    return pl.pallas_call(
        kernel,
        grid_spec=pltpu.PrefetchScalarGridSpec(
            num_scalar_prefetch=1,
            grid=grid,
            in_specs=specs if specs is not None else [VM] * len(args),
            out_specs=out_specs if out_specs is not None else [VM] * len(outs),
            scratch_shapes=list(scratch),
        ),
        out_shape=list(outs),
        compiler_params=params(),
        cost_estimate=cost(us),
        input_output_aliases=aliases or {},
    )(meta, *args)


def cut_kernel(meta, up_ref, out_ref, down_ref, wt_ref, ub_ref, qvb_ref, a_ref, d_ref, q_ref, bias_s):
    lanes = a_ref.shape[1]
    up_rows, out_rows, part = up_ref.shape[0], out_ref.shape[0], wt_ref.shape[1]
    a_ref[:up_rows, :] = up_ref[...]
    a_ref[up_rows : up_rows + out_rows, :] = out_ref[...]
    bias_s[...] = jnp.zeros_like(bias_s)
    up_bias = row_of(ub_ref)
    bias_s[0:1, :] = up_bias[:, :lanes]
    bias_s[1:2, :] = up_bias[:, lanes:]
    bias_s[2:4, : qvb_ref.shape[1]] = qvb_ref[...].astype(F32)
    a_ref[up_rows + out_rows :, :] = bias_s[...].astype(BF)
    d_ref[...] = down_ref[...]
    for m in range(3):
        q_ref[m * part : (m + 1) * part, :] = wt_ref[m]


def cut(meta, up_weight, out_weight, down_weight, wt, up_bias, qv_bias):
    dim, hidden = up_weight.shape
    width = wt.shape[1]
    lanes = dim // 2
    place = lambda i, m: (m[1], m[2])
    return local_call(
        cut_kernel,
        meta,
        (up_weight, out_weight, down_weight, wt, up_bias, qv_bias),
        [
            whole(dim // 4 + width // 4 + 16, lanes, dtype=BF),
            whole(hidden // 4, lanes, dtype=BF),
            whole(3 * width // 4, lanes, dtype=BF),
        ],
        specs=[
            pl.BlockSpec((dim // 4, lanes), place),
            pl.BlockSpec((width // 4, lanes), place),
            pl.BlockSpec((hidden // 4, lanes), place),
            pl.BlockSpec((3, width // 4, lanes), lambda i, m: (0, m[1], m[2])),
            VM,
            VM,
        ],
        scratch=[pltpu.VMEM((16, lanes), F32)],
    )


def place_copies(pieces, parts, meta, sems):
    copies = []
    for place, piece in enumerate(pieces):
        quarter = meta[1] ^ (place % 4)
        side = meta[2] ^ (place // 4)
        lanes = piece.shape[2]
        for scratch, first, rows, base in parts:
            start = pl.multiple_of(quarter * rows + base, 16)
            copies.append(
                pltpu.make_async_copy(
                    piece.at[:, pl.ds(first, rows), :],
                    scratch.at[:, pl.ds(start, rows), pl.ds(pl.multiple_of(side * lanes, 128), lanes)],
                    sems.at[len(copies)],
                )
            )
    return copies


def split_three(rows):
    high = rows.astype(BF).astype(F32)
    middle = (rows - high).astype(BF).astype(F32)
    return high, middle, rows - high - middle


def attend_kernel(meta, x_ref, wt_ref, b_ref, o0_ref, o1_ref, q_s, k_s, v_s):
    x = x_ref[...]
    length, width = q_s.shape
    heads = width // HEAD_DIM
    half = length // 2
    scale = HEAD_DIM ** (-0.5) * LOG2E
    q_s[...] = (nt(x, wt_ref[0]) + b_ref[0:1, :].astype(F32)).astype(BF)
    k_s[...] = nt(x, wt_ref[1]).astype(BF)
    v_s[...] = (nt(x, wt_ref[2]) + b_ref[1:2, :].astype(F32)).astype(BF)
    block = 256
    for k, o_ref in enumerate((o0_ref, o1_ref)):
        start = ((meta[0] % 2) ^ k) * half
        for part in range(half // block):
            rows = pl.ds(pl.multiple_of(start + part * block, block), block)
            q = q_s[rows, :]
            mixed = jnp.zeros((block, width), F32)
            stats = jnp.zeros((block, 128), F32)
            stat_lane = lax.broadcasted_iota(jnp.int32, (block, 128), 1)
            for h in range(heads):
                mask = head_mask(block, width, h)
                s = nt(jnp.where(mask, q, jnp.zeros_like(q)), k_s[...])
                top = jnp.max(s, axis=-1, keepdims=True)
                p = jnp.exp2((s - top) * scale)
                total = jnp.sum(p, axis=-1, keepdims=True)
                o = nn(p.astype(BF), v_s[...]) * (1.0 / total)
                mixed = jnp.where(mask, o, mixed)
                stats = jnp.where(stat_lane == h, top * scale + jnp.log2(total), stats)
            span = slice(part * block, (part + 1) * block)
            o_ref[:width, span] = jnp.transpose(mixed).astype(BF)
            logs = jnp.transpose(stats)[:8, :]
            o_ref[width:, span] = jnp.concatenate(split_three(logs) + (jnp.zeros_like(logs),), axis=0).astype(BF)


def attend(meta, inputs, wt, qv_bias, length, other):
    width, dim = wt.shape[1:]
    return local_call(
        attend_kernel,
        meta,
        (inputs, wt, qv_bias),
        [whole(width + 32, length // 2, dtype=BF)] * 2,
        specs=[pl.BlockSpec((length, dim), lambda i, m: ((m[0] // 2) ^ other, 0)), VM, VM],
        scratch=[pltpu.VMEM((length, width), BF)] * 3,
        us=8,
    )


def up_kernel(meta, x_ref, t0, t1, t2, t3, ob_ref, ag_ref, as_ref, ub_ref, qvb_ref, wo_ref, wu_ref, *refs):
    pieces = refs[:8]
    n1_ref, r1_ref, ulow_ref, act_ref, der_ref, o_ref, lse_ref, qvb_all_ref = refs[8:16]
    wo_s, wu_s, bias_s, sems = refs[16:]
    dim = x_ref.shape[1]
    lanes = dim // 2
    up_rows, out_rows = wu_ref.shape[0] // 4, wo_ref.shape[0] // 4
    width = wo_ref.shape[0]
    copies = []
    for part, (first, rows, scratch) in enumerate(((up_rows, out_rows, wo_s), (0, up_rows, wu_s))):
        copies.append(place_copies(pieces, ((scratch, first, rows, 0),), meta, sems.at[part]))
    rows = pl.ds(up_rows + out_rows, 16)
    copies[0].append(pltpu.make_async_copy(pieces[0].at[:, rows, :], bias_s, sems.at[2, 0]))
    for copy in copies[0] + copies[1]:
        copy.start()
    total = x_ref[...].astype(F32) + row_of(ob_ref)
    for copy in copies[0]:
        copy.wait()
    for r, t_ref in enumerate((t0, t1, t2, t3)):
        mixed = jnp.transpose(t_ref[:width, :])
        o_ref[r, :, :width] = mixed
        logs = t_ref[width:, :].astype(F32)
        lse_ref[r] = logs[0:8] + logs[8:16] + logs[16:24]
        total = total + nn(mixed, wo_ref[...] if r == 0 else wo_s[r - 1])
        qvb_all_ref[r] = jnp.zeros_like(qvb_all_ref[r])
        if r == 0:
            qvb_all_ref[r, 0:2, :width] = qvb_ref[...].astype(F32)
        else:
            qvb_all_ref[r, 0:2, :width] = bias_s[r - 1].astype(F32)[2:4, :width]
    normed, inverse = row_norm(total)
    n1_ref[...] = normed
    r1_ref[...] = inverse
    ulow_ref[...] = (normed * row_of(ag_ref) + row_of(as_ref)).astype(BF)

    def hidden(r, weight, bias):
        for c in range(0, dim, 256):
            z = nn(ulow_ref[...], weight[:, c : c + 256]) + bias[:, c : c + 256]
            act, der = gelu_both(z)
            act_ref[r, :, c : c + 256] = act.astype(BF)
            der_ref[r, :, c : c + 256] = der.astype(BF)

    hidden(0, wu_ref, row_of(ub_ref))
    for copy in copies[1]:
        copy.wait()
    for r in range(1, 4):
        bias = bias_s[r - 1].astype(F32)
        hidden(r, wu_s.at[r - 1], jnp.concatenate([bias[0:1, :lanes], bias[1:2, :lanes]], axis=1))


def down_kernel(meta, keep_ref, n1_ref, ag_ref, as_ref, db_ref, fg_ref, fs_ref, act_ref, x_ref, cot_ref, wd_ref, *refs):
    pieces = refs[:8]
    out_ref, half0_ref, half1_ref, dh2_ref, df_ref, small_ref, wd_s, sems = refs[8:]
    copies = place_copies(pieces, ((wd_s, 0, wd_ref.shape[0] // 4, 0),), meta, sems)
    for copy in copies:
        copy.start()
    first = n1_ref[...] * row_of(ag_ref) + row_of(as_ref)
    total = first + row_of(db_ref) + nn(act_ref[0], wd_ref[...])
    for copy in copies:
        copy.wait()
    for r in range(1, 4):
        total = total + nn(act_ref[r], wd_s[r - 1])
    normed, inverse = row_norm(total)
    gain = row_of(fg_ref)
    keep = keep_ref[meta[0] // 2] > 0
    second = normed * gain + row_of(fs_ref)
    low = jnp.where(keep, second, x_ref[...].astype(F32)).astype(BF)
    half = low.shape[0] // 2
    out_ref[...] = low
    half0_ref[...] = low[:half]
    half1_ref[...] = low[half:]
    grad = jnp.where(keep, cot_ref[...].astype(F32), 0.0)
    dh2 = row_norm_back(grad * gain, normed, inverse)
    dh2_ref[...] = dh2
    df_ref[...] = dh2.astype(BF)
    small_ref[...] = jnp.zeros_like(small_ref)
    small_ref[0:1, :] = jnp.sum(grad * normed, axis=0, keepdims=True)
    small_ref[1:2, :] = jnp.sum(grad, axis=0, keepdims=True)
    small_ref[2:3, :] = jnp.sum(dh2, axis=0, keepdims=True)


def ffn_back_kernel(meta, df_ref, dh2_ref, der_ref, wd_ref, wu_ref, *refs):
    downs, pieces = refs[:8], refs[8:16]
    dz_ref, du1_ref, small_ref, wd_s, wu_s, sems = refs[16:]
    dim = df_ref.shape[1]
    copies = place_copies(downs, ((wd_s, 0, wd_ref.shape[0] // 4, 0),), meta, sems.at[0])
    copies += place_copies(pieces, ((wu_s, 0, wu_ref.shape[0] // 4, 0),), meta, sems.at[1])
    for copy in copies:
        copy.start()
    small_ref[...] = jnp.zeros_like(small_ref)
    du1_ref[...] = dh2_ref[...]

    def hidden(r, down, up):
        for c in range(0, dim, 256):
            dz = (nt(df_ref[...], down[c : c + 256, :]) * der_ref[r, :, c : c + 256].astype(F32)).astype(BF)
            dz_ref[r, :, c : c + 256] = dz
            small_ref[r : r + 1, c : c + 256] = jnp.sum(dz.astype(F32), axis=0, keepdims=True)
        du1_ref[...] += nt(dz_ref[r], up[...])

    hidden(0, wd_ref, wu_ref)
    for copy in copies:
        copy.wait()
    for r in range(1, 4):
        hidden(r, wd_s.at[r - 1], wu_s.at[r - 1])


def norm_back_kernel(meta, du1_ref, n1_ref, r1_ref, ag_ref, o_ref, wo_ref, *refs):
    pieces = refs[:8]
    dh1_ref, da_ref, do_ref, delta_ref, small_ref, wo_s, sems = refs[8:]
    width, dim = wo_ref.shape
    copies = place_copies(pieces, ((wo_s, dim // 4, width // 4, 0),), meta, sems)
    for copy in copies:
        copy.start()
    du1 = du1_ref[...]
    normed = n1_ref[...]
    small_ref[...] = jnp.zeros_like(small_ref)
    small_ref[0:1, :] = jnp.sum(du1 * normed, axis=0, keepdims=True)
    small_ref[1:2, :] = jnp.sum(du1, axis=0, keepdims=True)
    dh1 = row_norm_back(du1 * row_of(ag_ref), normed, r1_ref[...])
    small_ref[2:3, :] = jnp.sum(dh1, axis=0, keepdims=True)
    dh1_ref[...] = dh1
    da_ref[...] = dh1.astype(BF)
    for copy in copies:
        copy.wait()
    rows = du1.shape[0]
    stat_lane = lax.broadcasted_iota(jnp.int32, (rows, 128), 1)
    for r in range(4):
        do = nt(da_ref[...], wo_ref[...] if r == 0 else wo_s[r - 1]).astype(BF)
        do_ref[r] = do
        product = do.astype(F32) * o_ref[r, :, :width].astype(F32)
        stats = jnp.zeros((rows, 128), F32)
        for h in range(width // HEAD_DIM):
            inner = jnp.sum(jnp.where(head_mask(rows, width, h), product, 0.0), axis=-1, keepdims=True)
            stats = jnp.where(stat_lane == h, inner, stats)
        delta_ref[r] = jnp.transpose(stats)[:8, :]


def ffn_weight_kernel(meta, u_ref, v_ref, df_ref, dg_ref, dz_ref, dy_ref, act_ref, adt_ref, *refs):
    outs, (t_s, lu_s, ld_s) = refs[:4], refs[4:]
    tokens = u_ref.shape[0]
    part = outs[0].shape[2]

    @pl.when(pl.program_id(0) == 0)
    def _():
        for source, target, base in ((u_ref, lu_s, 0), (v_ref, lu_s, tokens), (df_ref, ld_s, 0), (dg_ref, ld_s, tokens)):
            t_s[...] = jnp.transpose(source[...])
            for j in range(4):
                start = pl.multiple_of((2 * (meta[1] ^ j) + meta[2]) * part, 16)
                target[j * part : (j + 1) * part, base : base + tokens] = t_s[pl.ds(start, part), :]

    for i, (left, own, other) in enumerate(((lu_s, dz_ref, dy_ref), (ld_s, act_ref, adt_ref))):
        acc = (nn(left[:, :tokens], own[0]) + nn(left[:, tokens:], other[0])).astype(BF)
        for j in range(4):
            outs[j][i, 0] = acc[j * part : (j + 1) * part, :]


def ffn_weight_grads(meta, ulow, ulow_o, dfeed, dfeed_o, dz, dz_o, act, act_o):
    rows, dim = ulow.shape
    part = dim // 8
    full = pl.BlockSpec((rows, dim), lambda r, m: (0, 0))
    group = pl.BlockSpec((1, rows, dim), lambda r, m: (r, 0, 0))
    out = pl.BlockSpec((2, 1, part, dim), lambda r, m: (0, r, 0, 0))
    return local_call(
        ffn_weight_kernel,
        meta,
        (ulow, ulow_o, dfeed, dfeed_o, dz, dz_o, act, act_o),
        [whole(2, 4, part, dim, dtype=BF)] * 4,
        specs=[full] * 4 + [group] * 4,
        out_specs=[out] * 4,
        scratch=[pltpu.VMEM((dim, rows), BF)] + [pltpu.VMEM((4 * part, 2 * rows), BF)] * 2,
        grid=(4,),
        us=9,
    )


def add(a, b):
    return a.astype(F32) + b.astype(F32)


def ffn_plane_kernel(meta, own, px, py, pd, send_ref, keep_ref):
    total = add(own[:, 0], px[:, 0]) + add(py[:, 0], pd[:, 0])
    near = pl.program_id(0) % 2 == 0

    @pl.when(near)
    def _():
        keep_ref[:, 0] = total

    @pl.when(jnp.logical_not(near))
    def _():
        send_ref[:, 0] = total.astype(BF)


def ffn_plane(meta, parts):
    _, groups, part, dim = parts[0].shape
    half = pl.BlockSpec((2, 1, part, dim), lambda r, m: (0, r // 2, 0, 0))
    return local_call(
        ffn_plane_kernel,
        meta,
        parts,
        [whole(2, 2, part, dim, dtype=BF), whole(2, 2, part, dim)],
        specs=[pl.BlockSpec((2, 1, part, dim), lambda r, m: (0, r, 0, 0))] * 4,
        out_specs=[half, half],
        grid=(groups,),
    )


def ffn_near_kernel(meta, keep, arrived, send_ref, mine_ref):
    for i in range(2):
        mine_ref[i] = keep[i, 0] + arrived[i, 0].astype(F32)
        send_ref[i] = (keep[i, 1] + arrived[i, 1].astype(F32)).astype(BF)


def attend_back_kernel(own, meta, xq_ref, xk_ref, wt_ref, b_ref, do_ref, lse_ref, delta_ref, *refs):
    pieces = refs[:8]
    if own:
        dqt_ref, sd_ref, sn_ref, su_ref, sp_ref, dh1_ref, cot_ref, keep_ref, dx_ref, dkv_ref, small_ref, w_s, sems, qm_s, dom_s, kt_s = refs[8:]
        base = 1
    else:
        dqt_ref, dxl_ref, dkv_ref, small_ref, w_s, sems, qm_s, dom_s, kt_s, dx_ref = refs[8:]
        base = 0
    width = wt_ref.shape[1]
    heads = width // HEAD_DIM
    rows, dim = xq_ref.shape
    keys = xk_ref.shape[0]
    scale = HEAD_DIM ** (-0.5)
    quarter_rows = width // 4
    copies = [
        pltpu.make_async_copy(wt_ref.at[m], w_s.at[0, pl.ds(m * width, width), :], sems.at[1, m])
        for m in range(3)
    ]
    copies += place_copies(
        pieces,
        tuple((w_s.at[pl.ds(1, 3)], m * quarter_rows, quarter_rows, m * width) for m in range(3)),
        meta,
        sems.at[0],
    )
    for copy in copies:
        copy.start()
    for copy in copies:
        copy.wait()
    small_ref[...] = jnp.zeros_like(small_ref)
    if own:
        small_ref[0:3, :] = sd_ref[0:3, :]
        small_ref[3:6, :] = sn_ref[0:3, :]
        small_ref[8:12, :] = su_ref[0:4, :]
    dx_ref[...] = dh1_ref[...] if own else jnp.zeros_like(dx_ref)
    block = 256

    def group(r, carry):
        bias = b_ref[r][:, :width]
        q = (nt(xq_ref[...], w_s[r, 0:width, :]) + bias[0:1, :]).astype(BF)
        k = nt(xk_ref[...], w_s[r, width : 2 * width, :]).astype(BF)
        v = (nt(xk_ref[...], w_s[r, 2 * width : 3 * width, :]) + bias[1:2, :]).astype(BF)
        do = do_ref[r]
        zero = jnp.zeros_like(q)
        for h in range(heads):
            mask = head_mask(rows, width, h)
            qm_s[h] = jnp.where(mask, q, zero)
            dom_s[h] = jnp.where(mask, do, zero)
        kt_s[...] = jnp.transpose(k)
        dqt = [None] * heads
        dv_sum = sp_ref[r, 0:1, :] if own else jnp.zeros((1, width), F32)
        for kb in range(keys // block):
            span = slice(kb * block, (kb + 1) * block)
            dk = dv = None
            for h in range(heads):
                s = nt(k[span, :], qm_s[h])
                p = jnp.exp2(s * (scale * LOG2E) - lse_ref[r, h : h + 1, :])
                dp = nt(v[span, :], dom_s[h])
                ds = (p * (dp - delta_ref[r, h : h + 1, :])).astype(BF)
                dv_part = nn(p.astype(BF), dom_s[h])
                dk_part = nn(ds, qm_s[h])
                dq_part = nn(kt_s[h * HEAD_DIM : (h + 1) * HEAD_DIM, span], ds)
                dv = dv_part if dv is None else dv + dv_part
                dk = dk_part if dk is None else dk + dk_part
                dqt[h] = dq_part if dqt[h] is None else dqt[h] + dq_part
            dk_low = (dk * scale).astype(BF)
            dv_low = dv.astype(BF)
            dkv_ref[base, r, span, :width] = dk_low
            dkv_ref[base + 1, r, span, :width] = dv_low
            dv_sum = dv_sum + jnp.sum(dv_low.astype(F32), axis=0, keepdims=True)
            dx_ref[span, :] += (
                nn(dk_low, w_s[r, width : 2 * width, :]) + nn(dv_low, w_s[r, 2 * width : 3 * width, :])
            ).astype(dx_ref.dtype)
        all_heads = jnp.concatenate(dqt, axis=0)
        if own:
            dq_low = (jnp.transpose(all_heads + dqt_ref[r]) * scale).astype(BF)
            dkv_ref[0, r, :, :width] = dq_low
            small_ref[pl.ds(12 + r, 1), :width] = jnp.sum(dq_low.astype(F32), axis=0, keepdims=True)
            small_ref[pl.ds(16 + r, 1), :width] = dv_sum
            dx_ref[...] += nn(dq_low, w_s[r, 0:width, :])
        else:
            dqt_ref[r] = all_heads
            small_ref[r, 0:1, :] = dv_sum
        return carry

    lax.fori_loop(0, 4, group, 0)
    if own:

        @pl.when(keep_ref[meta[0] // 2] <= 0)
        def _():
            dx_ref[...] = cot_ref[...].astype(F32)

    else:
        dxl_ref[...] = dx_ref[...].astype(BF)


def attend_back(meta, own, inputs, wt, bias, do, lse, delta, pieces, extra=()):
    rows, width = do.shape[1:]
    dim = inputs.shape[1]
    other = 0 if own else 1
    own_rows = pl.BlockSpec((rows, dim), lambda i, m: (m[0], 0))
    if own:
        outs = [whole(rows, dim), whole(3, 4, rows, PADDED, dtype=BF), whole(24, dim)]
    else:
        outs = [
            whole(4, width, rows),
            whole(rows, dim, dtype=BF),
            whole(2, 4, rows, PADDED, dtype=BF),
            whole(4, 8, width),
        ]
    low = pltpu.VMEM((width // HEAD_DIM, rows, width), BF)
    return local_call(
        partial(attend_back_kernel, own),
        meta,
        (inputs, inputs, wt, bias, do, lse, delta, *pieces, *extra),
        outs,
        specs=[
            own_rows,
            pl.BlockSpec((rows, dim), lambda i, m: (m[0] ^ other, 0)),
            ANY,
        ]
        + [VM] * 4
        + [ANY] * 8
        + ([VM] * 6 + [own_rows, pl.BlockSpec(memory_space=pltpu.SMEM)] if own else []),
        scratch=[
            pltpu.VMEM((4, 3 * width, dim), BF),
            pltpu.SemaphoreType.DMA((2, 24)),
            low,
            low,
            pltpu.VMEM((width, rows), BF),
        ]
        + ([] if own else [pltpu.VMEM((rows, dim), F32)]),
        us=14,
    )


def attend_weight_kernel(
    meta, xq, yq, xk, yk, da, ea, g_own, h_own, g_far, h_far, o_ref, p_ref, small, small_o, p0, p1, p2, p3, t_s, lq_s, lk_s, la_s
):
    outs = (p0, p1, p2, p3)
    tokens = xq.shape[0]
    part = t_s.shape[0] // 8
    r = pl.program_id(0)

    @pl.when(r == 0)
    def _():
        pairs = ((xq, lq_s, 0), (yq, lq_s, tokens), (xk, lk_s, 0), (yk, lk_s, tokens), (da, la_s, 0), (ea, la_s, tokens))
        for source, target, base in pairs:
            t_s[...] = jnp.transpose(source[...])
            for j in range(4):
                start = pl.multiple_of((2 * (meta[1] ^ j) + meta[2]) * part, 16)
                target[j * part : (j + 1) * part, base : base + tokens] = t_s[pl.ds(start, part), :]
        packed = pack_small(small[...] + small_o[...])
        for ref in outs:
            ref[4 * part :, :] = packed

    width = t_s.shape[0] // 4
    first, second = slice(0, tokens), slice(tokens, 2 * tokens)
    both = lambda left, a, b: nn(left[:, first], a[:, :width]) + nn(left[:, second], b[:, :width])
    acc = jnp.concatenate(
        [both(lq_s, g_own[0, 0], h_own[0, 0])]
        + [both(lq_s, g_own[m, 0], h_own[m, 0]) + both(lk_s, g_far[m - 1, 0], h_far[m - 1, 0]) for m in (1, 2)]
        + [both(la_s, o_ref[0], p_ref[0])],
        axis=1,
    ).astype(BF)
    rows = pl.ds(pl.multiple_of(r * part, 16), part)
    for j in range(4):
        outs[j][rows, :] = acc[j * part : (j + 1) * part, :]


def attend_weight_grads(meta, inputs, inputs_o, dattn, dattn_o, g_own, h_own, g_far, h_far, mixed, mixed_o, small, small_o):
    rows, dim = dattn.shape
    width = mixed.shape[2]
    part = dim // 8
    own = pl.BlockSpec((rows, dim), lambda r, m: (m[0], 0))
    far = pl.BlockSpec((rows, dim), lambda r, m: (m[0] ^ 1, 0))
    full = pl.BlockSpec((rows, dim), lambda r, m: (0, 0))
    three = pl.BlockSpec((3, 1, rows, width), lambda r, m: (0, r, 0, 0))
    two = pl.BlockSpec((2, 1, rows, width), lambda r, m: (0, r, 0, 0))
    group = pl.BlockSpec((1, rows, width), lambda r, m: (r, 0, 0))
    left = pltpu.VMEM((4 * part, 2 * rows), BF)
    return local_call(
        attend_weight_kernel,
        meta,
        (inputs, inputs_o, inputs, inputs_o, dattn, dattn_o, g_own, h_own, g_far, h_far, mixed, mixed_o, small, small_o),
        [whole(4 * part + 48, dim, dtype=BF)] * 4,
        specs=[own, own, far, far, full, full, three, three, two, two, group, group, VM, VM],
        scratch=[pltpu.VMEM((dim, rows), BF), left, left, left],
        grid=(4,),
        us=8,
    )


def pack_small(rows):
    high = rows.astype(BF).astype(F32)
    return jnp.concatenate([high, rows - high], axis=0).astype(BF)


def unpack_small(rows):
    rows = rows.astype(F32)
    return rows[:24] + rows[24:]


def plane_sum_kernel(meta, own, px, py, pd, s1, s2, s3, keep_ref, small_ref):
    part = keep_ref.shape[0]
    for r, ref in enumerate((keep_ref, s1, s2, s3)):
        s = slice(r * part, (r + 1) * part)
        total = add(own[s, :], px[s, :]) + add(py[s, :], pd[s, :])
        ref[:part, :] = total.astype(ref.dtype)
    s = slice(4 * part, 4 * part + 48)
    small = (unpack_small(own[s, :]) + unpack_small(px[s, :])) + (unpack_small(py[s, :]) + unpack_small(pd[s, :]))
    packed = pack_small(small)
    for ref in (s1, s2, s3):
        ref[part:, :] = packed
    small_ref[...] = unpack_small(packed)


def final_sum_kernel(meta, mine, small, a1, a2, a3, gqkv_ref, gout_ref, ub_ref, qv_ref, *same_refs):
    part = mine.shape[0]
    width = gqkv_ref.shape[2]
    total = (mine[...] + a1[:part, :].astype(F32)) + add(a2[:part, :], a3[:part, :])
    for m in range(3):
        gqkv_ref[m] = total[:, m * width : (m + 1) * width]
    gout_ref[...] = jnp.transpose(total[:, 3 * width :])
    s0, s1, s2, s3 = small[...], unpack_small(a1[part:, :]), unpack_small(a2[part:, :]), unpack_small(a3[part:, :])
    same = (s0[0:8] + s1[0:8]) + (s2[0:8] + s3[0:8])
    for i, ref in enumerate(same_refs):
        ref[...] = same[i : i + 1].reshape(ref.shape)
    mine_rows = [(s0[i : i + 1] + s1[i + 1 : i + 2]) + (s2[i + 2 : i + 3] + s3[i + 3 : i + 4]) for i in (8, 12, 16)]
    ub_ref[...] = mine_rows[0].reshape(ub_ref.shape)
    qv_ref[0:1, :] = mine_rows[1][:, :width]
    qv_ref[1:2, :] = mine_rows[2][:, :width]


def place_kernel(steps, meta, *refs):
    out_ref = refs[-1]
    start = 0
    for ref, count in zip(refs[:-1], steps):

        @pl.when((pl.program_id(0) >= start) & (pl.program_id(0) < start + count))
        def _():
            out_ref[...] = ref[...].astype(out_ref.dtype)

        start += count


def place(meta, blocks, tokens, dtype, step):
    dim = blocks[0].shape[1]
    per_group = tokens // 4 // step
    steps = [b.shape[0] // step for b in blocks]
    starts = np.cumsum([0] + steps)
    specs = [
        pl.BlockSpec((step, dim), lambda i, m, a=int(a), n=n: (jnp.clip(i - a, 0, n - 1), 0)) for a, n in zip(starts, steps)
    ]
    return local_call(
        partial(place_kernel, steps),
        meta,
        blocks,
        [whole(tokens, dim, dtype=dtype)],
        specs=specs,
        out_specs=[pl.BlockSpec((step, dim), lambda i, m: ((m[0] ^ (i // per_group)) * per_group + i % per_group, 0))],
        grid=(int(starts[-1]),),
    )[0]


def place_last_kernel(meta, rest, a, out_ref):
    out_ref[...] = a[...].astype(F32)


def over_z(x, r):
    return lax.ppermute(x, "tensor", [(i, i ^ r) for i in range(4)])


def over_dp(x, offset, size):
    return lax.ppermute(x, "dp", [(i, i ^ offset) for i in range(size)])


def tick(*arrays):
    return lax.optimization_barrier(arrays)


def per_device(
    dp,
    inputs,
    qkv_weight,
    qv_bias,
    out_weight,
    out_bias,
    attn_gain,
    attn_shift,
    up_weight,
    up_bias,
    down_weight,
    down_bias,
    ffn_gain,
    ffn_shift,
    keep_mask,
    cotangent,
):
    tokens, dim = inputs.shape
    length = tokens // keep_mask.shape[0]
    width = qkv_weight.shape[2]
    rows = tokens // 4
    part = dim // 8
    z = lax.axis_index("tensor")
    me = lax.axis_index("dp")
    meta = jnp.stack([z, (me // 2) % 4, me % 2]).astype(jnp.int32)
    wt = qkv_weight.transpose(0, 2, 1)
    own_rows = pl.BlockSpec((rows, dim), lambda i, m: (m[0], 0))
    smem = pl.BlockSpec(memory_space=pltpu.SMEM)
    low, wide = whole(rows, dim, dtype=BF), whole(rows, dim)
    hidden_low = whole(4, rows, dim, dtype=BF)
    heads_low = whole(4, rows, width, dtype=BF)
    out_scratch = pltpu.VMEM((3, width, dim), BF)
    square = pltpu.VMEM((3, dim, dim), BF)
    dma = pltpu.SemaphoreType.DMA
    plane = lambda block: [over_dp(block, 2 * j, dp) for j in (1, 2, 3)]
    cores = lambda blocks: [over_dp(b, 1, dp) for b in blocks]

    a, d, q = cut(meta, up_weight, out_weight, down_weight, wt, up_bias, qv_bias)
    a1, a2, a3 = over_z(a, 1), over_z(a, 2), over_z(a, 3)
    far0, far1 = attend(meta, inputs, wt, qv_bias, length, 1)
    m, a1, a2, a3, far0, far1, d = tick(meta, a1, a2, a3, far0, far1, d)

    t2, t3 = over_z(far0, 2), over_z(far1, 3)
    up_out = jnp.stack([a1, a2, a3])
    up_out = [up_out] + plane(up_out)
    t0, near = attend(m, inputs, wt, qv_bias, length, 0)
    m, d, t0, t2, t3, near, *up_out = tick(m, d, t0, t2, t3, near, *up_out)

    t1, d1, d2, d3 = over_z(near, 1), over_z(d, 1), over_z(d, 2), over_z(d, 3)
    up_out += cores(up_out)
    m, q, t1, d1, d2, d3, *up_out = tick(m, q, t1, d1, d2, d3, *up_out)

    down = jnp.stack([d1, d2, d3])
    down = [down] + plane(down)
    q1, q2 = over_z(q, 1), over_z(q, 2)
    vector = full(dim)
    heads_t = full(*t1.shape)
    n1, r1, ulow, act, der, mixed, lse, qvb = local_call(
        up_kernel,
        m,
        (inputs, t0, t1, t2, t3, out_bias, attn_gain, attn_shift, up_bias, qv_bias, out_weight, up_weight, *up_out),
        [wide, whole(rows, 1), low, hidden_low, hidden_low, whole(4, rows, PADDED, dtype=BF), whole(4, 8, rows), whole(4, 8, 256)],
        specs=[own_rows, VM] + [heads_t] * 3 + [vector] * 4 + [full(2, width), VM, VM] + [ANY] * 8,
        scratch=[out_scratch, square, pltpu.VMEM((3, 16, dim // 2), BF), dma((3, 8))],
        us=12,
    )
    m, q, q1, q2, act, ulow, mixed, *down = tick(m, q, q1, q2, act, ulow, mixed, *down)

    q3 = over_z(q, 3)
    down += cores(down)
    m, act, ulow, mixed, *down = tick(m, act, ulow, mixed, *down)
    act_o, ulow_o, mixed_o = cores([act, ulow, mixed])
    outputs_own, half0, half1, dh2, dfeed, small_down = local_call(
        down_kernel,
        m,
        (keep_mask, n1, attn_gain, attn_shift, down_bias, ffn_gain, ffn_shift, act, inputs, cotangent, down_weight, *down),
        [low, whole(rows // 2, dim, dtype=BF), whole(rows // 2, dim, dtype=BF), wide, low, whole(8, dim)],
        specs=[smem, VM] + [vector] * 5 + [VM] + [own_rows] * 2 + [VM] + [ANY] * 8,
        scratch=[square, dma((8,))],
        us=6,
    )
    m, q3, act_o, ulow_o, mixed_o, outputs_own, half0, half1, dfeed = tick(
        m, q3, act_o, ulow_o, mixed_o, outputs_own, half0, half1, dfeed
    )

    out1 = over_z(outputs_own, 1)
    qkv = jnp.stack([q1, q2, q3])
    qkv = [qkv] + plane(qkv)
    dfeed_o = over_dp(dfeed, 1, dp)
    dz, du1, small_up = local_call(
        ffn_back_kernel,
        m,
        (dfeed, dh2, der, down_weight, up_weight, *down, *up_out),
        [hidden_low, wide, whole(8, dim)],
        specs=[VM] * 5 + [ANY] * 16,
        scratch=[square, square, dma((2, 8))],
        us=10,
    )
    m, dfeed_o, dz, out1, half0, half1, *qkv = tick(m, dfeed_o, dz, out1, half0, half1, *qkv)

    dz_o = over_dp(dz, 1, dp)
    qkv += cores(qkv)
    dh1, dattn, do, delta, small_norm = local_call(
        norm_back_kernel,
        m,
        (du1, n1, r1, attn_gain, mixed, out_weight, *up_out),
        [wide, low, heads_low, whole(4, 8, rows), whole(8, dim)],
        specs=[VM] * 3 + [vector] + [VM] * 2 + [ANY] * 8,
        scratch=[out_scratch, dma((8,))],
        us=4,
    )
    m, dz_o, dattn, half0, half1, *qkv = tick(m, dz_o, dattn, half0, half1, *qkv)

    out20 = over_z(half0, 2)
    dattn_o, inputs_o = cores([dattn, inputs])
    parts = ffn_weight_grads(m, ulow, ulow_o, dfeed, dfeed_o, dz, dz_o, act, act_o)
    m, out20, half1, dattn_o, inputs_o, *parts = tick(m, out20, half1, dattn_o, inputs_o, *parts)

    out21, out30 = over_z(half1, 2), over_z(out20, 1)
    extra = []
    if dp == 8:
        extra = [over_dp(parts[1], 2, dp), over_dp(parts[2], 4, dp)]
    dqt, dx_other, g_far, small_other = attend_back(m, False, inputs, wt, qvb, do, lse, delta, qkv)
    m, out21, out30, dx_other, g_far, *rest = tick(m, out21, out30, dx_other, g_far, *parts, *extra)
    parts, extra = rest[:4], rest[4:]

    out31, dx_arrived, h_far = over_z(out21, 1), over_z(dx_other, 1), over_dp(g_far, 1, dp)
    if dp == 8:
        extra.append(over_dp(parts[3], 6, dp))
    dx_own, g_own, small = attend_back(
        m, True, inputs, wt, qvb, do, lse, delta, qkv,
        (dqt, small_down, small_norm, small_up, small_other, dh1, cotangent, keep_mask),
    )
    m, out31, dx_arrived, h_far, g_own, small, dx_own, *extra = tick(
        m, out31, dx_arrived, h_far, g_own, small, dx_own, *extra
    )

    h_own, small_o = over_dp(g_own, 1, dp), over_dp(small, 1, dp)
    grad_own = (dx_own + dx_arrived.astype(F32)).astype(BF)
    g2, g1 = over_z(grad_own, 2), over_z(grad_own, 1)
    if dp == 8:
        m, grad_own = tick(m, grad_own)
        ffn_send, ffn_keep = ffn_plane(m, [parts[0]] + extra)
    else:
        ffn_send, ffn_keep = plane_any(parts, me, dp)
    final = ffn_keep.shape[2]
    m, h_own, small_o, ffn_send = tick(m, h_own, small_o, ffn_send)
    pieces = attend_weight_grads(
        m, inputs, inputs_o, dattn, dattn_o, g_own, h_own, g_far, h_far, mixed, mixed_o, small, small_o
    )
    m, ffn_send, *pieces = tick(m, ffn_send, *pieces)
    if dp == 8:
        blocks = [pieces[0]] + [over_dp(pieces[j], 2 * j, dp) for j in (1, 2, 3)]
    outputs = place(m, [outputs_own, out1, out20, out21, out30, out31], tokens, BF, rows // 2)
    m, g2, g1, ffn_send, outputs = tick(m, g2, g1, ffn_send, outputs)
    g3, ffn_arrived = over_z(g2, 1), over_z(ffn_send, 1)
    grad_inputs = place(m, [grad_own, g1, g2], tokens, F32, rows // 2)
    if dp == 8:
        m, grad_inputs, *blocks = tick(m, grad_inputs, *blocks)
        *sends, block_mine, small = local_call(
            plane_sum_kernel,
            m,
            blocks,
            [whole(part + 48, dim, dtype=BF)] * 3 + [whole(part, dim), whole(24, dim)],
            specs=[full(*blocks[0].shape)] * 4,
        )
    else:
        sends, block_mine, small = attend_any(pieces, me, dp)
    arrived = [over_z(sends[r - 1], r) for r in (1, 2, 3)]
    ffn_send, ffn_mine = local_call(
        ffn_near_kernel,
        m,
        (ffn_keep, ffn_arrived),
        [whole(2, final, dim, dtype=BF), whole(2, final, dim)],
        specs=[full(2, 2, final, dim)] * 2,
    )
    ffn_arrived = over_z(ffn_send, 2)
    step = rows // 2
    (grad_inputs,) = local_call(
        place_last_kernel,
        m,
        (grad_inputs, g3),
        [whole(tokens, dim)],
        specs=[ANY, pl.BlockSpec((step, dim), lambda i, m: (i, 0))],
        out_specs=[pl.BlockSpec((step, dim), lambda i, m: ((m[0] ^ 3) * 2 + i, 0))],
        grid=(2,),
        aliases={1: 0},
    )
    grad_up = ffn_mine[0] + ffn_arrived[0].astype(F32)
    grad_down = ffn_mine[1] + ffn_arrived[1].astype(F32)
    grad_qkv, grad_out, grad_up_bias, grad_qv_bias, *same = local_call(
        final_sum_kernel,
        m,
        (block_mine, small, *arrived),
        [whole(3, final, width), whole(width, final), whole(dim), whole(2, width)] + [whole(dim)] * 6,
        specs=[VM, VM] + [full(final + 48, dim)] * 3,
    )
    return (
        outputs,
        grad_inputs,
        grad_qkv,
        grad_qv_bias,
        grad_out,
        same[5],
        same[3],
        same[4],
        grad_up,
        grad_up_bias,
        grad_down.T,
        same[2],
        same[0],
        same[1],
    )


def scatter_any(blocks, dp):
    eight, groups, part, dim = blocks.shape
    flat = blocks.transpose(0, 2, 1, 3).reshape(eight * part, groups * dim).astype(F32)
    mine = lax.psum_scatter(flat, "dp", scatter_dimension=0, tiled=True)
    return mine.reshape(-1, groups, dim).transpose(1, 0, 2)


def order_any(by_offset, me, dp):
    mine = jnp.take(by_offset, jnp.arange(4) ^ ((me // 2) % 4), axis=0)
    other = over_dp(mine, 1, dp)
    even = jnp.where(me % 2 == 0, mine, other)
    odd = jnp.where(me % 2 == 0, other, mine)
    return jnp.stack([even, odd], 1).reshape((8,) + mine.shape[1:])


def plane_any(parts, me, dp):
    sums = jnp.stack([scatter_any(order_any(jnp.stack([p[i] for p in parts]), me, dp), dp) * 0.5 for i in range(2)])
    return sums[:, 1::2].astype(BF), sums[:, 0::2]


def attend_any(pieces, me, dp):
    pieces = jnp.stack(pieces)
    part = pieces.shape[1] // 4 // 16 * 16
    small = unpack_small(pieces[0, 4 * part :])
    blocks = pieces[:, : 4 * part].reshape(4, 4, part, -1)
    sums = scatter_any(order_any(blocks, me, dp), dp) * 0.5
    offset = 2
    while offset < dp:
        small = small + over_dp(small, offset, dp)
        offset *= 2
    packed = pack_small(small)
    sends = [jnp.concatenate([sums[r].astype(BF), packed]) for r in (1, 2, 3)]
    return sends, sums[0], unpack_small(packed)


def solution(mesh):
    placed = (
        P("dp", None),
        P(None, None, "tensor"),
        P(None, "tensor"),
        P("tensor", None),
        P(),
        P(),
        P(),
        P(None, "tensor"),
        P("tensor"),
        P("tensor", None),
        P(),
        P(),
        P(),
        P("dp"),
        P("dp", None),
    )
    return jax.shard_map(
        partial(per_device, mesh.shape["dp"]),
        mesh=mesh,
        in_specs=placed,
        out_specs=(
            P("dp", None),
            P("dp", None),
            P(None, "dp", "tensor"),
            P(None, "tensor"),
            P("tensor", "dp"),
            P(),
            P(),
            P(),
            P("dp", "tensor"),
            P("tensor"),
            P("tensor", "dp"),
            P(),
            P(),
            P(),
        ),
        check_vma=False,
    )
```

```python
from functools import partial

import jax
import jax.numpy as jnp
import numpy as np
from jax import lax
from jax.experimental import pallas as pl
from jax.experimental.pallas import tpu as pltpu
from jax.sharding import PartitionSpec as P

HEAD_DIM = 64
EPS = 1e-05
PADDED = 256
LOG2E = 1.4426950408889634
BF = jnp.bfloat16
F32 = jnp.float32
ANY = pl.BlockSpec(memory_space=pl.ANY)
HBM = pl.BlockSpec(memory_space=pltpu.HBM)
VM = pl.BlockSpec(memory_space=pltpu.VMEM)
LIMIT = 24 * 1024 * 1024


def nn(a, b):
    return lax.dot_general(a, b, (((1,), (0,)), ((), ())), preferred_element_type=F32)


def nt(a, b):
    return lax.dot_general(a, b, (((1,), (1,)), ((), ())), preferred_element_type=F32)


def cost(us):
    return pl.CostEstimate(flops=int(us * 1e3), bytes_accessed=1024, transcendentals=0)


def params(**kw):
    return pltpu.CompilerParams(vmem_limit_bytes=LIMIT, **kw)


def head_mask(rows, width, head):
    lane = lax.broadcasted_iota(jnp.int32, (rows, width), 1)
    return (lane >= head * HEAD_DIM) & (lane < (head + 1) * HEAD_DIM)


def row_norm(values):
    row_mean = jnp.mean(values, axis=-1, keepdims=True)
    centred = values - row_mean
    variance = jnp.mean(centred * centred, axis=-1, keepdims=True)
    inverse = lax.rsqrt(variance + EPS)
    return centred * inverse, inverse


def row_norm_back(grad_normed, normed, inverse):
    first_term = jnp.mean(grad_normed, axis=-1, keepdims=True)
    second_term = jnp.mean(grad_normed * normed, axis=-1, keepdims=True)
    return inverse * (grad_normed - first_term - normed * second_term)


def gelu_both(x):
    e = jnp.exp2(x * x * (-0.5 * LOG2E))
    t = 1.0 / (1.0 + (0.3275911 * 0.7071067811865476) * jnp.abs(x))
    poly = t * (
        0.5 * 0.254829592
        + t
        * (
            0.5 * -0.284496736
            + t * (0.5 * 1.421413741 + t * (0.5 * -1.453152027 + t * (0.5 * 1.061405429)))
        )
    )
    tail = poly * e
    cdf = jnp.where(x < 0, tail, 1.0 - tail)
    return x * cdf, cdf + x * (e * 0.3989422804014327)


def row_of(ref):
    return ref[...].astype(F32).reshape(1, ref.shape[0])


def whole(*shape, dtype=F32):
    return jax.ShapeDtypeStruct(shape, dtype)


def full(*shape):
    return pl.BlockSpec(shape, lambda *_: (0,) * len(shape))


def local_call(kernel, meta, args, outs, specs=None, scratch=(), us=1, out_specs=None, grid=(1,), aliases=None, near=()):
    args = [
        a if i in near or a.dtype == jnp.int32 or a.ndim < 2 else pltpu.with_memory_space_constraint(a, pltpu.HBM)
        for i, a in enumerate(args)
    ]
    return pl.pallas_call(
        kernel,
        grid_spec=pltpu.PrefetchScalarGridSpec(
            num_scalar_prefetch=1,
            grid=grid,
            in_specs=specs if specs is not None else [VM] * len(args),
            out_specs=out_specs if out_specs is not None else [VM] * len(outs),
            scratch_shapes=list(scratch),
        ),
        out_shape=list(outs),
        compiler_params=params(),
        cost_estimate=cost(us),
        input_output_aliases=aliases or {},
    )(meta, *args)


def cut_kernel(meta, up_ref, out_ref, down_ref, wt_ref, ub_ref, qvb_ref, a_ref, d_ref, q_ref, bias_s):
    lanes = a_ref.shape[1]
    up_rows, out_rows, part = up_ref.shape[0], out_ref.shape[0], wt_ref.shape[1]
    a_ref[:up_rows, :] = up_ref[...]
    a_ref[up_rows : up_rows + out_rows, :] = out_ref[...]
    bias_s[...] = jnp.zeros_like(bias_s)
    up_bias = row_of(ub_ref)
    bias_s[0:1, :] = up_bias[:, :lanes]
    bias_s[1:2, :] = up_bias[:, lanes:]
    bias_s[2:4, : qvb_ref.shape[1]] = qvb_ref[...].astype(F32)
    a_ref[up_rows + out_rows :, :] = bias_s[...].astype(BF)
    d_ref[...] = down_ref[...]
    for m in range(3):
        q_ref[m * part : (m + 1) * part, :] = wt_ref[m]


def cut(meta, up_weight, out_weight, down_weight, wt, up_bias, qv_bias):
    dim, hidden = up_weight.shape
    width = wt.shape[1]
    lanes = dim // 2
    place = lambda i, m: (m[1], m[2])
    return local_call(
        cut_kernel,
        meta,
        (up_weight, out_weight, down_weight, wt, up_bias, qv_bias),
        [
            whole(dim // 4 + width // 4 + 16, lanes, dtype=BF),
            whole(hidden // 4, lanes, dtype=BF),
            whole(3 * width // 4, lanes, dtype=BF),
        ],
        specs=[
            pl.BlockSpec((dim // 4, lanes), place),
            pl.BlockSpec((width // 4, lanes), place),
            pl.BlockSpec((hidden // 4, lanes), place),
            pl.BlockSpec((3, width // 4, lanes), lambda i, m: (0, m[1], m[2])),
            full(dim),
            full(2, width),
        ],
        scratch=[pltpu.VMEM((16, lanes), F32)],
    )


class Weights:
    def __init__(self, meta, own, pieces, scratch, sems, first, rows):
        self.meta, self.own, self.pieces, self.scratch, self.sems = meta, own, pieces, scratch, sems
        self.first, self.rows = first, rows

    def others(self, r):
        for place, piece in enumerate(self.pieces):
            quarter = self.meta[1] ^ (place % 4)
            side = self.meta[2] ^ (place // 4)
            lanes = piece.shape[2]
            start = pl.multiple_of(quarter * self.rows, 16)
            yield pltpu.make_async_copy(
                piece.at[r - 1, pl.ds(self.first, self.rows), :],
                self.scratch.at[r, pl.ds(start, self.rows), pl.ds(pl.multiple_of(side * lanes, 128), lanes)],
                self.sems.at[r, place],
            )

    def mine(self):
        return pltpu.make_async_copy(self.own, self.scratch.at[0], self.sems.at[0, 0])

    def start(self):
        self.mine().start()
        for r in range(1, 4):
            for copy in self.others(r):
                copy.start()

    def wait(self, r):
        @pl.when(r == 0)
        def _():
            self.mine().wait()

        @pl.when(r > 0)
        def _():
            for copy in self.others(r):
                copy.wait()

    def wait_all(self):
        self.mine().wait()
        for r in range(1, 4):
            for copy in self.others(r):
                copy.wait()


def split_three(rows):
    high = rows.astype(BF).astype(F32)
    middle = (rows - high).astype(BF).astype(F32)
    return high, middle, rows - high - middle


def attend_kernel(meta, x_ref, wt_ref, b_ref, down_ref, o0_ref, o1_ref, q_s, k_s, v_s, l_s):
    x = x_ref[...]
    length, width = q_s.shape
    heads = width // HEAD_DIM
    half = length // 2
    block = half // 2
    scale = HEAD_DIM ** (-0.5) * LOG2E
    q_s[...] = (nt(x, wt_ref[0]) + b_ref[0:1, :].astype(F32)).astype(BF)
    k_s[...] = nt(x, wt_ref[1]).astype(BF)
    v_s[...] = (nt(x, wt_ref[2]) + b_ref[1:2, :].astype(F32)).astype(BF)
    for k, o_ref in enumerate((o0_ref, o1_ref)):
        start = ((meta[0] % 2) ^ k) * half
        for part in range(2):
            rows = pl.ds(pl.multiple_of(start + part * block, block), block)
            q = q_s[rows, :]
            mixed = jnp.zeros((block, width), F32)
            stats = jnp.zeros((block, 128), F32)
            stat_lane = lax.broadcasted_iota(jnp.int32, (block, 128), 1)
            for h in range(heads):
                mask = head_mask(block, width, h)
                s = nt(jnp.where(mask, q, jnp.zeros_like(q)), k_s[...])
                top = jnp.max(s, axis=-1, keepdims=True)
                p = jnp.exp2((s - top) * scale)
                total = jnp.sum(p, axis=-1, keepdims=True)
                o = nn(p.astype(BF), v_s[...]) * (1.0 / total)
                mixed = jnp.where(mask, o, mixed)
                stats = jnp.where(stat_lane == h, top * scale + jnp.log2(total), stats)
            o_ref[:block, part * width : (part + 1) * width] = mixed.astype(BF)
            logs = split_three(jnp.transpose(stats)[:8, :])
            for i in range(3):
                l_s[part * 24 + i * 8 : part * 24 + i * 8 + 8, :] = logs[i]
        o_ref[block : block + 48, :block] = l_s[...].astype(BF)
        if o_ref.shape[0] > block + 48:
            o_ref[block + 48 :, :] = down_ref[...]


def attend(meta, inputs, wt, qv_bias, down_weight, length, other, carriers):
    width, dim = wt.shape[1:]
    hidden, lanes = down_weight.shape[0], dim // 2
    block = length // 4
    return local_call(
        attend_kernel,
        meta,
        (inputs, wt, qv_bias, down_weight),
        [whole(block + 48 + carried * hidden // 4, lanes, dtype=BF) for carried in carriers],
        specs=[
            pl.BlockSpec((length, dim), lambda i, m: ((m[0] // 2) ^ other, 0)),
            VM,
            full(2, width),
            pl.BlockSpec((hidden // 4, lanes), lambda i, m: (m[1], m[2])),
        ],
        out_specs=[full(block + 48 + carried * hidden // 4, lanes) for carried in carriers],
        scratch=[pltpu.VMEM((length, width), BF)] * 3 + [pltpu.VMEM((48, block), F32)],
        us=8,
    )


def up_kernel(meta, x_ref, t0, t1, t2, t3, ob_ref, ag_ref, as_ref, ub_ref, qvb_ref, wo_ref, wu_ref, *refs):
    pieces = refs[:8]
    n1_ref, r1_ref, ulow_ref, act_ref, der_ref, o_ref, lse_ref, qvb_all_ref = refs[8:16]
    wo_s, wu_s, bias_s, bias_all_s, z_s, sems = refs[16:]
    dim = x_ref.shape[1]
    lanes = dim // 2
    width = wo_ref.shape[0]
    up_rows, out_rows = wu_ref.shape[0] // 4, width // 4
    out = Weights(meta, wo_ref, pieces, wo_s, sems.at[0], up_rows, out_rows)
    up = Weights(meta, wu_ref, pieces, wu_s, sems.at[1], 0, up_rows)
    r = pl.program_id(0)

    @pl.when(r == 0)
    def _():
        rows = pl.ds(up_rows + out_rows, 16)
        biases = pltpu.make_async_copy(pieces[0].at[:, rows, :], bias_s, sems.at[0, 0, 1])
        out.start()
        biases.start()
        up.start()
        total = x_ref[...].astype(F32) + row_of(ob_ref)
        half = x_ref.shape[0] // 2
        for g, t_ref in enumerate((t0, t1, t2, t3)):
            logs = t_ref[half : half + 48, :half].astype(F32)
            for i in range(2):
                o_ref[g, i * half : (i + 1) * half, :width] = t_ref[:half, i * width : (i + 1) * width]
                lse_ref[g, :, i * half : (i + 1) * half] = (
                    logs[24 * i : 24 * i + 8] + logs[24 * i + 8 : 24 * i + 16] + logs[24 * i + 16 : 24 * i + 24]
                )
        qvb_all_ref[...] = jnp.zeros_like(qvb_all_ref)
        qvb_all_ref[0, 0:2, :width] = qvb_ref[...].astype(F32)
        bias_all_s[0, 0:1, :] = row_of(ub_ref)
        biases.wait()
        for g in range(1, 4):
            bias = bias_s[g - 1].astype(F32)
            bias_all_s[g, 0:1, :lanes] = bias[0:1]
            bias_all_s[g, 0:1, lanes:] = bias[1:2]
            qvb_all_ref[g, 0:2, :width] = bias[2:4, :width]
        out.wait_all()
        for g in range(4):
            total = total + nn(o_ref[g, :, :width], wo_s[g])
        normed, inverse = row_norm(total)
        n1_ref[...] = normed
        r1_ref[...] = inverse
        ulow_ref[...] = (normed * row_of(ag_ref) + row_of(as_ref)).astype(BF)

    up.wait(r)
    for c in range(0, dim, 256):
        z_s[...] = nn(ulow_ref[...], wu_s[r, :, c : c + 256])
        for b in range(0, z_s.shape[0], 32):
            act, der = gelu_both(z_s[b : b + 32, :] + bias_all_s[r, 0:1, c : c + 256])
            act_ref[0, b : b + 32, c : c + 256] = act.astype(BF)
            der_ref[0, b : b + 32, c : c + 256] = der.astype(BF)


def down_kernel(meta, keep_ref, n1_ref, ag_ref, as_ref, db_ref, fg_ref, fs_ref, act_ref, x_ref, cot_ref, wd_ref, *refs):
    pieces = refs[:8]
    out0_ref, out1_ref, dh2_ref, df_ref, small_ref, wd_s, acc, sems = refs[8:]
    down = Weights(meta, wd_ref, pieces, wd_s, sems, 0, wd_ref.shape[0] // 4)
    r = pl.program_id(0)

    @pl.when(r == 0)
    def _():
        down.start()
        acc[...] = n1_ref[...] * row_of(ag_ref) + (row_of(as_ref) + row_of(db_ref))

    down.wait(r)
    acc[...] += nn(act_ref[0], wd_s[r])

    @pl.when(r == 3)
    def _():
        normed, inverse = row_norm(acc[...])
        gain = row_of(fg_ref)
        keep = keep_ref[meta[0] // 2] > 0
        second = normed * gain + row_of(fs_ref)
        low = jnp.where(keep, second, x_ref[...].astype(F32)).astype(BF)
        cut_row = out0_ref.shape[0]
        out0_ref[...] = low[:cut_row]
        out1_ref[...] = low[cut_row:]
        grad = jnp.where(keep, cot_ref[...].astype(F32), 0.0)
        dh2 = row_norm_back(grad * gain, normed, inverse)
        dh2_ref[...] = dh2
        df_ref[...] = dh2.astype(BF)
        small_ref[...] = jnp.zeros_like(small_ref)
        small_ref[0:1, :] = jnp.sum(grad * normed, axis=0, keepdims=True)
        small_ref[1:2, :] = jnp.sum(grad, axis=0, keepdims=True)
        small_ref[2:3, :] = jnp.sum(dh2, axis=0, keepdims=True)


def ffn_back_kernel(meta, df_ref, dh2_ref, der_ref, wd_ref, wu_ref, *refs):
    downs, pieces = refs[:8], refs[8:16]
    dz_ref, du1_ref, small_ref, wd_s, wu_s, sems = refs[16:]
    dim = df_ref.shape[1]
    down = Weights(meta, wd_ref, downs, wd_s, sems.at[0], 0, wd_ref.shape[0] // 4)
    up = Weights(meta, wu_ref, pieces, wu_s, sems.at[1], 0, wu_ref.shape[0] // 4)
    r = pl.program_id(0)

    @pl.when(r == 0)
    def _():
        down.start()
        up.start()
        small_ref[...] = jnp.zeros_like(small_ref)
        du1_ref[...] = dh2_ref[...]

    down.wait(r)
    for c in range(0, dim, 256):
        dz = (nt(df_ref[...], wd_s[r, c : c + 256, :]) * der_ref[0, :, c : c + 256].astype(F32)).astype(BF)
        dz_ref[0, :, c : c + 256] = dz
        small_ref[pl.ds(r, 1), c : c + 256] = jnp.sum(dz.astype(F32), axis=0, keepdims=True)
    up.wait(r)
    du1_ref[...] += nt(dz_ref[0], wu_s[r])


def norm_back_kernel(meta, du1_ref, n1_ref, r1_ref, ag_ref, o_ref, wo_ref, *refs):
    pieces = refs[:8]
    dh1_ref, da_ref, do_ref, delta_ref, small_ref, wo_s, sems = refs[8:]
    width, dim = wo_ref.shape
    out = Weights(meta, wo_ref, pieces, wo_s, sems, dim // 4, width // 4)
    out.start()
    du1 = du1_ref[...]
    normed = n1_ref[...]
    small_ref[...] = jnp.zeros_like(small_ref)
    small_ref[0:1, :] = jnp.sum(du1 * normed, axis=0, keepdims=True)
    small_ref[1:2, :] = jnp.sum(du1, axis=0, keepdims=True)
    dh1 = row_norm_back(du1 * row_of(ag_ref), normed, r1_ref[...])
    small_ref[2:3, :] = jnp.sum(dh1, axis=0, keepdims=True)
    dh1_ref[...] = dh1
    da_ref[...] = dh1.astype(BF)
    out.wait_all()
    rows = du1.shape[0]
    stat_lane = lax.broadcasted_iota(jnp.int32, (rows, 128), 1)
    for r in range(4):
        do = nt(da_ref[...], wo_s[r]).astype(BF)
        do_ref[r] = do
        product = do.astype(F32) * o_ref[r, :, :width].astype(F32)
        stats = jnp.zeros((rows, 128), F32)
        for h in range(width // HEAD_DIM):
            inner = jnp.sum(jnp.where(head_mask(rows, width, h), product, 0.0), axis=-1, keepdims=True)
            stats = jnp.where(stat_lane == h, inner, stats)
        delta_ref[r] = jnp.transpose(stats)[:8, :]


def ffn_weight_kernel(meta, u_ref, v_ref, df_ref, dg_ref, dz_ref, dy_ref, act_ref, adt_ref, *refs):
    outs, (t_s, lu_s, ld_s) = refs[:4], refs[4:]
    tokens = u_ref.shape[0]
    part = outs[0].shape[2]

    @pl.when(pl.program_id(0) == 0)
    def _():
        for source, target, base in ((u_ref, lu_s, 0), (v_ref, lu_s, tokens), (df_ref, ld_s, 0), (dg_ref, ld_s, tokens)):
            t_s[...] = jnp.transpose(source[...])
            for j in range(4):
                start = pl.multiple_of((2 * (meta[1] ^ j) + meta[2]) * part, 16)
                target[j * part : (j + 1) * part, base : base + tokens] = t_s[pl.ds(start, part), :]

    for i, (left, own, other) in enumerate(((lu_s, dz_ref, dy_ref), (ld_s, act_ref, adt_ref))):
        acc = (nn(left[:, :tokens], own[0]) + nn(left[:, tokens:], other[0])).astype(BF)
        for j in range(4):
            outs[j][i, 0] = acc[j * part : (j + 1) * part, :]


def ffn_weight_grads(meta, ulow, ulow_o, dfeed, dfeed_o, dz, dz_o, act, act_o):
    rows, dim = ulow.shape
    part = dim // 8
    full = pl.BlockSpec((rows, dim), lambda r, m: (0, 0))
    group = pl.BlockSpec((1, rows, dim), lambda r, m: (r, 0, 0))
    out = pl.BlockSpec((2, 1, part, dim), lambda r, m: (0, r, 0, 0))
    return local_call(
        ffn_weight_kernel,
        meta,
        (ulow, ulow_o, dfeed, dfeed_o, dz, dz_o, act, act_o),
        [whole(2, 4, part, dim, dtype=BF)] * 4,
        specs=[full] * 4 + [group] * 4,
        out_specs=[out] * 4,
        scratch=[pltpu.VMEM((dim, rows), BF)] + [pltpu.VMEM((4 * part, 2 * rows), BF)] * 2,
        grid=(4,),
        us=9,
        near=(2, 4),
    )


def add(a, b):
    return a.astype(F32) + b.astype(F32)


def ffn_plane_kernel(meta, own, px, py, pd, send_ref, keep_ref):
    total = add(own[:, 0], px[:, 0]) + add(py[:, 0], pd[:, 0])
    near = pl.program_id(0) % 2 == 0

    @pl.when(near)
    def _():
        keep_ref[:, 0] = total

    @pl.when(jnp.logical_not(near))
    def _():
        send_ref[:, 0] = total.astype(BF)


def ffn_plane(meta, parts):
    _, groups, part, dim = parts[0].shape
    half = pl.BlockSpec((2, 1, part, dim), lambda r, m: (0, r // 2, 0, 0))
    return local_call(
        ffn_plane_kernel,
        meta,
        parts,
        [whole(2, 2, part, dim, dtype=BF), whole(2, 2, part, dim)],
        specs=[pl.BlockSpec((2, 1, part, dim), lambda r, m: (0, r, 0, 0))] * 4,
        out_specs=[half, half],
        grid=(groups,),
    )


def attend_back_kernel(own, meta, xq_ref, xk_ref, wt_ref, b_ref, do_ref, lse_ref, delta_ref, *refs):
    pieces = refs[:8]
    if own:
        dqt_ref, sd_ref, sn_ref, su_ref, sp_ref, dh1_ref, cot_ref, keep_ref, dx_ref, dkv_ref, small_ref = refs[8:19]
        w_s, sems, qm_s, dom_s, kt_s, s_s, dp_s, p_s, ds_s = refs[19:]
        base = 1
    else:
        dqt_ref, dxl_ref, dkv_ref, small_ref = refs[8:12]
        w_s, sems, qm_s, dom_s, kt_s, s_s, dp_s, p_s, ds_s, dx_ref = refs[12:]
        base = 0
    width = wt_ref.shape[1]
    heads = width // HEAD_DIM
    rows, dim = xq_ref.shape
    keys = xk_ref.shape[0]
    part = width // 4
    scale = HEAD_DIM ** (-0.5)
    r = pl.program_id(0)

    mine = [
        pltpu.make_async_copy(
            wt_ref.at[m, pl.ds(q * part, part), :], w_s.at[0, q, pl.ds(m * part, part), :], sems.at[0, m * 4 + q]
        )
        for m in range(3)
        for q in range(4)
    ]

    def others(g):
        for place, piece in enumerate(pieces):
            lanes = piece.shape[2]
            side = pl.multiple_of((meta[2] ^ (place // 4)) * lanes, 128)
            yield pltpu.make_async_copy(
                piece.at[g - 1], w_s.at[g, meta[1] ^ (place % 4), :, pl.ds(side, lanes)], sems.at[g, place]
            )

    @pl.when(r == 0)
    def _():
        for copy in mine:
            copy.start()
        for g in range(1, 4):
            for copy in others(g):
                copy.start()
        small_ref[...] = jnp.zeros_like(small_ref)
        if own:
            small_ref[0:3, :] = sd_ref[0:3, :]
            small_ref[3:6, :] = sn_ref[0:3, :]
            small_ref[8:12, :] = su_ref[0:4, :]
        dx_ref[...] = dh1_ref[...] if own else jnp.zeros_like(dx_ref)
        for copy in mine:
            copy.wait()

    @pl.when(r > 0)
    def _():
        for copy in others(r):
            copy.wait()

    wq, wk, wv = (w_s[r, :, m * part : (m + 1) * part, :].reshape(width, dim) for m in range(3))
    bias = b_ref[r][:, :width]
    q = (nt(xq_ref[...], wq) + bias[0:1, :]).astype(BF)
    k = nt(xk_ref[...], wk).astype(BF)
    v = (nt(xk_ref[...], wv) + bias[1:2, :]).astype(BF)
    do = do_ref[0]
    zero = jnp.zeros_like(q)
    for h in range(heads):
        mask = head_mask(rows, width, h)
        qm_s[h] = jnp.where(mask, q, zero)
        dom_s[h] = jnp.where(mask, do, zero)
    kt_s[...] = jnp.transpose(k)
    dqt = []
    dk = dv = None
    for h in range(heads):
        slot = h % 2
        s_s[slot] = nt(k, qm_s[h])
        dp_s[slot] = nt(v, dom_s[h])
        lse, delta = lse_ref[0, h : h + 1, :], delta_ref[0, h : h + 1, :]
        for b in range(0, keys, 32):
            p = jnp.exp2(s_s[slot, b : b + 32, :] * (scale * LOG2E) - lse)
            p_s[slot, b : b + 32, :] = p.astype(BF)
            ds_s[slot, b : b + 32, :] = (p * (dp_s[slot, b : b + 32, :] - delta)).astype(BF)
        dv_part = nn(p_s[slot], dom_s[h])
        dk_part = nn(ds_s[slot], qm_s[h])
        dqt.append(nn(kt_s[h * HEAD_DIM : (h + 1) * HEAD_DIM, :], ds_s[slot]))
        dv = dv_part if dv is None else dv + dv_part
        dk = dk_part if dk is None else dk + dk_part
    dk_low = (dk * scale).astype(BF)
    dv_low = dv.astype(BF)
    dkv_ref[base, 0, :, :width] = dk_low
    dkv_ref[base + 1, 0, :, :width] = dv_low
    dv_sum = jnp.sum(dv_low.astype(F32), axis=0, keepdims=True)
    all_heads = jnp.concatenate(dqt, axis=0)
    dx = nn(dk_low, wk) + nn(dv_low, wv)
    if own:
        dq_low = (jnp.transpose(all_heads + dqt_ref[0]) * scale).astype(BF)
        dkv_ref[0, 0, :, :width] = dq_low
        small_ref[pl.ds(12 + r, 1), :width] = jnp.sum(dq_low.astype(F32), axis=0, keepdims=True)
        small_ref[pl.ds(16 + r, 1), :width] = dv_sum + sp_ref[r, 0:1, :]
        dx = dx + nn(dq_low, wq)
    else:
        dqt_ref[0] = all_heads
        small_ref[r, 0:1, :] = dv_sum
    dx_ref[...] += dx

    @pl.when(r == 3)
    def _():
        if own:

            @pl.when(keep_ref[meta[0] // 2] <= 0)
            def _():
                dx_ref[...] = cot_ref[...].astype(F32)

        else:
            dxl_ref[...] = dx_ref[...].astype(BF)


def attend_back(meta, own, inputs, wt, bias, do, lse, delta, pieces, extra=()):
    rows, width = do.shape[1:]
    dim = inputs.shape[1]
    other = 0 if own else 1
    own_rows = pl.BlockSpec((rows, dim), lambda i, m: (m[0], 0))
    group = lambda *shape: pl.BlockSpec((1,) + shape, lambda i, m: (i,) + (0,) * len(shape))
    many = lambda count: pl.BlockSpec((count, 1, rows, PADDED), lambda i, m: (0, i, 0, 0))
    if own:
        outs = [whole(rows, dim), whole(3, 4, rows, PADDED, dtype=BF), whole(24, dim)]
        out_specs = [full(rows, dim), many(3), full(24, dim)]
    else:
        outs = [
            whole(4, width, rows),
            whole(rows, dim, dtype=BF),
            whole(2, 4, rows, PADDED, dtype=BF),
            whole(4, 8, width),
        ]
        out_specs = [group(width, rows), full(rows, dim), many(2), full(4, 8, width)]
    low = pltpu.VMEM((width // HEAD_DIM, rows, width), BF)
    return local_call(
        partial(attend_back_kernel, own),
        meta,
        (inputs, inputs, wt, bias, do, lse, delta, *pieces, *extra),
        outs,
        specs=[
            own_rows,
            pl.BlockSpec((rows, dim), lambda i, m: (m[0] ^ other, 0)),
            HBM,
            full(*bias.shape),
            group(rows, width),
            group(8, rows),
            group(8, rows),
        ]
        + [HBM] * 8
        + ([group(width, rows)] + [full(*e.shape) for e in extra[1:6]] + [own_rows, pl.BlockSpec(memory_space=pltpu.SMEM)] if own else []),
        out_specs=out_specs,
        scratch=[
            pltpu.VMEM((4, 4, 3 * width // 4, dim), BF),
            pltpu.SemaphoreType.DMA((4, 12)),
            low,
            low,
            pltpu.VMEM((width, rows), BF),
        ]
        + [pltpu.VMEM((2, rows, rows), F32)] * 2
        + [pltpu.VMEM((2, rows, rows), BF)] * 2
        + ([] if own else [pltpu.VMEM((rows, dim), F32)]),
        grid=(4,),
        us=14,
        near=(3, 4, 5, 6, 15, 16, 17, 18, 19),
    )


def attend_weight_kernel(
    meta, xq, yq, xk, yk, da, ea, g_own, h_own, g_far, h_far, o_ref, p_ref, small, small_o, p0, p1, p2, p3, t_s, lq_s, lk_s, la_s
):
    outs = (p0, p1, p2, p3)
    tokens = xq.shape[0]
    part = t_s.shape[0] // 8
    r = pl.program_id(0)

    @pl.when(r == 0)
    def _():
        pairs = ((xq, lq_s, 0), (yq, lq_s, tokens), (xk, lk_s, 0), (yk, lk_s, tokens), (da, la_s, 0), (ea, la_s, tokens))
        for source, target, base in pairs:
            t_s[...] = jnp.transpose(source[...])
            for j in range(4):
                start = pl.multiple_of((2 * (meta[1] ^ j) + meta[2]) * part, 16)
                target[j * part : (j + 1) * part, base : base + tokens] = t_s[pl.ds(start, part), :]
        packed = pack_small(small[...] + small_o[...])
        for ref in outs:
            ref[4 * part :, :] = packed

    width = t_s.shape[0] // 4
    first, second = slice(0, tokens), slice(tokens, 2 * tokens)
    both = lambda left, a, b: nn(left[:, first], a[:, :width]) + nn(left[:, second], b[:, :width])
    terms = [both(lq_s, g_own[0, 0], h_own[0, 0])]
    terms += [both(lq_s, g_own[m, 0], h_own[m, 0]) + both(lk_s, g_far[m - 1, 0], h_far[m - 1, 0]) for m in (1, 2)]
    terms.append(both(la_s, o_ref[0], p_ref[0]))
    acc = jnp.concatenate([term.astype(BF) for term in terms], axis=1)
    rows = pl.ds(pl.multiple_of(r * part, 16), part)
    for j in range(4):
        outs[j][rows, :] = acc[j * part : (j + 1) * part, :]


def attend_weight_grads(meta, inputs, inputs_o, dattn, dattn_o, g_own, h_own, g_far, h_far, mixed, mixed_o, small, small_o):
    rows, dim = dattn.shape
    width = mixed.shape[2]
    part = dim // 8
    own = pl.BlockSpec((rows, dim), lambda r, m: (m[0], 0))
    far = pl.BlockSpec((rows, dim), lambda r, m: (m[0] ^ 1, 0))
    full = pl.BlockSpec((rows, dim), lambda r, m: (0, 0))
    three = pl.BlockSpec((3, 1, rows, width), lambda r, m: (0, r, 0, 0))
    two = pl.BlockSpec((2, 1, rows, width), lambda r, m: (0, r, 0, 0))
    group = pl.BlockSpec((1, rows, width), lambda r, m: (r, 0, 0))
    left = pltpu.VMEM((4 * part, 2 * rows), BF)
    return local_call(
        attend_weight_kernel,
        meta,
        (inputs, inputs_o, inputs, inputs_o, dattn, dattn_o, g_own, h_own, g_far, h_far, mixed, mixed_o, small, small_o),
        [whole(4 * part + 48, dim, dtype=BF)] * 4,
        specs=[own, own, far, far, full, full, three, three, two, two, group, group, VM, VM],
        scratch=[pltpu.VMEM((dim, rows), BF), left, left, left],
        grid=(4,),
        us=8,
    )


def pack_small(rows):
    high = rows.astype(BF).astype(F32)
    return jnp.concatenate([high, rows - high], axis=0).astype(BF)


def unpack_small(rows):
    rows = rows.astype(F32)
    return rows[:24] + rows[24:]


def plane_sum_kernel(meta, own, px, py, pd, s1, s2, s3, keep_ref, small_ref):
    part = keep_ref.shape[0]
    for r, ref in enumerate((keep_ref, s1, s2, s3)):
        s = slice(r * part, (r + 1) * part)
        total = add(own[s, :], px[s, :]) + add(py[s, :], pd[s, :])
        ref[:part, :] = total.astype(ref.dtype)
    s = slice(4 * part, 4 * part + 48)
    small = (unpack_small(own[s, :]) + unpack_small(px[s, :])) + (unpack_small(py[s, :]) + unpack_small(pd[s, :]))
    packed = pack_small(small)
    for ref in (s1, s2, s3):
        ref[part:, :] = packed
    small_ref[...] = unpack_small(packed)


def final_sum_kernel(meta, mine, small, a1, a2, a3, gqkv_ref, gout_ref, ub_ref, qv_ref, *same_refs):
    part = mine.shape[0]
    width = gqkv_ref.shape[2]
    total = (mine[...] + a1[:part, :].astype(F32)) + add(a2[:part, :], a3[:part, :])
    for m in range(3):
        gqkv_ref[m] = total[:, m * width : (m + 1) * width]
    gout_ref[...] = jnp.transpose(total[:, 3 * width :])
    s0, s1, s2, s3 = small[...], unpack_small(a1[part:, :]), unpack_small(a2[part:, :]), unpack_small(a3[part:, :])
    same = (s0[0:8] + s1[0:8]) + (s2[0:8] + s3[0:8])
    for i, ref in enumerate(same_refs):
        ref[...] = same[i : i + 1].reshape(ref.shape)
    mine_rows = [(s0[i : i + 1] + s1[i + 1 : i + 2]) + (s2[i + 2 : i + 3] + s3[i + 3 : i + 4]) for i in (8, 12, 16)]
    ub_ref[...] = mine_rows[0].reshape(ub_ref.shape)
    qv_ref[0:1, :] = mine_rows[1][:, :width]
    qv_ref[1:2, :] = mine_rows[2][:, :width]


def place_kernel(spots, meta, *refs):
    blocks, out_ref = refs[: len(spots)], refs[len(spots)]
    wide_s, sems = refs[len(spots) + 1 :] if len(refs) > len(spots) + 2 else (None, refs[-1])
    rows = out_ref.shape[0] // 4
    copies = []
    for i, ((group, base), ref) in enumerate(zip(spots, blocks)):
        source = ref
        if wide_s is not None:
            source = wide_s.at[i]
            wide_s[i] = ref[...].astype(F32)
        start = pl.multiple_of((meta[0] ^ group) * rows + base, 16)
        copies.append(pltpu.make_async_copy(source, out_ref.at[pl.ds(start, ref.shape[0])], sems.at[i]))
        copies[-1].start()
    for copy in copies:
        copy.wait()


def place(meta, blocks, spots, tokens, dtype):
    dim = blocks[0].shape[1]
    wide = [pltpu.VMEM((len(blocks),) + blocks[0].shape, F32)] if dtype == F32 else []
    return local_call(
        partial(place_kernel, spots),
        meta,
        blocks,
        [whole(tokens, dim, dtype=dtype)],
        specs=[full(*b.shape) for b in blocks],
        out_specs=[HBM],
        scratch=wide + [pltpu.SemaphoreType.DMA((len(blocks),))],
    )[0]


def over_z(x, r):
    return lax.ppermute(x, "tensor", [(i, i ^ r) for i in range(4)])


def over_dp(x, offset, size):
    return lax.ppermute(x, "dp", [(i, i ^ offset) for i in range(size)])


def tick(*arrays):
    return lax.optimization_barrier(arrays)


def per_device(
    dp,
    inputs,
    qkv_weight,
    qv_bias,
    out_weight,
    out_bias,
    attn_gain,
    attn_shift,
    up_weight,
    up_bias,
    down_weight,
    down_bias,
    ffn_gain,
    ffn_shift,
    keep_mask,
    cotangent,
):
    tokens, dim = inputs.shape
    length = tokens // keep_mask.shape[0]
    width = qkv_weight.shape[2]
    rows = tokens // 4
    part = dim // 8
    z = lax.axis_index("tensor")
    me = lax.axis_index("dp")
    meta = jnp.stack([z, (me // 2) % 4, me % 2]).astype(jnp.int32)
    wt = qkv_weight.transpose(0, 2, 1)
    own_rows = pl.BlockSpec((rows, dim), lambda i, m: (m[0], 0))
    smem = pl.BlockSpec(memory_space=pltpu.SMEM)
    low, wide = whole(rows, dim, dtype=BF), whole(rows, dim)
    hidden_low = whole(4, rows, dim, dtype=BF)
    heads_low = whole(4, rows, width, dtype=BF)
    out_scratch = pltpu.VMEM((4, width, dim), BF)
    square = pltpu.VMEM((4, dim, dim), BF)
    group = pl.BlockSpec((1, rows, dim), lambda r, m: (r, 0, 0))
    dma = pltpu.SemaphoreType.DMA
    plane = lambda block: [over_dp(block, 2 * j, dp) for j in (1, 2, 3)]
    cores = lambda blocks: [over_dp(b, 1, dp) for b in blocks]

    a, d, q = cut(meta, up_weight, out_weight, down_weight, wt, up_bias, qv_bias)
    a1, a2, a3, d1, inputs_o = over_z(a, 1), over_z(a, 2), over_z(a, 3), over_z(d, 1), over_dp(inputs, 1, dp)
    far0, far1 = attend(meta, inputs, wt, qv_bias, down_weight, length, 1, (1, 0))
    m, a1, a2, a3, d1, inputs_o, far0, far1 = tick(meta, a1, a2, a3, d1, inputs_o, far0, far1)

    t2, t3 = over_z(far0, 2), over_z(far1, 3)
    up_out = jnp.stack([a1, a2, a3])
    up_out = [up_out] + plane(up_out)
    t0, near = attend(m, inputs, wt, qv_bias, down_weight, length, 0, (0, 0))
    m, t0, near, t2, t3, *up_out = tick(m, t0, near, t2, t3, *up_out)

    down_rows = down_weight.shape[0] // 4
    t1, d3 = over_z(near, 1), over_z(t2[-down_rows:], 1)
    up_out += cores(up_out)
    m, q, t1, d3, *up_out = tick(m, q, t1, d3, *up_out)

    down = jnp.stack([d1, t2[-down_rows:], d3])
    down = [down] + plane(down)
    q1, q2 = over_z(q, 1), over_z(q, 2)
    vector = full(dim)
    n1, r1, ulow, act, der, mixed, lse, qvb = local_call(
        up_kernel,
        m,
        (inputs, t0, t1, t2, t3, out_bias, attn_gain, attn_shift, up_bias, qv_bias, out_weight, up_weight, *up_out),
        [wide, whole(rows, 1), low, hidden_low, hidden_low, whole(4, rows, PADDED, dtype=BF), whole(4, 8, rows), whole(4, 8, 256)],
        specs=[own_rows] + [full(*t.shape) for t in (t0, t1, t2, t3)] + [vector] * 4 + [full(2, width)] + [HBM] * 10,
        out_specs=[
            full(rows, dim), full(rows, 1), full(rows, dim), group, group, full(4, rows, PADDED), full(4, 8, rows), full(4, 8, 256)
        ],
        scratch=[
            out_scratch,
            square,
            pltpu.VMEM((3, 16, dim // 2), BF),
            pltpu.VMEM((4, 8, dim), F32),
            pltpu.VMEM((rows, 256), F32),
            dma((2, 4, 8)),
        ],
        grid=(4,),
        us=12,
        near=(1, 2, 3, 4),
    )
    m, q, q1, q2, act, ulow, mixed, *down = tick(m, q, q1, q2, act, ulow, mixed, *down)

    q3 = over_z(q, 3)
    down += cores(down)
    m, act, ulow, mixed, *down = tick(m, act, ulow, mixed, *down)
    act_o, ulow_o, mixed_o = cores([act, ulow, mixed])
    first = rows * 3 // 8
    out0a, out0b, dh2, dfeed, small_down = local_call(
        down_kernel,
        m,
        (keep_mask, n1, attn_gain, attn_shift, down_bias, ffn_gain, ffn_shift, act, inputs, cotangent, down_weight, *down),
        [whole(first, dim, dtype=BF), whole(rows - first, dim, dtype=BF), wide, low, whole(8, dim)],
        specs=[smem, full(rows, dim)] + [vector] * 5 + [group] + [own_rows] * 2 + [HBM] * 9,
        out_specs=[full(first, dim), full(rows - first, dim), full(rows, dim), full(rows, dim), full(8, dim)],
        scratch=[square, pltpu.VMEM((rows, dim), F32), dma((4, 8))],
        grid=(4,),
        us=6,
        near=(1, 7),
    )
    m, q3, act_o, ulow_o, mixed_o, out0a, out0b, dfeed = tick(m, q3, act_o, ulow_o, mixed_o, out0a, out0b, dfeed)

    out2a = over_z(out0a, 2)
    qkv = jnp.stack([q1, q2, q3])
    qkv = [qkv] + plane(qkv)
    dfeed_o = over_dp(dfeed, 1, dp)
    dz, du1, small_up = local_call(
        ffn_back_kernel,
        m,
        (dfeed, dh2, der, down_weight, up_weight, *down, *up_out),
        [hidden_low, wide, whole(8, dim)],
        specs=[full(rows, dim)] * 2 + [group] + [HBM] * 18,
        out_specs=[group, full(rows, dim), full(8, dim)],
        scratch=[square, square, dma((2, 4, 8))],
        grid=(4,),
        us=10,
        near=(0, 1, 2),
    )
    m, dfeed_o, dz, out2a, out0a, out0b, *qkv = tick(m, dfeed_o, dz, out2a, out0a, out0b, *qkv)

    dz_o, out1a = over_dp(dz, 1, dp), over_z(out0a, 1)
    dh1, dattn, do, delta, small_norm = local_call(
        norm_back_kernel,
        m,
        (du1, n1, r1, attn_gain, mixed, out_weight, *up_out),
        [wide, low, heads_low, whole(4, 8, rows), whole(8, dim)],
        specs=[full(rows, dim)] * 2 + [full(rows, 1), vector, full(4, rows, PADDED)] + [HBM] * 9,
        scratch=[out_scratch, dma((4, 8))],
        us=4,
        near=(0, 1, 2, 4),
    )
    m, dz_o, out1a, dattn, out0b, out2a, *qkv = tick(m, dz_o, out1a, dattn, out0b, out2a, *qkv)

    out1b = over_z(out0b, 1)
    qkv += cores(qkv)
    parts = ffn_weight_grads(m, ulow, ulow_o, dfeed, dfeed_o, dz, dz_o, act, act_o)
    m, out1b, out0b, out2a, dattn, *rest = tick(m, out1b, out0b, out2a, dattn, *qkv, *parts)
    qkv, parts = rest[:8], rest[8:]

    out2b, out3a, dattn_o = over_z(out0b, 2), over_z(out2a, 1), over_dp(dattn, 1, dp)
    extra = []
    if dp == 8:
        extra = [over_dp(parts[1], 2, dp), over_dp(parts[2], 4, dp)]
    dqt, dx_other, g_far, small_other = attend_back(m, False, inputs, wt, qvb, do, lse, delta, qkv)
    m, out2b, out3a, dattn_o, dx_other, g_far, *rest = tick(m, out2b, out3a, dattn_o, dx_other, g_far, *parts, *extra)
    parts, extra = rest[:4], rest[4:]

    out3b, dx_arrived, h_far = over_z(out2b, 1), over_z(dx_other, 1), over_dp(g_far, 1, dp)
    if dp == 8:
        extra.append(over_dp(parts[3], 6, dp))
    dx_own, g_own, small = attend_back(
        m, True, inputs, wt, qvb, do, lse, delta, qkv,
        (dqt, small_down, small_norm, small_up, small_other, dh1, cotangent, keep_mask),
    )
    m, out3b, dx_arrived, h_far, g_own, small, dx_own, *extra = tick(
        m, out3b, dx_arrived, h_far, g_own, small, dx_own, *extra
    )

    h_own, small_o = over_dp(g_own, 1, dp), over_dp(small, 1, dp)
    grad_own = (dx_own + dx_arrived.astype(F32)).astype(BF)
    g2, g1 = over_z(grad_own, 2), over_z(grad_own, 1)
    m, h_own, small_o, grad_own = tick(m, h_own, small_o, grad_own)
    pieces = attend_weight_grads(
        m, inputs, inputs_o, dattn, dattn_o, g_own, h_own, g_far, h_far, mixed, mixed_o, small, small_o
    )
    m, *pieces = tick(m, *pieces)
    blocks = []
    if dp == 8:
        blocks = [over_dp(pieces[j], 2 * j, dp) for j in (1, 2, 3)]
        ffn_send, ffn_keep = ffn_plane(m, [parts[0]] + extra)
    else:
        ffn_send, ffn_keep = plane_any(parts, me, dp)
    final = ffn_keep.shape[2]
    places = ((0, 0), (0, first), (1, 0), (1, first), (2, 0), (2, first), (3, 0), (3, first))
    outputs = place(m, [out0a, out0b, out1a, out1b, out2a, out2b, out3a, out3b], places, tokens, BF)
    m, g2, g1, ffn_send, outputs, *rest = tick(m, g2, g1, ffn_send, outputs, *blocks[:2])
    blocks = rest + blocks[2:]
    g3, ffn_arrived = over_z(g2, 1), over_z(ffn_send, 1)
    grad_inputs = place(m, [grad_own, g1, g2], ((0, 0), (1, 0), (2, 0)), tokens, F32)
    if dp == 8:
        m, grad_inputs, *blocks = tick(m, grad_inputs, *blocks)
        *sends, block_mine, small = local_call(
            plane_sum_kernel,
            m,
            pieces[:1] + blocks,
            [whole(part + 48, dim, dtype=BF)] * 3 + [whole(part, dim), whole(24, dim)],
            specs=[full(*blocks[0].shape)] * 4,
        )
    else:
        sends, block_mine, small = attend_any(pieces, me, dp)
    arrived = [over_z(sends[r - 1], r) for r in (1, 2, 3)]
    ffn_mine = ffn_keep[:, 0] + ffn_arrived[:, 0].astype(F32)
    ffn_far = (ffn_keep[:, 1] + ffn_arrived[:, 1].astype(F32)).astype(BF)
    ffn_arrived = over_z(ffn_far, 2)
    grad_inputs = lax.dynamic_update_slice(grad_inputs, g3.astype(F32), ((z ^ 3) * rows, 0))
    grad_up = ffn_mine[0] + ffn_arrived[0].astype(F32)
    grad_down = ffn_mine[1] + ffn_arrived[1].astype(F32)
    grad_qkv, grad_out, grad_up_bias, grad_qv_bias, *same = local_call(
        final_sum_kernel,
        m,
        (block_mine, small, *arrived),
        [whole(3, final, width), whole(width, final), whole(dim), whole(2, width)] + [whole(dim)] * 6,
        specs=[VM, VM] + [full(final + 48, dim)] * 3,
    )
    return (
        outputs,
        grad_inputs,
        grad_qkv,
        grad_qv_bias,
        grad_out,
        same[5],
        same[3],
        same[4],
        grad_up,
        grad_up_bias,
        grad_down.T,
        same[2],
        same[0],
        same[1],
    )


def scatter_any(blocks, dp):
    eight, groups, part, dim = blocks.shape
    flat = blocks.transpose(0, 2, 1, 3).reshape(eight * part, groups * dim).astype(F32)
    mine = lax.psum_scatter(flat, "dp", scatter_dimension=0, tiled=True)
    return mine.reshape(-1, groups, dim).transpose(1, 0, 2)


def order_any(by_offset, me, dp):
    mine = jnp.take(by_offset, jnp.arange(4) ^ ((me // 2) % 4), axis=0)
    other = over_dp(mine, 1, dp)
    even = jnp.where(me % 2 == 0, mine, other)
    odd = jnp.where(me % 2 == 0, other, mine)
    return jnp.stack([even, odd], 1).reshape((8,) + mine.shape[1:])


def plane_any(parts, me, dp):
    sums = jnp.stack([scatter_any(order_any(jnp.stack([p[i] for p in parts]), me, dp), dp) * 0.5 for i in range(2)])
    return sums[:, 1::2].astype(BF), sums[:, 0::2]


def attend_any(pieces, me, dp):
    pieces = jnp.stack(pieces)
    part = pieces.shape[1] // 4 // 16 * 16
    small = unpack_small(pieces[0, 4 * part :])
    blocks = pieces[:, : 4 * part].reshape(4, 4, part, -1)
    sums = scatter_any(order_any(blocks, me, dp), dp) * 0.5
    offset = 2
    while offset < dp:
        small = small + over_dp(small, offset, dp)
        offset *= 2
    packed = pack_small(small)
    sends = [jnp.concatenate([sums[r].astype(BF), packed]) for r in (1, 2, 3)]
    return sends, sums[0], unpack_small(packed)


def solution(mesh):
    placed = (
        P("dp", None),
        P(None, None, "tensor"),
        P(None, "tensor"),
        P("tensor", None),
        P(),
        P(),
        P(),
        P(None, "tensor"),
        P("tensor"),
        P("tensor", None),
        P(),
        P(),
        P(),
        P("dp"),
        P("dp", None),
    )
    return jax.shard_map(
        partial(per_device, mesh.shape["dp"]),
        mesh=mesh,
        in_specs=placed,
        out_specs=(
            P("dp", None),
            P("dp", None),
            P(None, "dp", "tensor"),
            P(None, "tensor"),
            P("tensor", "dp"),
            P(),
            P(),
            P(),
            P("dp", "tensor"),
            P("tensor"),
            P("tensor", "dp"),
            P(),
            P(),
            P(),
        ),
        check_vma=False,
    )
```

```python
from functools import partial

import jax
import jax.numpy as jnp
import numpy as np
from jax import lax
from jax.experimental import pallas as pl
from jax.experimental.pallas import tpu as pltpu
from jax.sharding import PartitionSpec as P

HEAD_DIM = 64
EPS = 1e-05
PADDED = 256
LOG2E = 1.4426950408889634
BF = jnp.bfloat16
F32 = jnp.float32
ANY = pl.BlockSpec(memory_space=pl.ANY)
HBM = pl.BlockSpec(memory_space=pltpu.HBM)
VM = pl.BlockSpec(memory_space=pltpu.VMEM)
LIMIT = 24 * 1024 * 1024


def nn(a, b):
    return lax.dot_general(a, b, (((1,), (0,)), ((), ())), preferred_element_type=F32)


def nt(a, b):
    return lax.dot_general(a, b, (((1,), (1,)), ((), ())), preferred_element_type=F32)


def cost(us):
    return pl.CostEstimate(flops=int(us * 1e3), bytes_accessed=1024, transcendentals=0)


def params(**kw):
    return pltpu.CompilerParams(vmem_limit_bytes=LIMIT, **kw)


def head_mask(rows, width, head):
    lane = lax.broadcasted_iota(jnp.int32, (rows, width), 1)
    return (lane >= head * HEAD_DIM) & (lane < (head + 1) * HEAD_DIM)


def row_norm(values):
    row_mean = jnp.mean(values, axis=-1, keepdims=True)
    centred = values - row_mean
    variance = jnp.mean(centred * centred, axis=-1, keepdims=True)
    inverse = lax.rsqrt(variance + EPS)
    return centred * inverse, inverse


def row_norm_back(grad_normed, normed, inverse):
    first_term = jnp.mean(grad_normed, axis=-1, keepdims=True)
    second_term = jnp.mean(grad_normed * normed, axis=-1, keepdims=True)
    return inverse * (grad_normed - first_term - normed * second_term)


def gelu_both(x):
    e = jnp.exp2(x * x * (-0.5 * LOG2E))
    t = 1.0 / (1.0 + (0.3275911 * 0.7071067811865476) * jnp.abs(x))
    poly = t * (
        0.5 * 0.254829592
        + t
        * (
            0.5 * -0.284496736
            + t * (0.5 * 1.421413741 + t * (0.5 * -1.453152027 + t * (0.5 * 1.061405429)))
        )
    )
    tail = poly * e
    cdf = jnp.where(x < 0, tail, 1.0 - tail)
    return x * cdf, cdf + x * (e * 0.3989422804014327)


def row_of(ref):
    return ref[...].astype(F32).reshape(1, ref.shape[0])


def whole(*shape, dtype=F32):
    return jax.ShapeDtypeStruct(shape, dtype)


def full(*shape):
    return pl.BlockSpec(shape, lambda *_: (0,) * len(shape))


def local_call(kernel, meta, args, outs, specs=None, scratch=(), us=1, out_specs=None, grid=(1,), aliases=None, near=()):
    args = [
        a if i in near or a.dtype == jnp.int32 or a.ndim < 2 else pltpu.with_memory_space_constraint(a, pltpu.HBM)
        for i, a in enumerate(args)
    ]
    return pl.pallas_call(
        kernel,
        grid_spec=pltpu.PrefetchScalarGridSpec(
            num_scalar_prefetch=1,
            grid=grid,
            in_specs=specs if specs is not None else [VM] * len(args),
            out_specs=out_specs if out_specs is not None else [VM] * len(outs),
            scratch_shapes=list(scratch),
        ),
        out_shape=list(outs),
        compiler_params=params(),
        cost_estimate=cost(us),
        input_output_aliases=aliases or {},
    )(meta, *args)


def cut_kernel(meta, up_ref, out_ref, down_ref, wt_ref, ub_ref, qvb_ref, a_ref, d_ref, q_ref, bias_s):
    lanes = a_ref.shape[1]
    up_rows, out_rows, part = up_ref.shape[0], out_ref.shape[0], wt_ref.shape[1]
    a_ref[:up_rows, :] = up_ref[...]
    a_ref[up_rows : up_rows + out_rows, :] = out_ref[...]
    bias_s[...] = jnp.zeros_like(bias_s)
    up_bias = row_of(ub_ref)
    bias_s[0:1, :] = up_bias[:, :lanes]
    bias_s[1:2, :] = up_bias[:, lanes:]
    bias_s[2:4, : qvb_ref.shape[1]] = qvb_ref[...].astype(F32)
    a_ref[up_rows + out_rows :, :] = bias_s[...].astype(BF)
    d_ref[...] = down_ref[...]
    for m in range(3):
        q_ref[m * part : (m + 1) * part, :] = wt_ref[m]


def cut(meta, up_weight, out_weight, down_weight, wt, up_bias, qv_bias):
    dim, hidden = up_weight.shape
    width = wt.shape[1]
    lanes = dim // 2
    place = lambda i, m: (m[1], m[2])
    return local_call(
        cut_kernel,
        meta,
        (up_weight, out_weight, down_weight, wt, up_bias, qv_bias),
        [
            whole(dim // 4 + width // 4 + 16, lanes, dtype=BF),
            whole(hidden // 4, lanes, dtype=BF),
            whole(3 * width // 4, lanes, dtype=BF),
        ],
        specs=[
            pl.BlockSpec((dim // 4, lanes), place),
            pl.BlockSpec((width // 4, lanes), place),
            pl.BlockSpec((hidden // 4, lanes), place),
            pl.BlockSpec((3, width // 4, lanes), lambda i, m: (0, m[1], m[2])),
            full(dim),
            full(2, width),
        ],
        scratch=[pltpu.VMEM((16, lanes), F32)],
    )


class Weights:
    def __init__(self, meta, own, pieces, scratch, sems, first, rows):
        self.meta, self.own, self.pieces, self.scratch, self.sems = meta, own, pieces, scratch, sems
        self.first, self.rows = first, rows

    def others(self, r):
        for place, piece in enumerate(self.pieces):
            quarter = self.meta[1] ^ (place % 4)
            side = self.meta[2] ^ (place // 4)
            lanes = piece.shape[2]
            start = pl.multiple_of(quarter * self.rows, 16)
            yield pltpu.make_async_copy(
                piece.at[r - 1, pl.ds(self.first, self.rows), :],
                self.scratch.at[r, pl.ds(start, self.rows), pl.ds(pl.multiple_of(side * lanes, 128), lanes)],
                self.sems.at[r, place],
            )

    def mine(self):
        return pltpu.make_async_copy(self.own, self.scratch.at[0], self.sems.at[0, 0])

    def start(self):
        self.mine().start()
        for r in range(1, 4):
            for copy in self.others(r):
                copy.start()

    def wait(self, r):
        @pl.when(r == 0)
        def _():
            self.mine().wait()

        @pl.when(r > 0)
        def _():
            for copy in self.others(r):
                copy.wait()

    def wait_all(self):
        self.mine().wait()
        for r in range(1, 4):
            for copy in self.others(r):
                copy.wait()


def split_three(rows):
    high = rows.astype(BF).astype(F32)
    middle = (rows - high).astype(BF).astype(F32)
    return high, middle, rows - high - middle


def attend_kernel(meta, x_ref, wt_ref, b_ref, down_ref, o0_ref, o1_ref, q_s, k_s, v_s, l_s):
    x = x_ref[...]
    length, width = q_s.shape
    heads = width // HEAD_DIM
    half = length // 2
    block = half // 2
    scale = HEAD_DIM ** (-0.5) * LOG2E
    q_s[...] = (nt(x, wt_ref[0]) + b_ref[0:1, :].astype(F32)).astype(BF)
    k_s[...] = nt(x, wt_ref[1]).astype(BF)
    v_s[...] = (nt(x, wt_ref[2]) + b_ref[1:2, :].astype(F32)).astype(BF)
    for k, o_ref in enumerate((o0_ref, o1_ref)):
        start = ((meta[0] % 2) ^ k) * half
        for part in range(2):
            rows = pl.ds(pl.multiple_of(start + part * block, block), block)
            q = q_s[rows, :]
            mixed = jnp.zeros((block, width), F32)
            stats = jnp.zeros((block, 128), F32)
            stat_lane = lax.broadcasted_iota(jnp.int32, (block, 128), 1)
            for h in range(heads):
                mask = head_mask(block, width, h)
                s = nt(jnp.where(mask, q, jnp.zeros_like(q)), k_s[...])
                top = jnp.max(s, axis=-1, keepdims=True)
                p = jnp.exp2((s - top) * scale)
                total = jnp.sum(p, axis=-1, keepdims=True)
                o = nn(p.astype(BF), v_s[...]) * (1.0 / total)
                mixed = jnp.where(mask, o, mixed)
                stats = jnp.where(stat_lane == h, top * scale + jnp.log2(total), stats)
            o_ref[:block, part * width : (part + 1) * width] = mixed.astype(BF)
            logs = split_three(jnp.transpose(stats)[:8, :])
            for i in range(3):
                l_s[part * 24 + i * 8 : part * 24 + i * 8 + 8, :] = logs[i]
        o_ref[block : block + 48, :block] = l_s[...].astype(BF)
        if o_ref.shape[0] > block + 48:
            o_ref[block + 48 :, :] = down_ref[...]


def attend(meta, inputs, wt, qv_bias, down_weight, length, other, carriers):
    width, dim = wt.shape[1:]
    hidden, lanes = down_weight.shape[0], dim // 2
    block = length // 4
    return local_call(
        attend_kernel,
        meta,
        (inputs, wt, qv_bias, down_weight),
        [whole(block + 48 + carried * hidden // 4, lanes, dtype=BF) for carried in carriers],
        specs=[
            pl.BlockSpec((length, dim), lambda i, m: ((m[0] // 2) ^ other, 0)),
            VM,
            full(2, width),
            pl.BlockSpec((hidden // 4, lanes), lambda i, m: (m[1], m[2])),
        ],
        out_specs=[full(block + 48 + carried * hidden // 4, lanes) for carried in carriers],
        scratch=[pltpu.VMEM((length, width), BF)] * 3 + [pltpu.VMEM((48, block), F32)],
        us=8,
    )


def up_kernel(meta, x_ref, t0, t1, t2, t3, ob_ref, ag_ref, as_ref, ub_ref, qvb_ref, wo_ref, wu_ref, *refs):
    pieces = refs[:8]
    n1_ref, r1_ref, ulow_ref, act_ref, der_ref, o_ref, lse_ref, qvb_all_ref = refs[8:16]
    wo_s, wu_s, bias_s, bias_all_s, z_s, sems = refs[16:]
    dim = x_ref.shape[1]
    lanes = dim // 2
    width = wo_ref.shape[0]
    up_rows, out_rows = wu_ref.shape[0] // 4, width // 4
    out = Weights(meta, wo_ref, pieces, wo_s, sems.at[0], up_rows, out_rows)
    up = Weights(meta, wu_ref, pieces, wu_s, sems.at[1], 0, up_rows)
    r = pl.program_id(0)

    @pl.when(r == 0)
    def _():
        rows = pl.ds(up_rows + out_rows, 16)
        biases = pltpu.make_async_copy(pieces[0].at[:, rows, :], bias_s, sems.at[0, 0, 1])
        out.start()
        biases.start()
        up.start()
        total = x_ref[...].astype(F32) + row_of(ob_ref)
        half = x_ref.shape[0] // 2
        for g, t_ref in enumerate((t0, t1, t2, t3)):
            logs = t_ref[half : half + 48, :half].astype(F32)
            for i in range(2):
                o_ref[g, i * half : (i + 1) * half, :width] = t_ref[:half, i * width : (i + 1) * width]
                lse_ref[g, :, i * half : (i + 1) * half] = (
                    logs[24 * i : 24 * i + 8] + logs[24 * i + 8 : 24 * i + 16] + logs[24 * i + 16 : 24 * i + 24]
                )
        qvb_all_ref[...] = jnp.zeros_like(qvb_all_ref)
        qvb_all_ref[0, 0:2, :width] = qvb_ref[...].astype(F32)
        bias_all_s[0, 0:1, :] = row_of(ub_ref)
        biases.wait()
        for g in range(1, 4):
            bias = bias_s[g - 1].astype(F32)
            bias_all_s[g, 0:1, :lanes] = bias[0:1]
            bias_all_s[g, 0:1, lanes:] = bias[1:2]
            qvb_all_ref[g, 0:2, :width] = bias[2:4, :width]
        out.wait_all()
        for g in range(4):
            total = total + nn(o_ref[g, :, :width], wo_s[g])
        normed, inverse = row_norm(total)
        n1_ref[...] = normed
        r1_ref[...] = inverse
        ulow_ref[...] = (normed * row_of(ag_ref) + row_of(as_ref)).astype(BF)

    up.wait(r)
    for c in range(0, dim, 256):
        z_s[...] = nn(ulow_ref[...], wu_s[r, :, c : c + 256])
        for b in range(0, z_s.shape[0], 32):
            act, der = gelu_both(z_s[b : b + 32, :] + bias_all_s[r, 0:1, c : c + 256])
            act_ref[0, b : b + 32, c : c + 256] = act.astype(BF)
            der_ref[0, b : b + 32, c : c + 256] = der.astype(BF)


def down_kernel(meta, keep_ref, n1_ref, ag_ref, as_ref, db_ref, fg_ref, fs_ref, act_ref, x_ref, cot_ref, wd_ref, *refs):
    pieces = refs[:8]
    out0_ref, out1_ref, dh2_ref, df_ref, small_ref, wd_s, acc, sems = refs[8:]
    down = Weights(meta, wd_ref, pieces, wd_s, sems, 0, wd_ref.shape[0] // 4)
    r = pl.program_id(0)

    @pl.when(r == 0)
    def _():
        down.start()
        acc[...] = n1_ref[...] * row_of(ag_ref) + (row_of(as_ref) + row_of(db_ref))

    down.wait(r)
    acc[...] += nn(act_ref[0], wd_s[r])

    @pl.when(r == 3)
    def _():
        normed, inverse = row_norm(acc[...])
        gain = row_of(fg_ref)
        keep = keep_ref[meta[0] // 2] > 0
        second = normed * gain + row_of(fs_ref)
        low = jnp.where(keep, second, x_ref[...].astype(F32)).astype(BF)
        cut_row = out0_ref.shape[0]
        out0_ref[...] = low[:cut_row]
        out1_ref[...] = low[cut_row:]
        grad = jnp.where(keep, cot_ref[...].astype(F32), 0.0)
        dh2 = row_norm_back(grad * gain, normed, inverse)
        dh2_ref[...] = dh2
        df_ref[...] = dh2.astype(BF)
        small_ref[...] = jnp.zeros_like(small_ref)
        small_ref[0:1, :] = jnp.sum(grad * normed, axis=0, keepdims=True)
        small_ref[1:2, :] = jnp.sum(grad, axis=0, keepdims=True)
        small_ref[2:3, :] = jnp.sum(dh2, axis=0, keepdims=True)


def ffn_back_kernel(meta, df_ref, dh2_ref, der_ref, wd_ref, wu_ref, *refs):
    downs, pieces = refs[:8], refs[8:16]
    dz_ref, du1_ref, small_ref, wd_s, wu_s, sems = refs[16:]
    dim = df_ref.shape[1]
    down = Weights(meta, wd_ref, downs, wd_s, sems.at[0], 0, wd_ref.shape[0] // 4)
    up = Weights(meta, wu_ref, pieces, wu_s, sems.at[1], 0, wu_ref.shape[0] // 4)
    r = pl.program_id(0)

    @pl.when(r == 0)
    def _():
        down.start()
        up.start()
        small_ref[...] = jnp.zeros_like(small_ref)
        du1_ref[...] = dh2_ref[...]

    down.wait(r)
    for c in range(0, dim, 256):
        dz = (nt(df_ref[...], wd_s[r, c : c + 256, :]) * der_ref[0, :, c : c + 256].astype(F32)).astype(BF)
        dz_ref[0, :, c : c + 256] = dz
        small_ref[pl.ds(r, 1), c : c + 256] = jnp.sum(dz.astype(F32), axis=0, keepdims=True)
    up.wait(r)
    du1_ref[...] += nt(dz_ref[0], wu_s[r])


def norm_back_kernel(meta, du1_ref, n1_ref, r1_ref, ag_ref, o_ref, wo_ref, *refs):
    pieces = refs[:8]
    dh1_ref, da_ref, do_ref, delta_ref, small_ref, wo_s, sems = refs[8:]
    width, dim = wo_ref.shape
    out = Weights(meta, wo_ref, pieces, wo_s, sems, dim // 4, width // 4)
    out.start()
    du1 = du1_ref[...]
    normed = n1_ref[...]
    small_ref[...] = jnp.zeros_like(small_ref)
    small_ref[0:1, :] = jnp.sum(du1 * normed, axis=0, keepdims=True)
    small_ref[1:2, :] = jnp.sum(du1, axis=0, keepdims=True)
    dh1 = row_norm_back(du1 * row_of(ag_ref), normed, r1_ref[...])
    small_ref[2:3, :] = jnp.sum(dh1, axis=0, keepdims=True)
    dh1_ref[...] = dh1
    da_ref[...] = dh1.astype(BF)
    out.wait_all()
    rows = du1.shape[0]
    stat_lane = lax.broadcasted_iota(jnp.int32, (rows, 128), 1)
    for r in range(4):
        do = nt(da_ref[...], wo_s[r]).astype(BF)
        do_ref[r] = do
        product = do.astype(F32) * o_ref[r, :, :width].astype(F32)
        stats = jnp.zeros((rows, 128), F32)
        for h in range(width // HEAD_DIM):
            inner = jnp.sum(jnp.where(head_mask(rows, width, h), product, 0.0), axis=-1, keepdims=True)
            stats = jnp.where(stat_lane == h, inner, stats)
        delta_ref[r] = jnp.transpose(stats)[:8, :]


def ffn_weight_kernel(meta, u_ref, v_ref, df_ref, dg_ref, dz_ref, dy_ref, act_ref, adt_ref, *refs):
    outs, (t_s, lu_s, ld_s) = refs[:4], refs[4:]
    tokens = u_ref.shape[0]
    part = outs[0].shape[2]

    @pl.when(pl.program_id(0) == 0)
    def _():
        for source, target, base in ((u_ref, lu_s, 0), (v_ref, lu_s, tokens), (df_ref, ld_s, 0), (dg_ref, ld_s, tokens)):
            t_s[...] = jnp.transpose(source[...])
            for j in range(4):
                start = pl.multiple_of((2 * (meta[1] ^ j) + meta[2]) * part, 16)
                target[j * part : (j + 1) * part, base : base + tokens] = t_s[pl.ds(start, part), :]

    for i, (left, own, other) in enumerate(((lu_s, dz_ref, dy_ref), (ld_s, act_ref, adt_ref))):
        acc = (nn(left[:, :tokens], own[0]) + nn(left[:, tokens:], other[0])).astype(BF)
        for j in range(4):
            outs[j][i, 0] = acc[j * part : (j + 1) * part, :]


def ffn_weight_grads(meta, ulow, ulow_o, dfeed, dfeed_o, dz, dz_o, act, act_o):
    rows, dim = ulow.shape
    part = dim // 8
    full = pl.BlockSpec((rows, dim), lambda r, m: (0, 0))
    group = pl.BlockSpec((1, rows, dim), lambda r, m: (r, 0, 0))
    out = pl.BlockSpec((2, 1, part, dim), lambda r, m: (0, r, 0, 0))
    return local_call(
        ffn_weight_kernel,
        meta,
        (ulow, ulow_o, dfeed, dfeed_o, dz, dz_o, act, act_o),
        [whole(2, 4, part, dim, dtype=BF)] * 4,
        specs=[full] * 4 + [group] * 4,
        out_specs=[out] * 4,
        scratch=[pltpu.VMEM((dim, rows), BF)] + [pltpu.VMEM((4 * part, 2 * rows), BF)] * 2,
        grid=(4,),
        us=9,
        near=(2, 4),
    )


def add(a, b):
    return a.astype(F32) + b.astype(F32)


def ffn_plane_kernel(meta, own, px, py, pd, send_ref, keep_ref):
    total = add(own[:, 0], px[:, 0]) + add(py[:, 0], pd[:, 0])
    near = pl.program_id(0) % 2 == 0

    @pl.when(near)
    def _():
        keep_ref[:, 0] = total

    @pl.when(jnp.logical_not(near))
    def _():
        send_ref[:, 0] = total.astype(BF)


def ffn_plane(meta, parts):
    _, groups, part, dim = parts[0].shape
    half = pl.BlockSpec((2, 1, part, dim), lambda r, m: (0, r // 2, 0, 0))
    return local_call(
        ffn_plane_kernel,
        meta,
        parts,
        [whole(2, 2, part, dim, dtype=BF), whole(2, 2, part, dim)],
        specs=[pl.BlockSpec((2, 1, part, dim), lambda r, m: (0, r, 0, 0))] * 4,
        out_specs=[half, half],
        grid=(groups,),
    )


def attend_back_kernel(own, meta, xq_ref, xk_ref, wt_ref, b_ref, do_ref, lse_ref, delta_ref, *refs):
    pieces = refs[:8]
    if own:
        dqt_ref, sd_ref, sn_ref, su_ref, sp_ref, dh1_ref, cot_ref, keep_ref, dx_ref, dkv_ref, small_ref = refs[8:19]
        w_s, sems, qm_s, dom_s, kt_s, s_s, dp_s, p_s, ds_s = refs[19:]
        base = 1
    else:
        dqt_ref, dxl_ref, dkv_ref, small_ref = refs[8:12]
        w_s, sems, qm_s, dom_s, kt_s, s_s, dp_s, p_s, ds_s, dx_ref = refs[12:]
        base = 0
    width = wt_ref.shape[1]
    heads = width // HEAD_DIM
    rows, dim = xq_ref.shape
    keys = xk_ref.shape[0]
    part = width // 4
    scale = HEAD_DIM ** (-0.5)
    r = pl.program_id(0)

    mine = [
        pltpu.make_async_copy(
            wt_ref.at[m, pl.ds(q * part, part), :], w_s.at[0, q, pl.ds(m * part, part), :], sems.at[0, m * 4 + q]
        )
        for m in range(3)
        for q in range(4)
    ]

    def others(g):
        for place, piece in enumerate(pieces):
            lanes = piece.shape[2]
            side = pl.multiple_of((meta[2] ^ (place // 4)) * lanes, 128)
            yield pltpu.make_async_copy(
                piece.at[g - 1], w_s.at[g, meta[1] ^ (place % 4), :, pl.ds(side, lanes)], sems.at[g, place]
            )

    @pl.when(r == 0)
    def _():
        for copy in mine:
            copy.start()
        for g in range(1, 4):
            for copy in others(g):
                copy.start()
        small_ref[...] = jnp.zeros_like(small_ref)
        if own:
            small_ref[0:3, :] = sd_ref[0:3, :]
            small_ref[3:6, :] = sn_ref[0:3, :]
            small_ref[8:12, :] = su_ref[0:4, :]
        dx_ref[...] = dh1_ref[...] if own else jnp.zeros_like(dx_ref)
        for copy in mine:
            copy.wait()

    @pl.when(r > 0)
    def _():
        for copy in others(r):
            copy.wait()

    wq, wk, wv = (w_s[r, :, m * part : (m + 1) * part, :].reshape(width, dim) for m in range(3))
    bias = b_ref[r][:, :width]
    q = (nt(xq_ref[...], wq) + bias[0:1, :]).astype(BF)
    k = nt(xk_ref[...], wk).astype(BF)
    v = (nt(xk_ref[...], wv) + bias[1:2, :]).astype(BF)
    do = do_ref[0]
    zero = jnp.zeros_like(q)
    for h in range(heads):
        mask = head_mask(rows, width, h)
        qm_s[h] = jnp.where(mask, q, zero)
        dom_s[h] = jnp.where(mask, do, zero)
    kt_s[...] = jnp.transpose(k)
    dqt = []
    dk = dv = None
    for h in range(heads):
        slot = h % 2
        s_s[slot] = nt(k, qm_s[h])
        dp_s[slot] = nt(v, dom_s[h])
        lse, delta = lse_ref[0, h : h + 1, :], delta_ref[0, h : h + 1, :]
        for b in range(0, keys, 32):
            p = jnp.exp2(s_s[slot, b : b + 32, :] * (scale * LOG2E) - lse)
            p_s[slot, b : b + 32, :] = p.astype(BF)
            ds_s[slot, b : b + 32, :] = (p * (dp_s[slot, b : b + 32, :] - delta)).astype(BF)
        dv_part = nn(p_s[slot], dom_s[h])
        dk_part = nn(ds_s[slot], qm_s[h])
        dqt.append(nn(kt_s[h * HEAD_DIM : (h + 1) * HEAD_DIM, :], ds_s[slot]))
        dv = dv_part if dv is None else dv + dv_part
        dk = dk_part if dk is None else dk + dk_part
    dk_low = (dk * scale).astype(BF)
    dv_low = dv.astype(BF)
    dkv_ref[base, 0, :, :width] = dk_low
    dkv_ref[base + 1, 0, :, :width] = dv_low
    dv_sum = jnp.sum(dv_low.astype(F32), axis=0, keepdims=True)
    all_heads = jnp.concatenate(dqt, axis=0)
    dx = nn(dk_low, wk) + nn(dv_low, wv)
    if own:
        dq_low = (jnp.transpose(all_heads + dqt_ref[0]) * scale).astype(BF)
        dkv_ref[0, 0, :, :width] = dq_low
        small_ref[pl.ds(12 + r, 1), :width] = jnp.sum(dq_low.astype(F32), axis=0, keepdims=True)
        small_ref[pl.ds(16 + r, 1), :width] = dv_sum + sp_ref[r, 0:1, :]
        dx = dx + nn(dq_low, wq)
    else:
        dqt_ref[0] = all_heads
        small_ref[r, 0:1, :] = dv_sum
    dx_ref[...] += dx

    @pl.when(r == 3)
    def _():
        if own:

            @pl.when(keep_ref[meta[0] // 2] <= 0)
            def _():
                dx_ref[...] = cot_ref[...].astype(F32)

        else:
            dxl_ref[...] = dx_ref[...].astype(BF)


def attend_back(meta, own, inputs, wt, bias, do, lse, delta, pieces, extra=()):
    rows, width = do.shape[1:]
    dim = inputs.shape[1]
    other = 0 if own else 1
    own_rows = pl.BlockSpec((rows, dim), lambda i, m: (m[0], 0))
    group = lambda *shape: pl.BlockSpec((1,) + shape, lambda i, m: (i,) + (0,) * len(shape))
    many = lambda count: pl.BlockSpec((count, 1, rows, PADDED), lambda i, m: (0, i, 0, 0))
    if own:
        outs = [whole(rows, dim), whole(3, 4, rows, PADDED, dtype=BF), whole(24, dim)]
        out_specs = [full(rows, dim), many(3), full(24, dim)]
    else:
        outs = [
            whole(4, width, rows),
            whole(rows, dim, dtype=BF),
            whole(2, 4, rows, PADDED, dtype=BF),
            whole(4, 8, width),
        ]
        out_specs = [group(width, rows), full(rows, dim), many(2), full(4, 8, width)]
    low = pltpu.VMEM((width // HEAD_DIM, rows, width), BF)
    return local_call(
        partial(attend_back_kernel, own),
        meta,
        (inputs, inputs, wt, bias, do, lse, delta, *pieces, *extra),
        outs,
        specs=[
            own_rows,
            pl.BlockSpec((rows, dim), lambda i, m: (m[0] ^ other, 0)),
            HBM,
            full(*bias.shape),
            group(rows, width),
            group(8, rows),
            group(8, rows),
        ]
        + [HBM] * 8
        + ([group(width, rows)] + [full(*e.shape) for e in extra[1:6]] + [own_rows, pl.BlockSpec(memory_space=pltpu.SMEM)] if own else []),
        out_specs=out_specs,
        scratch=[
            pltpu.VMEM((4, 4, 3 * width // 4, dim), BF),
            pltpu.SemaphoreType.DMA((4, 12)),
            low,
            low,
            pltpu.VMEM((width, rows), BF),
        ]
        + [pltpu.VMEM((2, rows, rows), F32)] * 2
        + [pltpu.VMEM((2, rows, rows), BF)] * 2
        + ([] if own else [pltpu.VMEM((rows, dim), F32)]),
        grid=(4,),
        us=14,
        near=(3, 4, 5, 6, 15, 16, 17, 18, 19),
    )


def attend_weight_kernel(
    meta, xq, yq, xk, yk, da, ea, g_own, h_own, g_far, h_far, o_ref, p_ref, small, small_o, p0, p1, p2, p3, t_s, lq_s, lk_s, la_s
):
    outs = (p0, p1, p2, p3)
    tokens = xq.shape[0]
    part = t_s.shape[0] // 8
    r = pl.program_id(0)

    @pl.when(r == 0)
    def _():
        pairs = ((xq, lq_s, 0), (yq, lq_s, tokens), (xk, lk_s, 0), (yk, lk_s, tokens), (da, la_s, 0), (ea, la_s, tokens))
        for source, target, base in pairs:
            t_s[...] = jnp.transpose(source[...])
            for j in range(4):
                start = pl.multiple_of((2 * (meta[1] ^ j) + meta[2]) * part, 16)
                target[j * part : (j + 1) * part, base : base + tokens] = t_s[pl.ds(start, part), :]
        packed = pack_small(small[...] + small_o[...])
        for ref in outs:
            ref[4 * part :, :] = packed

    width = t_s.shape[0] // 4
    first, second = slice(0, tokens), slice(tokens, 2 * tokens)
    both = lambda left, a, b: nn(left[:, first], a[:, :width]) + nn(left[:, second], b[:, :width])
    terms = [both(lq_s, g_own[0, 0], h_own[0, 0])]
    terms += [both(lq_s, g_own[m, 0], h_own[m, 0]) + both(lk_s, g_far[m - 1, 0], h_far[m - 1, 0]) for m in (1, 2)]
    terms.append(both(la_s, o_ref[0], p_ref[0]))
    acc = jnp.concatenate([term.astype(BF) for term in terms], axis=1)
    rows = pl.ds(pl.multiple_of(r * part, 16), part)
    for j in range(4):
        outs[j][rows, :] = acc[j * part : (j + 1) * part, :]


def attend_weight_grads(meta, inputs, inputs_o, dattn, dattn_o, g_own, h_own, g_far, h_far, mixed, mixed_o, small, small_o):
    rows, dim = dattn.shape
    width = mixed.shape[2]
    part = dim // 8
    own = pl.BlockSpec((rows, dim), lambda r, m: (m[0], 0))
    far = pl.BlockSpec((rows, dim), lambda r, m: (m[0] ^ 1, 0))
    full = pl.BlockSpec((rows, dim), lambda r, m: (0, 0))
    three = pl.BlockSpec((3, 1, rows, width), lambda r, m: (0, r, 0, 0))
    two = pl.BlockSpec((2, 1, rows, width), lambda r, m: (0, r, 0, 0))
    group = pl.BlockSpec((1, rows, width), lambda r, m: (r, 0, 0))
    left = pltpu.VMEM((4 * part, 2 * rows), BF)
    return local_call(
        attend_weight_kernel,
        meta,
        (inputs, inputs_o, inputs, inputs_o, dattn, dattn_o, g_own, h_own, g_far, h_far, mixed, mixed_o, small, small_o),
        [whole(4 * part + 48, dim, dtype=BF)] * 4,
        specs=[own, own, far, far, full, full, three, three, two, two, group, group, VM, VM],
        scratch=[pltpu.VMEM((dim, rows), BF), left, left, left],
        grid=(4,),
        us=8,
        near=(6, 7, 12, 13),
    )


def pack_small(rows):
    high = rows.astype(BF).astype(F32)
    return jnp.concatenate([high, rows - high], axis=0).astype(BF)


def unpack_small(rows):
    rows = rows.astype(F32)
    return rows[:24] + rows[24:]


def plane_sum_kernel(meta, own, px, py, pd, s1, s2, s3, keep_ref, small_ref):
    part = keep_ref.shape[0]
    for r, ref in enumerate((keep_ref, s1, s2, s3)):
        s = slice(r * part, (r + 1) * part)
        total = add(own[s, :], px[s, :]) + add(py[s, :], pd[s, :])
        ref[:part, :] = total.astype(ref.dtype)
    s = slice(4 * part, 4 * part + 48)
    small = (unpack_small(own[s, :]) + unpack_small(px[s, :])) + (unpack_small(py[s, :]) + unpack_small(pd[s, :]))
    packed = pack_small(small)
    for ref in (s1, s2, s3):
        ref[part:, :] = packed
    small_ref[...] = unpack_small(packed)


def final_sum_kernel(meta, mine, small, a1, a2, a3, gqkv_ref, gout_ref, ub_ref, qv_ref, *same_refs):
    part = mine.shape[0]
    width = gqkv_ref.shape[2]
    total = (mine[...] + a1[:part, :].astype(F32)) + add(a2[:part, :], a3[:part, :])
    for m in range(3):
        gqkv_ref[m] = total[:, m * width : (m + 1) * width]
    gout_ref[...] = jnp.transpose(total[:, 3 * width :])
    s0, s1, s2, s3 = small[...], unpack_small(a1[part:, :]), unpack_small(a2[part:, :]), unpack_small(a3[part:, :])
    same = (s0[0:8] + s1[0:8]) + (s2[0:8] + s3[0:8])
    for i, ref in enumerate(same_refs):
        ref[...] = same[i : i + 1].reshape(ref.shape)
    mine_rows = [(s0[i : i + 1] + s1[i + 1 : i + 2]) + (s2[i + 2 : i + 3] + s3[i + 3 : i + 4]) for i in (8, 12, 16)]
    ub_ref[...] = mine_rows[0].reshape(ub_ref.shape)
    qv_ref[0:1, :] = mine_rows[1][:, :width]
    qv_ref[1:2, :] = mine_rows[2][:, :width]


def place_kernel(spots, meta, *refs):
    blocks, out_ref = refs[: len(spots)], refs[len(spots)]
    wide_s, sems = refs[len(spots) + 1 :] if len(refs) > len(spots) + 2 else (None, refs[-1])
    rows = out_ref.shape[0] // 4
    copies = []
    for i, ((group, base), ref) in enumerate(zip(spots, blocks)):
        source = ref
        if wide_s is not None:
            source = wide_s.at[i]
            wide_s[i] = ref[...].astype(F32)
        start = pl.multiple_of((meta[0] ^ group) * rows + base, 16)
        copies.append(pltpu.make_async_copy(source, out_ref.at[pl.ds(start, ref.shape[0])], sems.at[i]))
        copies[-1].start()
    for copy in copies:
        copy.wait()


def place(meta, blocks, spots, tokens, dtype):
    dim = blocks[0].shape[1]
    wide = [pltpu.VMEM((len(blocks),) + blocks[0].shape, F32)] if dtype == F32 else []
    return local_call(
        partial(place_kernel, spots),
        meta,
        blocks,
        [whole(tokens, dim, dtype=dtype)],
        specs=[full(*b.shape) for b in blocks],
        out_specs=[HBM],
        scratch=wide + [pltpu.SemaphoreType.DMA((len(blocks),))],
        near=tuple(range(len(blocks))),
    )[0]


def over_z(x, r):
    return lax.ppermute(x, "tensor", [(i, i ^ r) for i in range(4)])


def over_dp(x, offset, size):
    return lax.ppermute(x, "dp", [(i, i ^ offset) for i in range(size)])


def tick(*arrays):
    return lax.optimization_barrier(arrays)


def per_device(
    dp,
    inputs,
    qkv_weight,
    qv_bias,
    out_weight,
    out_bias,
    attn_gain,
    attn_shift,
    up_weight,
    up_bias,
    down_weight,
    down_bias,
    ffn_gain,
    ffn_shift,
    keep_mask,
    cotangent,
):
    tokens, dim = inputs.shape
    length = tokens // keep_mask.shape[0]
    width = qkv_weight.shape[2]
    rows = tokens // 4
    part = dim // 8
    z = lax.axis_index("tensor")
    me = lax.axis_index("dp")
    meta = jnp.stack([z, (me // 2) % 4, me % 2]).astype(jnp.int32)
    wt = qkv_weight.transpose(0, 2, 1)
    own_rows = pl.BlockSpec((rows, dim), lambda i, m: (m[0], 0))
    smem = pl.BlockSpec(memory_space=pltpu.SMEM)
    low, wide = whole(rows, dim, dtype=BF), whole(rows, dim)
    hidden_low = whole(4, rows, dim, dtype=BF)
    heads_low = whole(4, rows, width, dtype=BF)
    out_scratch = pltpu.VMEM((4, width, dim), BF)
    square = pltpu.VMEM((4, dim, dim), BF)
    group = pl.BlockSpec((1, rows, dim), lambda r, m: (r, 0, 0))
    dma = pltpu.SemaphoreType.DMA
    plane = lambda block: [over_dp(block, 2 * j, dp) for j in (1, 2, 3)]
    cores = lambda blocks: [over_dp(b, 1, dp) for b in blocks]

    a, d, q = cut(meta, up_weight, out_weight, down_weight, wt, up_bias, qv_bias)
    a1, a2, a3, d1, inputs_o = over_z(a, 1), over_z(a, 2), over_z(a, 3), over_z(d, 1), over_dp(inputs, 1, dp)
    far0, far1 = attend(meta, inputs, wt, qv_bias, down_weight, length, 1, (1, 0))
    m, a1, a2, a3, d1, inputs_o, far0, far1 = tick(meta, a1, a2, a3, d1, inputs_o, far0, far1)

    t2, t3 = over_z(far0, 2), over_z(far1, 3)
    up_out = jnp.stack([a1, a2, a3])
    up_out = [up_out] + plane(up_out)
    t0, near = attend(m, inputs, wt, qv_bias, down_weight, length, 0, (0, 0))
    m, t0, near, t2, t3, *up_out = tick(m, t0, near, t2, t3, *up_out)

    down_rows = down_weight.shape[0] // 4
    d3 = over_z(t2[-down_rows:], 1)
    up_out += cores(up_out)
    m, q, near, d3, *up_out = tick(m, q, near, d3, *up_out)

    t1 = over_z(near, 1)
    down = jnp.stack([d1, t2[-down_rows:], d3])
    down = [down] + plane(down)
    m, t1, q = tick(m, t1, q)
    q1, q2 = over_z(q, 1), over_z(q, 2)
    vector = full(dim)
    n1, r1, ulow, act, der, mixed, lse, qvb = local_call(
        up_kernel,
        m,
        (inputs, t0, t1, t2, t3, out_bias, attn_gain, attn_shift, up_bias, qv_bias, out_weight, up_weight, *up_out),
        [wide, whole(rows, 1), low, hidden_low, hidden_low, whole(4, rows, PADDED, dtype=BF), whole(4, 8, rows), whole(4, 8, 256)],
        specs=[own_rows] + [full(*t.shape) for t in (t0, t1, t2, t3)] + [vector] * 4 + [full(2, width)] + [HBM] * 10,
        out_specs=[
            full(rows, dim), full(rows, 1), full(rows, dim), group, group, full(4, rows, PADDED), full(4, 8, rows), full(4, 8, 256)
        ],
        scratch=[
            out_scratch,
            square,
            pltpu.VMEM((3, 16, dim // 2), BF),
            pltpu.VMEM((4, 8, dim), F32),
            pltpu.VMEM((rows, 256), F32),
            dma((2, 4, 8)),
        ],
        grid=(4,),
        us=12,
        near=(1, 2, 3, 4),
    )
    m, q, q1, q2, act, ulow, mixed, *down = tick(m, q, q1, q2, act, ulow, mixed, *down)

    q3 = over_z(q, 3)
    down += cores(down)
    m, act, ulow, mixed, *down = tick(m, act, ulow, mixed, *down)
    act_o, ulow_o, mixed_o = cores([act, ulow, mixed])
    first = rows * 3 // 8
    out0a, out0b, dh2, dfeed, small_down = local_call(
        down_kernel,
        m,
        (keep_mask, n1, attn_gain, attn_shift, down_bias, ffn_gain, ffn_shift, act, inputs, cotangent, down_weight, *down),
        [whole(first, dim, dtype=BF), whole(rows - first, dim, dtype=BF), wide, low, whole(8, dim)],
        specs=[smem, full(rows, dim)] + [vector] * 5 + [group] + [own_rows] * 2 + [HBM] * 9,
        out_specs=[full(first, dim), full(rows - first, dim), full(rows, dim), full(rows, dim), full(8, dim)],
        scratch=[square, pltpu.VMEM((rows, dim), F32), dma((4, 8))],
        grid=(4,),
        us=6,
        near=(1, 7),
    )
    m, q3, act_o, ulow_o, mixed_o, out0a, out0b, dfeed = tick(m, q3, act_o, ulow_o, mixed_o, out0a, out0b, dfeed)

    out2a = over_z(out0a, 2)
    qkv = jnp.stack([q1, q2, q3])
    qkv = [qkv] + plane(qkv)
    dfeed_o = over_dp(dfeed, 1, dp)
    dz, du1, small_up = local_call(
        ffn_back_kernel,
        m,
        (dfeed, dh2, der, down_weight, up_weight, *down, *up_out),
        [hidden_low, wide, whole(8, dim)],
        specs=[full(rows, dim)] * 2 + [group] + [HBM] * 18,
        out_specs=[group, full(rows, dim), full(8, dim)],
        scratch=[square, square, dma((2, 4, 8))],
        grid=(4,),
        us=10,
        near=(0, 1, 2),
    )
    m, dfeed_o, dz, out2a, out0a, out0b, *qkv = tick(m, dfeed_o, dz, out2a, out0a, out0b, *qkv)

    dz_o, out1a = over_dp(dz, 1, dp), over_z(out0a, 1)
    dh1, dattn, do, delta, small_norm = local_call(
        norm_back_kernel,
        m,
        (du1, n1, r1, attn_gain, mixed, out_weight, *up_out),
        [wide, low, heads_low, whole(4, 8, rows), whole(8, dim)],
        specs=[full(rows, dim)] * 2 + [full(rows, 1), vector, full(4, rows, PADDED)] + [HBM] * 9,
        scratch=[out_scratch, dma((4, 8))],
        us=4,
        near=(0, 1, 2, 4),
    )
    m, dz_o, out1a, dattn, out0b, out2a, *qkv = tick(m, dz_o, out1a, dattn, out0b, out2a, *qkv)

    out1b = over_z(out0b, 1)
    qkv += cores(qkv)
    parts = ffn_weight_grads(m, ulow, ulow_o, dfeed, dfeed_o, dz, dz_o, act, act_o)
    m, out1b, out0b, out2a, dattn, *rest = tick(m, out1b, out0b, out2a, dattn, *qkv, *parts)
    qkv, parts = rest[:8], rest[8:]

    out2b, out3a, dattn_o = over_z(out0b, 2), over_z(out2a, 1), over_dp(dattn, 1, dp)
    extra = []
    if dp == 8:
        extra = [over_dp(parts[1], 2, dp), over_dp(parts[2], 4, dp)]
    dqt, dx_other, g_far, small_other = attend_back(m, False, inputs, wt, qvb, do, lse, delta, qkv)
    m, out2b, out3a, dattn_o, dx_other, g_far, *rest = tick(m, out2b, out3a, dattn_o, dx_other, g_far, *parts, *extra)
    parts, extra = rest[:4], rest[4:]

    out3b, dx_arrived, h_far = over_z(out2b, 1), over_z(dx_other, 1), over_dp(g_far, 1, dp)
    if dp == 8:
        extra.append(over_dp(parts[3], 6, dp))
    dx_own, g_own, small = attend_back(
        m, True, inputs, wt, qvb, do, lse, delta, qkv,
        (dqt, small_down, small_norm, small_up, small_other, dh1, cotangent, keep_mask),
    )
    m, out3b, dx_arrived, h_far, g_own, small, dx_own, *extra = tick(
        m, out3b, dx_arrived, h_far, g_own, small, dx_own, *extra
    )

    h_own, small_o = over_dp(g_own, 1, dp), over_dp(small, 1, dp)
    grad_own = (dx_own + dx_arrived.astype(F32)).astype(BF)
    g2, g1 = over_z(grad_own, 2), over_z(grad_own, 1)
    m, h_own, small_o, grad_own = tick(m, h_own, small_o, grad_own)
    pieces = attend_weight_grads(
        m, inputs, inputs_o, dattn, dattn_o, g_own, h_own, g_far, h_far, mixed, mixed_o, small, small_o
    )
    m, *pieces = tick(m, *pieces)
    blocks = []
    if dp == 8:
        blocks = [over_dp(pieces[1], 2, dp), over_dp(pieces[2], 4, dp)]
        ffn_send, ffn_keep = ffn_plane(m, [parts[0]] + extra)
    else:
        ffn_send, ffn_keep = plane_any(parts, me, dp)
    final = ffn_keep.shape[2]
    places = ((0, 0), (0, first), (1, 0), (1, first), (2, 0), (2, first), (3, 0), (3, first))
    outputs = place(m, [out0a, out0b, out1a, out1b, out2a, out2b, out3a, out3b], places, tokens, BF)
    m, g2, g1, ffn_send, outputs, last_piece, *blocks = tick(m, g2, g1, ffn_send, outputs, pieces[3], *blocks)
    g3, ffn_arrived = over_z(g2, 1), over_z(ffn_send, 1)
    if dp == 8:
        blocks.append(over_dp(last_piece, 6, dp))
    grad_inputs = place(m, [grad_own, g1, g2], ((0, 0), (1, 0), (2, 0)), tokens, F32)
    if dp == 8:
        m, grad_inputs, *blocks = tick(m, grad_inputs, *blocks)
        *sends, block_mine, small = local_call(
            plane_sum_kernel,
            m,
            pieces[:1] + blocks,
            [whole(part + 48, dim, dtype=BF)] * 3 + [whole(part, dim), whole(24, dim)],
            specs=[full(*blocks[0].shape)] * 4,
            near=(0, 1, 2, 3),
        )
    else:
        sends, block_mine, small = attend_any(pieces, me, dp)
    arrived = [over_z(sends[r - 1], r) for r in (1, 2, 3)]
    ffn_mine = ffn_keep[:, 0] + ffn_arrived[:, 0].astype(F32)
    ffn_far = (ffn_keep[:, 1] + ffn_arrived[:, 1].astype(F32)).astype(BF)
    ffn_arrived = over_z(ffn_far, 2)
    grad_inputs = lax.dynamic_update_slice(grad_inputs, g3.astype(F32), ((z ^ 3) * rows, 0))
    grad_up = ffn_mine[0] + ffn_arrived[0].astype(F32)
    grad_down = ffn_mine[1] + ffn_arrived[1].astype(F32)
    grad_qkv, grad_out, grad_up_bias, grad_qv_bias, *same = local_call(
        final_sum_kernel,
        m,
        (block_mine, small, *arrived),
        [whole(3, final, width), whole(width, final), whole(dim), whole(2, width)] + [whole(dim)] * 6,
        specs=[VM, VM] + [full(final + 48, dim)] * 3,
        near=(0, 1, 2, 3, 4),
    )
    return (
        outputs,
        grad_inputs,
        grad_qkv,
        grad_qv_bias,
        grad_out,
        same[5],
        same[3],
        same[4],
        grad_up,
        grad_up_bias,
        grad_down.T,
        same[2],
        same[0],
        same[1],
    )


def scatter_any(blocks, dp):
    eight, groups, part, dim = blocks.shape
    flat = blocks.transpose(0, 2, 1, 3).reshape(eight * part, groups * dim).astype(F32)
    mine = lax.psum_scatter(flat, "dp", scatter_dimension=0, tiled=True)
    return mine.reshape(-1, groups, dim).transpose(1, 0, 2)


def order_any(by_offset, me, dp):
    mine = jnp.take(by_offset, jnp.arange(4) ^ ((me // 2) % 4), axis=0)
    other = over_dp(mine, 1, dp)
    even = jnp.where(me % 2 == 0, mine, other)
    odd = jnp.where(me % 2 == 0, other, mine)
    return jnp.stack([even, odd], 1).reshape((8,) + mine.shape[1:])


def plane_any(parts, me, dp):
    sums = jnp.stack([scatter_any(order_any(jnp.stack([p[i] for p in parts]), me, dp), dp) * 0.5 for i in range(2)])
    return sums[:, 1::2].astype(BF), sums[:, 0::2]


def attend_any(pieces, me, dp):
    pieces = jnp.stack(pieces)
    part = pieces.shape[1] // 4 // 16 * 16
    small = unpack_small(pieces[0, 4 * part :])
    blocks = pieces[:, : 4 * part].reshape(4, 4, part, -1)
    sums = scatter_any(order_any(blocks, me, dp), dp) * 0.5
    offset = 2
    while offset < dp:
        small = small + over_dp(small, offset, dp)
        offset *= 2
    packed = pack_small(small)
    sends = [jnp.concatenate([sums[r].astype(BF), packed]) for r in (1, 2, 3)]
    return sends, sums[0], unpack_small(packed)


def solution(mesh):
    placed = (
        P("dp", None),
        P(None, None, "tensor"),
        P(None, "tensor"),
        P("tensor", None),
        P(),
        P(),
        P(),
        P(None, "tensor"),
        P("tensor"),
        P("tensor", None),
        P(),
        P(),
        P(),
        P("dp"),
        P("dp", None),
    )
    return jax.shard_map(
        partial(per_device, mesh.shape["dp"]),
        mesh=mesh,
        in_specs=placed,
        out_specs=(
            P("dp", None),
            P("dp", None),
            P(None, "dp", "tensor"),
            P(None, "tensor"),
            P("tensor", "dp"),
            P(),
            P(),
            P(),
            P("dp", "tensor"),
            P("tensor"),
            P("tensor", "dp"),
            P(),
            P(),
            P(),
        ),
        check_vma=False,
    )
```

```python
from functools import partial

import jax
import jax.numpy as jnp
import numpy as np
from jax import lax
from jax.experimental import pallas as pl
from jax.experimental.pallas import tpu as pltpu
from jax.sharding import PartitionSpec as P

HEAD_DIM = 64
EPS = 1e-05
PADDED = 256
LOG2E = 1.4426950408889634
BF = jnp.bfloat16
F32 = jnp.float32
ANY = pl.BlockSpec(memory_space=pl.ANY)
HBM = pl.BlockSpec(memory_space=pltpu.HBM)
VM = pl.BlockSpec(memory_space=pltpu.VMEM)
LIMIT = 24 * 1024 * 1024


def nn(a, b):
    return lax.dot_general(a, b, (((1,), (0,)), ((), ())), preferred_element_type=F32)


def nt(a, b):
    return lax.dot_general(a, b, (((1,), (1,)), ((), ())), preferred_element_type=F32)


def cost(us):
    return pl.CostEstimate(flops=int(us * 1e3), bytes_accessed=1024, transcendentals=0)


def params(**kw):
    return pltpu.CompilerParams(vmem_limit_bytes=LIMIT, **kw)


def head_mask(rows, width, head):
    lane = lax.broadcasted_iota(jnp.int32, (rows, width), 1)
    return (lane >= head * HEAD_DIM) & (lane < (head + 1) * HEAD_DIM)


def row_norm(values):
    row_mean = jnp.mean(values, axis=-1, keepdims=True)
    centred = values - row_mean
    variance = jnp.mean(centred * centred, axis=-1, keepdims=True)
    inverse = lax.rsqrt(variance + EPS)
    return centred * inverse, inverse


def row_norm_back(grad_normed, normed, inverse):
    first_term = jnp.mean(grad_normed, axis=-1, keepdims=True)
    second_term = jnp.mean(grad_normed * normed, axis=-1, keepdims=True)
    return inverse * (grad_normed - first_term - normed * second_term)


def gelu_both(x):
    e = jnp.exp2(x * x * (-0.5 * LOG2E))
    t = 1.0 / (1.0 + (0.3275911 * 0.7071067811865476) * jnp.abs(x))
    poly = t * (
        0.5 * 0.254829592
        + t
        * (
            0.5 * -0.284496736
            + t * (0.5 * 1.421413741 + t * (0.5 * -1.453152027 + t * (0.5 * 1.061405429)))
        )
    )
    tail = poly * e
    cdf = jnp.where(x < 0, tail, 1.0 - tail)
    return x * cdf, cdf + x * (e * 0.3989422804014327)


def row_of(ref):
    return ref[...].astype(F32).reshape(1, ref.shape[0])


def whole(*shape, dtype=F32):
    return jax.ShapeDtypeStruct(shape, dtype)


def full(*shape):
    return pl.BlockSpec(shape, lambda *_: (0,) * len(shape))


def local_call(kernel, meta, args, outs, specs=None, scratch=(), us=1, out_specs=None, grid=(1,), aliases=None, near=()):
    args = [
        a if i in near or a.dtype == jnp.int32 or a.ndim < 2 else pltpu.with_memory_space_constraint(a, pltpu.HBM)
        for i, a in enumerate(args)
    ]
    return pl.pallas_call(
        kernel,
        grid_spec=pltpu.PrefetchScalarGridSpec(
            num_scalar_prefetch=1,
            grid=grid,
            in_specs=specs if specs is not None else [VM] * len(args),
            out_specs=out_specs if out_specs is not None else [VM] * len(outs),
            scratch_shapes=list(scratch),
        ),
        out_shape=list(outs),
        compiler_params=params(),
        cost_estimate=cost(us),
        input_output_aliases=aliases or {},
    )(meta, *args)


def cut_kernel(meta, up_ref, out_ref, down_ref, wt_ref, ub_ref, qvb_ref, a_ref, d_ref, q_ref, bias_s):
    lanes = a_ref.shape[1]
    up_rows, out_rows, part = up_ref.shape[0], out_ref.shape[0], wt_ref.shape[1]
    a_ref[:up_rows, :] = up_ref[...]
    a_ref[up_rows : up_rows + out_rows, :] = out_ref[...]
    bias_s[...] = jnp.zeros_like(bias_s)
    up_bias = row_of(ub_ref)
    bias_s[0:1, :] = up_bias[:, :lanes]
    bias_s[1:2, :] = up_bias[:, lanes:]
    bias_s[2:4, : qvb_ref.shape[1]] = qvb_ref[...].astype(F32)
    a_ref[up_rows + out_rows :, :] = bias_s[...].astype(BF)
    d_ref[...] = down_ref[...]
    for m in range(3):
        q_ref[m * part : (m + 1) * part, :] = wt_ref[m]


def cut(meta, up_weight, out_weight, down_weight, wt, up_bias, qv_bias):
    dim, hidden = up_weight.shape
    width = wt.shape[1]
    lanes = dim // 2
    place = lambda i, m: (m[1], m[2])
    return local_call(
        cut_kernel,
        meta,
        (up_weight, out_weight, down_weight, wt, up_bias, qv_bias),
        [
            whole(dim // 4 + width // 4 + 16, lanes, dtype=BF),
            whole(hidden // 4, lanes, dtype=BF),
            whole(3 * width // 4, lanes, dtype=BF),
        ],
        specs=[
            pl.BlockSpec((dim // 4, lanes), place),
            pl.BlockSpec((width // 4, lanes), place),
            pl.BlockSpec((hidden // 4, lanes), place),
            pl.BlockSpec((3, width // 4, lanes), lambda i, m: (0, m[1], m[2])),
            full(dim),
            full(2, width),
        ],
        scratch=[pltpu.VMEM((16, lanes), F32)],
    )


class Weights:
    def __init__(self, meta, own, pieces, scratch, sems, first, rows):
        self.meta, self.own, self.pieces, self.scratch, self.sems = meta, own, pieces, scratch, sems
        self.first, self.rows = first, rows

    def others(self, r):
        for place, piece in enumerate(self.pieces):
            quarter = self.meta[1] ^ (place % 4)
            side = self.meta[2] ^ (place // 4)
            lanes = piece.shape[2]
            start = pl.multiple_of(quarter * self.rows, 16)
            yield pltpu.make_async_copy(
                piece.at[r - 1, pl.ds(self.first, self.rows), :],
                self.scratch.at[r, pl.ds(start, self.rows), pl.ds(pl.multiple_of(side * lanes, 128), lanes)],
                self.sems.at[r, place],
            )

    def mine(self):
        return pltpu.make_async_copy(self.own, self.scratch.at[0], self.sems.at[0, 0])

    def start(self):
        self.mine().start()
        for r in range(1, 4):
            for copy in self.others(r):
                copy.start()

    def wait(self, r):
        @pl.when(r == 0)
        def _():
            self.mine().wait()

        @pl.when(r > 0)
        def _():
            for copy in self.others(r):
                copy.wait()

    def wait_all(self):
        self.mine().wait()
        for r in range(1, 4):
            for copy in self.others(r):
                copy.wait()


def split_three(rows):
    high = rows.astype(BF).astype(F32)
    middle = (rows - high).astype(BF).astype(F32)
    return high, middle, rows - high - middle


def attend_kernel(meta, x_ref, wt_ref, b_ref, down_ref, o0_ref, o1_ref, q_s, k_s, v_s, l_s):
    x = x_ref[...]
    length, width = q_s.shape
    heads = width // HEAD_DIM
    half = length // 2
    block = half // 2
    scale = HEAD_DIM ** (-0.5) * LOG2E
    q_s[...] = (nt(x, wt_ref[0]) + b_ref[0:1, :].astype(F32)).astype(BF)
    k_s[...] = nt(x, wt_ref[1]).astype(BF)
    v_s[...] = (nt(x, wt_ref[2]) + b_ref[1:2, :].astype(F32)).astype(BF)
    for k, o_ref in enumerate((o0_ref, o1_ref)):
        start = ((meta[0] % 2) ^ k) * half
        for part in range(2):
            rows = pl.ds(pl.multiple_of(start + part * block, block), block)
            q = q_s[rows, :]
            mixed = jnp.zeros((block, width), F32)
            stats = jnp.zeros((block, 128), F32)
            stat_lane = lax.broadcasted_iota(jnp.int32, (block, 128), 1)
            for h in range(heads):
                mask = head_mask(block, width, h)
                s = nt(jnp.where(mask, q, jnp.zeros_like(q)), k_s[...])
                top = jnp.max(s, axis=-1, keepdims=True)
                p = jnp.exp2((s - top) * scale)
                total = jnp.sum(p, axis=-1, keepdims=True)
                o = nn(p.astype(BF), v_s[...]) * (1.0 / total)
                mixed = jnp.where(mask, o, mixed)
                stats = jnp.where(stat_lane == h, top * scale + jnp.log2(total), stats)
            o_ref[:block, part * width : (part + 1) * width] = mixed.astype(BF)
            logs = split_three(jnp.transpose(stats)[:8, :])
            for i in range(3):
                l_s[part * 24 + i * 8 : part * 24 + i * 8 + 8, :] = logs[i]
        o_ref[block : block + 48, :block] = l_s[...].astype(BF)
        if o_ref.shape[0] > block + 48:
            o_ref[block + 48 :, :] = down_ref[...]


def attend(meta, inputs, wt, qv_bias, down_weight, length, other, carriers):
    width, dim = wt.shape[1:]
    hidden, lanes = down_weight.shape[0], dim // 2
    block = length // 4
    return local_call(
        attend_kernel,
        meta,
        (inputs, wt, qv_bias, down_weight),
        [whole(block + 48 + carried * hidden // 4, lanes, dtype=BF) for carried in carriers],
        specs=[
            pl.BlockSpec((length, dim), lambda i, m: ((m[0] // 2) ^ other, 0)),
            VM,
            full(2, width),
            pl.BlockSpec((hidden // 4, lanes), lambda i, m: (m[1], m[2])),
        ],
        out_specs=[full(block + 48 + carried * hidden // 4, lanes) for carried in carriers],
        scratch=[pltpu.VMEM((length, width), BF)] * 3 + [pltpu.VMEM((48, block), F32)],
        us=8,
    )


def up_kernel(meta, x_ref, t0, t1, t2, t3, ob_ref, ag_ref, as_ref, ub_ref, qvb_ref, wo_ref, wu_ref, *refs):
    pieces = refs[:8]
    n1_ref, r1_ref, ulow_ref, act_ref, der_ref, o_ref, lse_ref, qvb_all_ref = refs[8:16]
    wo_s, wu_s, bias_s, bias_all_s, z_s, sems = refs[16:]
    dim = x_ref.shape[1]
    lanes = dim // 2
    width = wo_ref.shape[0]
    up_rows, out_rows = wu_ref.shape[0] // 4, width // 4
    out = Weights(meta, wo_ref, pieces, wo_s, sems.at[0], up_rows, out_rows)
    up = Weights(meta, wu_ref, pieces, wu_s, sems.at[1], 0, up_rows)
    r = pl.program_id(0)

    @pl.when(r == 0)
    def _():
        rows = pl.ds(up_rows + out_rows, 16)
        biases = pltpu.make_async_copy(pieces[0].at[:, rows, :], bias_s, sems.at[0, 0, 1])
        out.start()
        biases.start()
        up.start()
        total = x_ref[...].astype(F32) + row_of(ob_ref)
        half = x_ref.shape[0] // 2
        for g, t_ref in enumerate((t0, t1, t2, t3)):
            logs = t_ref[half : half + 48, :half].astype(F32)
            for i in range(2):
                o_ref[g, i * half : (i + 1) * half, :width] = t_ref[:half, i * width : (i + 1) * width]
                lse_ref[g, :, i * half : (i + 1) * half] = (
                    logs[24 * i : 24 * i + 8] + logs[24 * i + 8 : 24 * i + 16] + logs[24 * i + 16 : 24 * i + 24]
                )
        qvb_all_ref[...] = jnp.zeros_like(qvb_all_ref)
        qvb_all_ref[0, 0:2, :width] = qvb_ref[...].astype(F32)
        bias_all_s[0, 0:1, :] = row_of(ub_ref)
        biases.wait()
        for g in range(1, 4):
            bias = bias_s[g - 1].astype(F32)
            bias_all_s[g, 0:1, :lanes] = bias[0:1]
            bias_all_s[g, 0:1, lanes:] = bias[1:2]
            qvb_all_ref[g, 0:2, :width] = bias[2:4, :width]
        out.wait_all()
        for g in range(4):
            total = total + nn(o_ref[g, :, :width], wo_s[g])
        normed, inverse = row_norm(total)
        n1_ref[...] = normed
        r1_ref[...] = inverse
        ulow_ref[...] = (normed * row_of(ag_ref) + row_of(as_ref)).astype(BF)

    up.wait(r)
    for c in range(0, dim, 256):
        z_s[...] = nn(ulow_ref[...], wu_s[r, :, c : c + 256])
        for b in range(0, z_s.shape[0], 32):
            act, der = gelu_both(z_s[b : b + 32, :] + bias_all_s[r, 0:1, c : c + 256])
            act_ref[0, b : b + 32, c : c + 256] = act.astype(BF)
            der_ref[0, b : b + 32, c : c + 256] = der.astype(BF)


def down_kernel(meta, keep_ref, n1_ref, ag_ref, as_ref, db_ref, fg_ref, fs_ref, act_ref, x_ref, cot_ref, wd_ref, *refs):
    pieces = refs[:8]
    out0_ref, out1_ref, dh2_ref, df_ref, small_ref, wd_s, acc, sems = refs[8:]
    down = Weights(meta, wd_ref, pieces, wd_s, sems, 0, wd_ref.shape[0] // 4)
    r = pl.program_id(0)

    @pl.when(r == 0)
    def _():
        down.start()
        acc[...] = n1_ref[...] * row_of(ag_ref) + (row_of(as_ref) + row_of(db_ref))

    down.wait(r)
    acc[...] += nn(act_ref[0], wd_s[r])

    @pl.when(r == 3)
    def _():
        normed, inverse = row_norm(acc[...])
        gain = row_of(fg_ref)
        keep = keep_ref[meta[0] // 2] > 0
        second = normed * gain + row_of(fs_ref)
        low = jnp.where(keep, second, x_ref[...].astype(F32)).astype(BF)
        cut_row = out0_ref.shape[0]
        out0_ref[...] = low[:cut_row]
        out1_ref[...] = low[cut_row:]
        grad = jnp.where(keep, cot_ref[...].astype(F32), 0.0)
        dh2 = row_norm_back(grad * gain, normed, inverse)
        dh2_ref[...] = dh2
        df_ref[...] = dh2.astype(BF)
        small_ref[...] = jnp.zeros_like(small_ref)
        small_ref[0:1, :] = jnp.sum(grad * normed, axis=0, keepdims=True)
        small_ref[1:2, :] = jnp.sum(grad, axis=0, keepdims=True)
        small_ref[2:3, :] = jnp.sum(dh2, axis=0, keepdims=True)


def ffn_back_kernel(meta, df_ref, dh2_ref, der_ref, wd_ref, wu_ref, *refs):
    downs, pieces = refs[:8], refs[8:16]
    dz_ref, du1_ref, small_ref, wd_s, wu_s, sems = refs[16:]
    dim = df_ref.shape[1]
    down = Weights(meta, wd_ref, downs, wd_s, sems.at[0], 0, wd_ref.shape[0] // 4)
    up = Weights(meta, wu_ref, pieces, wu_s, sems.at[1], 0, wu_ref.shape[0] // 4)
    r = pl.program_id(0)

    @pl.when(r == 0)
    def _():
        down.start()
        up.start()
        small_ref[...] = jnp.zeros_like(small_ref)
        du1_ref[...] = dh2_ref[...]

    down.wait(r)
    for c in range(0, dim, 256):
        dz = (nt(df_ref[...], wd_s[r, c : c + 256, :]) * der_ref[0, :, c : c + 256].astype(F32)).astype(BF)
        dz_ref[0, :, c : c + 256] = dz
        small_ref[pl.ds(r, 1), c : c + 256] = jnp.sum(dz.astype(F32), axis=0, keepdims=True)
    up.wait(r)
    du1_ref[...] += nt(dz_ref[0], wu_s[r])


def norm_back_kernel(meta, du1_ref, n1_ref, r1_ref, ag_ref, o_ref, wo_ref, *refs):
    pieces = refs[:8]
    dh1_ref, da_ref, do_ref, delta_ref, small_ref, wo_s, sems = refs[8:]
    width, dim = wo_ref.shape
    out = Weights(meta, wo_ref, pieces, wo_s, sems, dim // 4, width // 4)
    out.start()
    du1 = du1_ref[...]
    normed = n1_ref[...]
    small_ref[...] = jnp.zeros_like(small_ref)
    small_ref[0:1, :] = jnp.sum(du1 * normed, axis=0, keepdims=True)
    small_ref[1:2, :] = jnp.sum(du1, axis=0, keepdims=True)
    dh1 = row_norm_back(du1 * row_of(ag_ref), normed, r1_ref[...])
    small_ref[2:3, :] = jnp.sum(dh1, axis=0, keepdims=True)
    dh1_ref[...] = dh1
    da_ref[...] = dh1.astype(BF)
    out.wait_all()
    rows = du1.shape[0]
    stat_lane = lax.broadcasted_iota(jnp.int32, (rows, 128), 1)
    for r in range(4):
        do = nt(da_ref[...], wo_s[r]).astype(BF)
        do_ref[r] = do
        product = do.astype(F32) * o_ref[r, :, :width].astype(F32)
        stats = jnp.zeros((rows, 128), F32)
        for h in range(width // HEAD_DIM):
            inner = jnp.sum(jnp.where(head_mask(rows, width, h), product, 0.0), axis=-1, keepdims=True)
            stats = jnp.where(stat_lane == h, inner, stats)
        delta_ref[r] = jnp.transpose(stats)[:8, :]


def ffn_weight_kernel(meta, u_ref, v_ref, df_ref, dg_ref, dz_ref, dy_ref, act_ref, adt_ref, *refs):
    outs, (t_s, lu_s, ld_s) = refs[:4], refs[4:]
    tokens = u_ref.shape[0]
    part = outs[0].shape[2]

    @pl.when(pl.program_id(0) == 0)
    def _():
        for source, target, base in ((u_ref, lu_s, 0), (v_ref, lu_s, tokens), (df_ref, ld_s, 0), (dg_ref, ld_s, tokens)):
            t_s[...] = jnp.transpose(source[...])
            for j in range(4):
                start = pl.multiple_of((2 * (meta[1] ^ j) + meta[2]) * part, 16)
                target[j * part : (j + 1) * part, base : base + tokens] = t_s[pl.ds(start, part), :]

    for i, (left, own, other) in enumerate(((lu_s, dz_ref, dy_ref), (ld_s, act_ref, adt_ref))):
        acc = (nn(left[:, :tokens], own[0]) + nn(left[:, tokens:], other[0])).astype(BF)
        for j in range(4):
            outs[j][i, 0] = acc[j * part : (j + 1) * part, :]


def ffn_weight_grads(meta, ulow, ulow_o, dfeed, dfeed_o, dz, dz_o, act, act_o):
    rows, dim = ulow.shape
    part = dim // 8
    full = pl.BlockSpec((rows, dim), lambda r, m: (0, 0))
    group = pl.BlockSpec((1, rows, dim), lambda r, m: (r, 0, 0))
    out = pl.BlockSpec((2, 1, part, dim), lambda r, m: (0, r, 0, 0))
    return local_call(
        ffn_weight_kernel,
        meta,
        (ulow, ulow_o, dfeed, dfeed_o, dz, dz_o, act, act_o),
        [whole(2, 4, part, dim, dtype=BF)] * 4,
        specs=[full] * 4 + [group] * 4,
        out_specs=[out] * 4,
        scratch=[pltpu.VMEM((dim, rows), BF)] + [pltpu.VMEM((4 * part, 2 * rows), BF)] * 2,
        grid=(4,),
        us=9,
        near=(2, 4),
    )


def add(a, b):
    return a.astype(F32) + b.astype(F32)


def ffn_plane_kernel(meta, own, px, py, pd, send_ref, keep_ref):
    total = add(own[:, 0], px[:, 0]) + add(py[:, 0], pd[:, 0])
    near = pl.program_id(0) % 2 == 0

    @pl.when(near)
    def _():
        keep_ref[:, 0] = total

    @pl.when(jnp.logical_not(near))
    def _():
        send_ref[:, 0] = total.astype(BF)


def ffn_plane(meta, parts):
    _, groups, part, dim = parts[0].shape
    half = pl.BlockSpec((2, 1, part, dim), lambda r, m: (0, r // 2, 0, 0))
    return local_call(
        ffn_plane_kernel,
        meta,
        parts,
        [whole(2, 2, part, dim, dtype=BF), whole(2, 2, part, dim)],
        specs=[pl.BlockSpec((2, 1, part, dim), lambda r, m: (0, r, 0, 0))] * 4,
        out_specs=[half, half],
        grid=(groups,),
    )


def attend_back_kernel(own, meta, xq_ref, xk_ref, wt_ref, b_ref, do_ref, lse_ref, delta_ref, *refs):
    pieces = refs[:8]
    if own:
        dqt_ref, sd_ref, sn_ref, su_ref, sp_ref, dh1_ref, cot_ref, keep_ref, dx_ref, dkv_ref, small_ref = refs[8:19]
        w_s, sems, qm_s, dom_s, kt_s, s_s, dp_s, p_s, ds_s = refs[19:]
        base = 1
    else:
        dqt_ref, dxl_ref, dkv_ref, small_ref = refs[8:12]
        w_s, sems, qm_s, dom_s, kt_s, s_s, dp_s, p_s, ds_s, dx_ref = refs[12:]
        base = 0
    width = wt_ref.shape[1]
    heads = width // HEAD_DIM
    rows, dim = xq_ref.shape
    keys = xk_ref.shape[0]
    part = width // 4
    scale = HEAD_DIM ** (-0.5)
    r = pl.program_id(0)

    mine = [
        pltpu.make_async_copy(
            wt_ref.at[m, pl.ds(q * part, part), :], w_s.at[0, q, pl.ds(m * part, part), :], sems.at[0, m * 4 + q]
        )
        for m in range(3)
        for q in range(4)
    ]

    def others(g):
        for place, piece in enumerate(pieces):
            lanes = piece.shape[2]
            side = pl.multiple_of((meta[2] ^ (place // 4)) * lanes, 128)
            yield pltpu.make_async_copy(
                piece.at[g - 1], w_s.at[g, meta[1] ^ (place % 4), :, pl.ds(side, lanes)], sems.at[g, place]
            )

    @pl.when(r == 0)
    def _():
        for copy in mine:
            copy.start()
        for g in range(1, 4):
            for copy in others(g):
                copy.start()
        small_ref[...] = jnp.zeros_like(small_ref)
        if own:
            small_ref[0:3, :] = sd_ref[0:3, :]
            small_ref[3:6, :] = sn_ref[0:3, :]
            small_ref[8:12, :] = su_ref[0:4, :]
        dx_ref[...] = dh1_ref[...] if own else jnp.zeros_like(dx_ref)
        for copy in mine:
            copy.wait()

    @pl.when(r > 0)
    def _():
        for copy in others(r):
            copy.wait()

    wq, wk, wv = (w_s[r, :, m * part : (m + 1) * part, :].reshape(width, dim) for m in range(3))
    bias = b_ref[r][:, :width]
    q = (nt(xq_ref[...], wq) + bias[0:1, :]).astype(BF)
    k = nt(xk_ref[...], wk).astype(BF)
    v = (nt(xk_ref[...], wv) + bias[1:2, :]).astype(BF)
    do = do_ref[0]
    zero = jnp.zeros_like(q)
    for h in range(heads):
        mask = head_mask(rows, width, h)
        qm_s[h] = jnp.where(mask, q, zero)
        dom_s[h] = jnp.where(mask, do, zero)
    kt_s[...] = jnp.transpose(k)
    dqt = []
    dk = dv = None
    for h in range(heads):
        slot = h % 2
        s_s[slot] = nt(k, qm_s[h])
        dp_s[slot] = nt(v, dom_s[h])
        lse, delta = lse_ref[0, h : h + 1, :], delta_ref[0, h : h + 1, :]
        for b in range(0, keys, 32):
            p = jnp.exp2(s_s[slot, b : b + 32, :] * (scale * LOG2E) - lse)
            p_s[slot, b : b + 32, :] = p.astype(BF)
            ds_s[slot, b : b + 32, :] = (p * (dp_s[slot, b : b + 32, :] - delta)).astype(BF)
        dv_part = nn(p_s[slot], dom_s[h])
        dk_part = nn(ds_s[slot], qm_s[h])
        dqt.append(nn(kt_s[h * HEAD_DIM : (h + 1) * HEAD_DIM, :], ds_s[slot]))
        dv = dv_part if dv is None else dv + dv_part
        dk = dk_part if dk is None else dk + dk_part
    dk_low = (dk * scale).astype(BF)
    dv_low = dv.astype(BF)
    dkv_ref[base, 0, :, :width] = dk_low
    dkv_ref[base + 1, 0, :, :width] = dv_low
    dv_sum = jnp.sum(dv_low.astype(F32), axis=0, keepdims=True)
    all_heads = jnp.concatenate(dqt, axis=0)
    dx = nn(dk_low, wk) + nn(dv_low, wv)
    if own:
        dq_low = (jnp.transpose(all_heads + dqt_ref[0]) * scale).astype(BF)
        dkv_ref[0, 0, :, :width] = dq_low
        small_ref[pl.ds(12 + r, 1), :width] = jnp.sum(dq_low.astype(F32), axis=0, keepdims=True)
        small_ref[pl.ds(16 + r, 1), :width] = dv_sum + sp_ref[r, 0:1, :]
        dx = dx + nn(dq_low, wq)
    else:
        dqt_ref[0] = all_heads
        small_ref[r, 0:1, :] = dv_sum
    dx_ref[...] += dx

    @pl.when(r == 3)
    def _():
        if own:

            @pl.when(keep_ref[meta[0] // 2] <= 0)
            def _():
                dx_ref[...] = cot_ref[...].astype(F32)

        else:
            dxl_ref[...] = dx_ref[...].astype(BF)


def attend_back(meta, own, inputs, wt, bias, do, lse, delta, pieces, extra=()):
    rows, width = do.shape[1:]
    dim = inputs.shape[1]
    other = 0 if own else 1
    own_rows = pl.BlockSpec((rows, dim), lambda i, m: (m[0], 0))
    group = lambda *shape: pl.BlockSpec((1,) + shape, lambda i, m: (i,) + (0,) * len(shape))
    many = lambda count: pl.BlockSpec((count, 1, rows, PADDED), lambda i, m: (0, i, 0, 0))
    if own:
        outs = [whole(rows, dim), whole(3, 4, rows, PADDED, dtype=BF), whole(24, dim)]
        out_specs = [full(rows, dim), many(3), full(24, dim)]
    else:
        outs = [
            whole(4, width, rows),
            whole(rows, dim, dtype=BF),
            whole(2, 4, rows, PADDED, dtype=BF),
            whole(4, 8, width),
        ]
        out_specs = [group(width, rows), full(rows, dim), many(2), full(4, 8, width)]
    low = pltpu.VMEM((width // HEAD_DIM, rows, width), BF)
    return local_call(
        partial(attend_back_kernel, own),
        meta,
        (inputs, inputs, wt, bias, do, lse, delta, *pieces, *extra),
        outs,
        specs=[
            own_rows,
            pl.BlockSpec((rows, dim), lambda i, m: (m[0] ^ other, 0)),
            HBM,
            full(*bias.shape),
            group(rows, width),
            group(8, rows),
            group(8, rows),
        ]
        + [HBM] * 8
        + ([group(width, rows)] + [full(*e.shape) for e in extra[1:6]] + [own_rows, pl.BlockSpec(memory_space=pltpu.SMEM)] if own else []),
        out_specs=out_specs,
        scratch=[
            pltpu.VMEM((4, 4, 3 * width // 4, dim), BF),
            pltpu.SemaphoreType.DMA((4, 12)),
            low,
            low,
            pltpu.VMEM((width, rows), BF),
        ]
        + [pltpu.VMEM((2, rows, rows), F32)] * 2
        + [pltpu.VMEM((2, rows, rows), BF)] * 2
        + ([] if own else [pltpu.VMEM((rows, dim), F32)]),
        grid=(4,),
        us=14,
        near=(3, 4, 5, 6, 15, 16, 17, 18, 19),
    )


def attend_weight_kernel(
    meta, xq, yq, xk, yk, da, ea, g_own, h_own, g_far, h_far, o_ref, p_ref, small, small_o, p0, p1, p2, p3, t_s, lq_s, lk_s, la_s
):
    outs = (p0, p1, p2, p3)
    tokens = xq.shape[0]
    part = t_s.shape[0] // 8
    r = pl.program_id(0)

    @pl.when(r == 0)
    def _():
        pairs = ((xq, lq_s, 0), (yq, lq_s, tokens), (xk, lk_s, 0), (yk, lk_s, tokens), (da, la_s, 0), (ea, la_s, tokens))
        for source, target, base in pairs:
            t_s[...] = jnp.transpose(source[...])
            for j in range(4):
                start = pl.multiple_of((2 * (meta[1] ^ j) + meta[2]) * part, 16)
                target[j * part : (j + 1) * part, base : base + tokens] = t_s[pl.ds(start, part), :]
        packed = pack_small(small[...] + small_o[...])
        for ref in outs:
            ref[4 * part :, :] = packed

    width = t_s.shape[0] // 4
    first, second = slice(0, tokens), slice(tokens, 2 * tokens)
    both = lambda left, a, b: nn(left[:, first], a[:, :width]) + nn(left[:, second], b[:, :width])
    terms = [both(lq_s, g_own[0, 0], h_own[0, 0])]
    terms += [both(lq_s, g_own[m, 0], h_own[m, 0]) + both(lk_s, g_far[m - 1, 0], h_far[m - 1, 0]) for m in (1, 2)]
    terms.append(both(la_s, o_ref[0], p_ref[0]))
    acc = jnp.concatenate([term.astype(BF) for term in terms], axis=1)
    rows = pl.ds(pl.multiple_of(r * part, 16), part)
    for j in range(4):
        outs[j][rows, :] = acc[j * part : (j + 1) * part, :]


def attend_weight_grads(meta, inputs, inputs_o, dattn, dattn_o, g_own, h_own, g_far, h_far, mixed, mixed_o, small, small_o):
    rows, dim = dattn.shape
    width = mixed.shape[2]
    part = dim // 8
    own = pl.BlockSpec((rows, dim), lambda r, m: (m[0], 0))
    far = pl.BlockSpec((rows, dim), lambda r, m: (m[0] ^ 1, 0))
    full = pl.BlockSpec((rows, dim), lambda r, m: (0, 0))
    three = pl.BlockSpec((3, 1, rows, width), lambda r, m: (0, r, 0, 0))
    two = pl.BlockSpec((2, 1, rows, width), lambda r, m: (0, r, 0, 0))
    group = pl.BlockSpec((1, rows, width), lambda r, m: (r, 0, 0))
    left = pltpu.VMEM((4 * part, 2 * rows), BF)
    return local_call(
        attend_weight_kernel,
        meta,
        (inputs, inputs_o, inputs, inputs_o, dattn, dattn_o, g_own, h_own, g_far, h_far, mixed, mixed_o, small, small_o),
        [whole(4 * part + 48, dim, dtype=BF)] * 4,
        specs=[own, own, far, far, full, full, three, three, two, two, group, group, VM, VM],
        scratch=[pltpu.VMEM((dim, rows), BF), left, left, left],
        grid=(4,),
        us=8,
        near=(6, 7, 12, 13),
    )


def pack_small(rows):
    high = rows.astype(BF).astype(F32)
    return jnp.concatenate([high, rows - high], axis=0).astype(BF)


def unpack_small(rows):
    rows = rows.astype(F32)
    return rows[:24] + rows[24:]


def plane_sum_kernel(meta, own, px, py, pd, s1, s2, s3, keep_ref, small_ref):
    part = keep_ref.shape[0]
    for r, ref in enumerate((keep_ref, s1, s2, s3)):
        s = slice(r * part, (r + 1) * part)
        total = add(own[s, :], px[s, :]) + add(py[s, :], pd[s, :])
        ref[:part, :] = total.astype(ref.dtype)
    s = slice(4 * part, 4 * part + 48)
    small = (unpack_small(own[s, :]) + unpack_small(px[s, :])) + (unpack_small(py[s, :]) + unpack_small(pd[s, :]))
    packed = pack_small(small)
    for ref in (s1, s2, s3):
        ref[part:, :] = packed
    small_ref[...] = unpack_small(packed)


def final_sum_kernel(meta, mine, small, a1, a2, a3, gqkv_ref, gout_ref, ub_ref, qv_ref, *same_refs):
    part = mine.shape[0]
    width = gqkv_ref.shape[2]
    total = (mine[...] + a1[:part, :].astype(F32)) + add(a2[:part, :], a3[:part, :])
    for m in range(3):
        gqkv_ref[m] = total[:, m * width : (m + 1) * width]
    gout_ref[...] = jnp.transpose(total[:, 3 * width :])
    s0, s1, s2, s3 = small[...], unpack_small(a1[part:, :]), unpack_small(a2[part:, :]), unpack_small(a3[part:, :])
    same = (s0[0:8] + s1[0:8]) + (s2[0:8] + s3[0:8])
    for i, ref in enumerate(same_refs):
        ref[...] = same[i : i + 1].reshape(ref.shape)
    mine_rows = [(s0[i : i + 1] + s1[i + 1 : i + 2]) + (s2[i + 2 : i + 3] + s3[i + 3 : i + 4]) for i in (8, 12, 16)]
    ub_ref[...] = mine_rows[0].reshape(ub_ref.shape)
    qv_ref[0:1, :] = mine_rows[1][:, :width]
    qv_ref[1:2, :] = mine_rows[2][:, :width]


def place_kernel(spots, meta, *refs):
    blocks, out_ref = refs[: len(spots)], refs[len(spots)]
    wide_s, sems = refs[len(spots) + 1 :] if len(refs) > len(spots) + 2 else (None, refs[-1])
    rows = out_ref.shape[0] // 4
    copies = []
    for i, ((group, base), ref) in enumerate(zip(spots, blocks)):
        source = ref
        if wide_s is not None:
            source = wide_s.at[i]
            wide_s[i] = ref[...].astype(F32)
        start = pl.multiple_of((meta[0] ^ group) * rows + base, 16)
        copies.append(pltpu.make_async_copy(source, out_ref.at[pl.ds(start, ref.shape[0])], sems.at[i]))
        copies[-1].start()
    for copy in copies:
        copy.wait()


def place(meta, blocks, spots, tokens, dtype):
    dim = blocks[0].shape[1]
    wide = [pltpu.VMEM((len(blocks),) + blocks[0].shape, F32)] if dtype == F32 else []
    return local_call(
        partial(place_kernel, spots),
        meta,
        blocks,
        [whole(tokens, dim, dtype=dtype)],
        specs=[full(*b.shape) for b in blocks],
        out_specs=[HBM],
        scratch=wide + [pltpu.SemaphoreType.DMA((len(blocks),))],
        near=tuple(range(len(blocks))),
    )[0]


def over_z(x, r):
    return lax.ppermute(x, "tensor", [(i, i ^ r) for i in range(4)])


def over_dp(x, offset, size):
    return lax.ppermute(x, "dp", [(i, i ^ offset) for i in range(size)])


def tick(*arrays):
    return lax.optimization_barrier(arrays)


def per_device(
    dp,
    inputs,
    qkv_weight,
    qv_bias,
    out_weight,
    out_bias,
    attn_gain,
    attn_shift,
    up_weight,
    up_bias,
    down_weight,
    down_bias,
    ffn_gain,
    ffn_shift,
    keep_mask,
    cotangent,
):
    tokens, dim = inputs.shape
    length = tokens // keep_mask.shape[0]
    width = qkv_weight.shape[2]
    rows = tokens // 4
    part = dim // 8
    z = lax.axis_index("tensor")
    me = lax.axis_index("dp")
    meta = jnp.stack([z, (me // 2) % 4, me % 2]).astype(jnp.int32)
    wt = qkv_weight.transpose(0, 2, 1)
    own_rows = pl.BlockSpec((rows, dim), lambda i, m: (m[0], 0))
    smem = pl.BlockSpec(memory_space=pltpu.SMEM)
    low, wide = whole(rows, dim, dtype=BF), whole(rows, dim)
    hidden_low = whole(4, rows, dim, dtype=BF)
    heads_low = whole(4, rows, width, dtype=BF)
    out_scratch = pltpu.VMEM((4, width, dim), BF)
    square = pltpu.VMEM((4, dim, dim), BF)
    group = pl.BlockSpec((1, rows, dim), lambda r, m: (r, 0, 0))
    dma = pltpu.SemaphoreType.DMA
    plane = lambda block: [over_dp(block, 2 * j, dp) for j in (1, 2, 3)]
    cores = lambda blocks: [over_dp(b, 1, dp) for b in blocks]

    a, d, q = cut(meta, up_weight, out_weight, down_weight, wt, up_bias, qv_bias)
    a1, a2, a3, d1 = over_z(a, 1), over_z(a, 2), over_z(a, 3), over_z(d, 1)
    far0, far1 = attend(meta, inputs, wt, qv_bias, down_weight, length, 1, (1, 0))
    m, a1, a2, a3, d1, far0, far1 = tick(meta, a1, a2, a3, d1, far0, far1)

    t2, t3 = over_z(far0, 2), over_z(far1, 3)
    up_out = jnp.stack([a1, a2, a3])
    up_out = [up_out] + plane(up_out)
    t0, near = attend(m, inputs, wt, qv_bias, down_weight, length, 0, (0, 0))
    m, t0, near, t2, t3, *up_out = tick(m, t0, near, t2, t3, *up_out)

    down_rows = down_weight.shape[0] // 4
    d3 = over_z(t2[-down_rows:], 1)
    up_out += cores(up_out)
    m, q, near, d3, *up_out = tick(m, q, near, d3, *up_out)

    t1 = over_z(near, 1)
    down = jnp.stack([d1, t2[-down_rows:], d3])
    down = [down] + plane(down)
    m, t1, q = tick(m, t1, q)
    q1, q2 = over_z(q, 1), over_z(q, 2)
    vector = full(dim)
    n1, r1, ulow, act, der, mixed, lse, qvb = local_call(
        up_kernel,
        m,
        (inputs, t0, t1, t2, t3, out_bias, attn_gain, attn_shift, up_bias, qv_bias, out_weight, up_weight, *up_out),
        [wide, whole(rows, 1), low, hidden_low, hidden_low, whole(4, rows, PADDED, dtype=BF), whole(4, 8, rows), whole(4, 8, 256)],
        specs=[own_rows] + [full(*t.shape) for t in (t0, t1, t2, t3)] + [vector] * 4 + [full(2, width)] + [HBM] * 10,
        out_specs=[
            full(rows, dim), full(rows, 1), full(rows, dim), group, group, full(4, rows, PADDED), full(4, 8, rows), full(4, 8, 256)
        ],
        scratch=[
            out_scratch,
            square,
            pltpu.VMEM((3, 16, dim // 2), BF),
            pltpu.VMEM((4, 8, dim), F32),
            pltpu.VMEM((rows, 256), F32),
            dma((2, 4, 8)),
        ],
        grid=(4,),
        us=12,
        near=(1, 2, 3, 4),
    )
    m, q, q1, q2, act, ulow, mixed, *down = tick(m, q, q1, q2, act, ulow, mixed, *down)

    q3 = over_z(q, 3)
    down += cores(down)
    m, act, ulow, mixed, *down = tick(m, act, ulow, mixed, *down)
    act_o, ulow_o, mixed_o = cores([act, ulow, mixed])
    first = rows * 3 // 8
    out0a, out0b, dh2, dfeed, small_down = local_call(
        down_kernel,
        m,
        (keep_mask, n1, attn_gain, attn_shift, down_bias, ffn_gain, ffn_shift, act, inputs, cotangent, down_weight, *down),
        [whole(first, dim, dtype=BF), whole(rows - first, dim, dtype=BF), wide, low, whole(8, dim)],
        specs=[smem, full(rows, dim)] + [vector] * 5 + [group] + [own_rows] * 2 + [HBM] * 9,
        out_specs=[full(first, dim), full(rows - first, dim), full(rows, dim), full(rows, dim), full(8, dim)],
        scratch=[square, pltpu.VMEM((rows, dim), F32), dma((4, 8))],
        grid=(4,),
        us=6,
        near=(1, 7),
    )
    m, q3, act_o, ulow_o, mixed_o, out0a, out0b, dfeed = tick(m, q3, act_o, ulow_o, mixed_o, out0a, out0b, dfeed)

    out2a = over_z(out0a, 2)
    qkv = jnp.stack([q1, q2, q3])
    qkv = [qkv] + plane(qkv)
    dfeed_o = over_dp(dfeed, 1, dp)
    dz, du1, small_up = local_call(
        ffn_back_kernel,
        m,
        (dfeed, dh2, der, down_weight, up_weight, *down, *up_out),
        [hidden_low, wide, whole(8, dim)],
        specs=[full(rows, dim)] * 2 + [group] + [HBM] * 18,
        out_specs=[group, full(rows, dim), full(8, dim)],
        scratch=[square, square, dma((2, 4, 8))],
        grid=(4,),
        us=10,
        near=(0, 1, 2),
    )
    m, dfeed_o, dz, out2a, out0a, out0b, *qkv = tick(m, dfeed_o, dz, out2a, out0a, out0b, *qkv)

    dz_o, out1a = over_dp(dz, 1, dp), over_z(out0a, 1)
    dh1, dattn, do, delta, small_norm = local_call(
        norm_back_kernel,
        m,
        (du1, n1, r1, attn_gain, mixed, out_weight, *up_out),
        [wide, low, heads_low, whole(4, 8, rows), whole(8, dim)],
        specs=[full(rows, dim)] * 2 + [full(rows, 1), vector, full(4, rows, PADDED)] + [HBM] * 9,
        scratch=[out_scratch, dma((4, 8))],
        us=4,
        near=(0, 1, 2, 4),
    )
    m, dz_o, out1a, dattn, out0b, out2a, *qkv = tick(m, dz_o, out1a, dattn, out0b, out2a, *qkv)

    out1b = over_z(out0b, 1)
    qkv += cores(qkv)
    parts = ffn_weight_grads(m, ulow, ulow_o, dfeed, dfeed_o, dz, dz_o, act, act_o)
    m, out1b, out0b, out2a, dattn, *rest = tick(m, out1b, out0b, out2a, dattn, *qkv, *parts)
    qkv, parts = rest[:8], rest[8:]

    out2b, out3a, dattn_o = over_z(out0b, 2), over_z(out2a, 1), over_dp(dattn, 1, dp)
    extra = []
    if dp == 8:
        extra = [over_dp(parts[1], 2, dp), over_dp(parts[2], 4, dp)]
    dqt, dx_other, g_far, small_other = attend_back(m, False, inputs, wt, qvb, do, lse, delta, qkv)
    m, out2b, out3a, dattn_o, dx_other, g_far, *rest = tick(m, out2b, out3a, dattn_o, dx_other, g_far, *parts, *extra)
    parts, extra = rest[:4], rest[4:]

    m, own_inputs = tick(m, inputs)
    inputs_o = over_dp(own_inputs, 1, dp)
    out3b, dx_arrived, h_far = over_z(out2b, 1), over_z(dx_other, 1), over_dp(g_far, 1, dp)
    if dp == 8:
        extra.append(over_dp(parts[3], 6, dp))
    dx_own, g_own, small = attend_back(
        m, True, inputs, wt, qvb, do, lse, delta, qkv,
        (dqt, small_down, small_norm, small_up, small_other, dh1, cotangent, keep_mask),
    )
    m, out3b, dx_arrived, h_far, inputs_o, g_own, small, dx_own, *extra = tick(
        m, out3b, dx_arrived, h_far, inputs_o, g_own, small, dx_own, *extra
    )

    h_own, small_o = over_dp(g_own, 1, dp), over_dp(small, 1, dp)
    grad_own = (dx_own + dx_arrived.astype(F32)).astype(BF)
    g2, g1 = over_z(grad_own, 2), over_z(grad_own, 1)
    m, h_own, small_o, grad_own = tick(m, h_own, small_o, grad_own)
    pieces = attend_weight_grads(
        m, inputs, inputs_o, dattn, dattn_o, g_own, h_own, g_far, h_far, mixed, mixed_o, small, small_o
    )
    m, *pieces = tick(m, *pieces)
    blocks = []
    if dp == 8:
        blocks = [over_dp(pieces[1], 2, dp), over_dp(pieces[2], 4, dp)]
        ffn_send, ffn_keep = ffn_plane(m, [parts[0]] + extra)
    else:
        ffn_send, ffn_keep = plane_any(parts, me, dp)
    final = ffn_keep.shape[2]
    places = ((0, 0), (0, first), (1, 0), (1, first), (2, 0), (2, first), (3, 0), (3, first))
    outputs = place(m, [out0a, out0b, out1a, out1b, out2a, out2b, out3a, out3b], places, tokens, BF)
    m, g2, g1, ffn_send, outputs, last_piece, *blocks = tick(m, g2, g1, ffn_send, outputs, pieces[3], *blocks)
    g3, ffn_arrived = over_z(g2, 1), over_z(ffn_send, 1)
    if dp == 8:
        blocks.append(over_dp(last_piece, 6, dp))
    grad_inputs = place(m, [grad_own, g1, g2], ((0, 0), (1, 0), (2, 0)), tokens, F32)
    if dp == 8:
        m, grad_inputs, *blocks = tick(m, grad_inputs, *blocks)
        *sends, block_mine, small = local_call(
            plane_sum_kernel,
            m,
            pieces[:1] + blocks,
            [whole(part + 48, dim, dtype=BF)] * 3 + [whole(part, dim), whole(24, dim)],
            specs=[full(*blocks[0].shape)] * 4,
            near=(0, 1, 2, 3),
        )
    else:
        sends, block_mine, small = attend_any(pieces, me, dp)
    arrived = [over_z(sends[r - 1], r) for r in (1, 2, 3)]
    ffn_mine = ffn_keep[:, 0] + ffn_arrived[:, 0].astype(F32)
    ffn_far = (ffn_keep[:, 1] + ffn_arrived[:, 1].astype(F32)).astype(BF)
    ffn_arrived = over_z(ffn_far, 2)
    grad_inputs = lax.dynamic_update_slice(grad_inputs, g3.astype(F32), ((z ^ 3) * rows, 0))
    grad_up = ffn_mine[0] + ffn_arrived[0].astype(F32)
    grad_down = ffn_mine[1] + ffn_arrived[1].astype(F32)
    grad_qkv, grad_out, grad_up_bias, grad_qv_bias, *same = local_call(
        final_sum_kernel,
        m,
        (block_mine, small, *arrived),
        [whole(3, final, width), whole(width, final), whole(dim), whole(2, width)] + [whole(dim)] * 6,
        specs=[VM, VM] + [full(final + 48, dim)] * 3,
        near=(0, 1, 2, 3, 4),
    )
    return (
        outputs,
        grad_inputs,
        grad_qkv,
        grad_qv_bias,
        grad_out,
        same[5],
        same[3],
        same[4],
        grad_up,
        grad_up_bias,
        grad_down.T,
        same[2],
        same[0],
        same[1],
    )


def scatter_any(blocks, dp):
    eight, groups, part, dim = blocks.shape
    flat = blocks.transpose(0, 2, 1, 3).reshape(eight * part, groups * dim).astype(F32)
    mine = lax.psum_scatter(flat, "dp", scatter_dimension=0, tiled=True)
    return mine.reshape(-1, groups, dim).transpose(1, 0, 2)


def order_any(by_offset, me, dp):
    mine = jnp.take(by_offset, jnp.arange(4) ^ ((me // 2) % 4), axis=0)
    other = over_dp(mine, 1, dp)
    even = jnp.where(me % 2 == 0, mine, other)
    odd = jnp.where(me % 2 == 0, other, mine)
    return jnp.stack([even, odd], 1).reshape((8,) + mine.shape[1:])


def plane_any(parts, me, dp):
    sums = jnp.stack([scatter_any(order_any(jnp.stack([p[i] for p in parts]), me, dp), dp) * 0.5 for i in range(2)])
    return sums[:, 1::2].astype(BF), sums[:, 0::2]


def attend_any(pieces, me, dp):
    pieces = jnp.stack(pieces)
    part = pieces.shape[1] // 4 // 16 * 16
    small = unpack_small(pieces[0, 4 * part :])
    blocks = pieces[:, : 4 * part].reshape(4, 4, part, -1)
    sums = scatter_any(order_any(blocks, me, dp), dp) * 0.5
    offset = 2
    while offset < dp:
        small = small + over_dp(small, offset, dp)
        offset *= 2
    packed = pack_small(small)
    sends = [jnp.concatenate([sums[r].astype(BF), packed]) for r in (1, 2, 3)]
    return sends, sums[0], unpack_small(packed)


def solution(mesh):
    placed = (
        P("dp", None),
        P(None, None, "tensor"),
        P(None, "tensor"),
        P("tensor", None),
        P(),
        P(),
        P(),
        P(None, "tensor"),
        P("tensor"),
        P("tensor", None),
        P(),
        P(),
        P(),
        P("dp"),
        P("dp", None),
    )
    return jax.shard_map(
        partial(per_device, mesh.shape["dp"]),
        mesh=mesh,
        in_specs=placed,
        out_specs=(
            P("dp", None),
            P("dp", None),
            P(None, "dp", "tensor"),
            P(None, "tensor"),
            P("tensor", "dp"),
            P(),
            P(),
            P(),
            P("dp", "tensor"),
            P("tensor"),
            P("tensor", "dp"),
            P(),
            P(),
            P(),
        ),
        check_vma=False,
    )
```
